128 devices in a mesh: seq: 16 (over y_hi, z, core), tp: 8 (over x, y_lo).
Axes of the slice: x: 4, y: 4 (y_hi: 2, y_lo: 2; y = y_hi * 2 + y_lo), z: 4, core: 2. Of those that a mesh axis runs over, the one named last changes fastest.
Arguments:
- tokens: bfloat16 [2048, 8192], P('tp', 'seq'), may hold values from -6 to 6
- in_weight: bfloat16 [8192, 3, 8192], P('seq', None, 'tp'), may hold values from -0.0625 to 0.0625
- residues: float32 [16, 8192], P(None, 'tp'), may hold values from -0.3125 to 0.3125
- decay_rates: float32 [16, 8192], P(None, 'tp'), may hold values from 0.000146484375 to 0.05
- skip_gain: float32 [8192], P('tp'), may hold values from 0.5 to 1.5
- out_weight: bfloat16 [8192, 8192], P('tp', 'seq'), may hold values from -0.0625 to 0.0625
Outputs:
- block_output: bfloat16 [2048, 8192], P('tp', 'seq')
The draws below stay inside these ranges and needn't reach their ends.
All inputs are finite; a program needn't handle non-finite values.
Results may differ from the reference program's by a relative error of at most 0.038.
Values may be sent and summed in bfloat16 or wider, within the bound.
A program may use at most 128 MiB of HBM per device.

```python
import math
import jax
import jax.numpy as jnp
from jax import lax

D = 8192
MODES = 16
TOKENS = 2048
N_SEQ = 16
N_TP = 8


def draw_decay_rates(key, part):
    key = jax.random.fold_in(key, 7)
    pick_key, slow_key, fast_key = jax.random.split(key, 3)
    slow_share = 0.5
    array_shape = (MODES, D)
    slow_rates = jnp.exp(jax.random.uniform(slow_key, array_shape, jnp.float32, jnp.log(0.3 / TOKENS), jnp.log(2.0 / TOKENS)))
    fast_rates = jnp.exp(jax.random.uniform(fast_key, array_shape, jnp.float32, jnp.log(0.02), jnp.log(0.05)))
    chosen = jax.random.uniform(pick_key, array_shape, jnp.float32) < slow_share
    return jnp.clip(jnp.where(chosen, slow_rates, fast_rates), 0.3 / TOKENS, 0.05)


def level_of(key, extent, cuts, least, largest):
    gain = 1.0
    for dim, parts in cuts:
        draws = jax.random.uniform(jax.random.fold_in(jax.random.fold_in(key, 6), dim), (parts,), jnp.float32, least / len(cuts), largest / len(cuts))
        gain = gain * jnp.repeat(jnp.exp(draws), extent[dim] // parts).reshape((-1,) + (1,) * (len(extent) - 1 - dim))
    return gain


def centred(key, shape, spread, most, pieces=(), held_as=jnp.bfloat16):
    loudness = level_of(key, shape, pieces, -0.22, 0.18) if pieces else 1.0
    values = jax.random.normal(key, shape, jnp.float32) * spread * loudness
    return jnp.minimum(jnp.maximum(values, -most), most).astype(held_as)


def setup_inputs(seed: int = 0) -> dict:
    splits = jax.random.split(jax.random.key(seed), 7)
    tokens = centred(splits[0], (TOKENS, D), 1.0, 6.0, ((0, 8), (1, 16)))
    in_weight = centred(splits[1], (D, 3, D), D ** -0.5, 0.0625, ((0, 16), (2, 8)))
    residues = centred(splits[2], (MODES, D), (1.0 / TOKENS ** 0.5), 0.3125, ((1, 8),), jnp.float32)
    decay_rates = draw_decay_rates(jax.random.fold_in(splits[6], 71), 0)
    skip_gain = jnp.clip(0.5 + 1.0 * jax.random.uniform(splits[4], (D,), jnp.float32) ** level_of(splits[4], (D,), ((0, 8),), -0.2, 0.2), 0.5, 1.5)
    out_weight = centred(splits[5], (D, D), D ** -0.5, 0.0625, ((0, 8), (1, 16)))
    return dict(tokens=tokens, in_weight=in_weight, residues=residues, decay_rates=decay_rates, skip_gain=skip_gain, out_weight=out_weight)


def grouped_product(left, right, groups):
    inner = left.shape[1] // groups

    def add_group(carry, group_index):
        offset = group_index * inner
        left_part = lax.dynamic_slice_in_dim(left, offset, inner, 1)
        right_part = lax.dynamic_slice_in_dim(right, offset, inner, 0)
        term = jnp.dot(left_part, right_part, preferred_element_type=jnp.float32).astype(jnp.bfloat16)
        term = lax.optimization_barrier(term)
        return carry + term.astype(jnp.float32), None

    start_sum = jnp.zeros((left.shape[0], right.shape[1]), jnp.float32)
    result, unused = lax.scan(add_group, start_sum, jnp.arange(groups, dtype=jnp.int32))
    return result


def convolve_block(packed):
    signal_block, residue_block, decay_block = packed
    positions = jnp.arange(TOKENS, dtype=jnp.float32)
    filter_taps = jnp.sum(residue_block[:, :, None] * jnp.exp(-decay_block[:, :, None] * positions[None, None, :]), axis=0)
    padded_size = 2 * TOKENS
    spectrum = jnp.fft.rfft(signal_block, n=padded_size, axis=1) * jnp.fft.rfft(filter_taps, n=padded_size, axis=1)
    return jnp.fft.irfft(spectrum, n=padded_size, axis=1)[:, :TOKENS]


def reference(tokens, in_weight, residues, decay_rates, skip_gain, out_weight):
    projected = grouped_product(tokens, in_weight.reshape(D, 3 * D), N_SEQ).astype(jnp.bfloat16).reshape(TOKENS, 3, D)
    query = projected[:, 0, :].astype(jnp.float32)
    signal = projected[:, 1, :].astype(jnp.float32) * projected[:, 2, :].astype(jnp.float32)
    channel_block = math.gcd(D, 512)
    block_count = D // channel_block
    signal_blocks = signal.T.reshape(block_count, channel_block, TOKENS)
    residue_blocks = residues.reshape(MODES, block_count, channel_block).transpose(1, 0, 2)
    decay_blocks = decay_rates.reshape(MODES, block_count, channel_block).transpose(1, 0, 2)
    convolved = lax.map(convolve_block, (signal_blocks, residue_blocks, decay_blocks))
    convolved = convolved.reshape(D, TOKENS).T
    gated = (query * (convolved + skip_gain * signal)).astype(jnp.bfloat16)
    return grouped_product(gated, out_weight, N_TP).astype(jnp.bfloat16)
```

```python
import functools

import jax
import jax.numpy as jnp
from jax import lax
from jax.experimental import pallas as pl
from jax.experimental.pallas import tpu as pltpu
from jax.sharding import PartitionSpec as P

MESH = pl.DeviceIdType.MESH
F32 = jnp.float32
BF16 = jnp.bfloat16
CHUNKS = 8
ROWS = 128
HALF = 64
LANES = 128
MODES = 16
SEGS = 8
STEPS = 16
QKV = 3 * LANES
FEATURES = 512
WIDE = 1024


def remote(src, dst, send_sem, recv_sem, device):
    return pltpu.make_async_remote_copy(
        src_ref=src,
        dst_ref=dst,
        send_sem=send_sem,
        recv_sem=recv_sem,
        device_id=device,
        device_id_type=MESH,
    )


def wait_bytes(ref, sem):
    pltpu.make_async_copy(ref, ref, sem).wait()


def aligned(value, step):
    return pl.multiple_of(value * step, step)


def kernel(
    tokens,
    in_weight,
    residues,
    decay_rates,
    skip_gain,
    out_weight,
    out,
    tok,
    w_in,
    w_out,
    part,
    relay,
    direct,
    summed,
    y_send,
    y_recv,
    s_scr,
    y_scr,
    q_scr,
    decay_b,
    res_b,
    seg_b,
    scan_b,
    ends,
    state_in,
    state_out,
    gath,
    p_out,
    o_relay,
    o_dir,
    o_sum,
    o_acc,
    o_y,
    o_fin,
    local_sem,
    tok_sem,
    w_sem,
    wo_sem,
    relay_sem,
    direct_sem,
    summed_sem,
    y_sem,
    state_sem,
    gath_sem,
    o_relay_sem,
    o_dir_sem,
    o_sum_sem,
    o_y_sem,
    fin_sem,
    send_sem,
):
    seq = lax.axis_index("seq")
    tp = lax.axis_index("tp")
    core = lax.rem(seq, 2)
    z = lax.rem(seq // 2, 4)
    y_hi = seq // 8
    x = tp // 2
    y_lo = lax.rem(tp, 2)

    def at(dx=0, dz=0, flip_hi=False, flip_lo=False, flip_core=False):
        a = 1 - y_hi if flip_hi else y_hi
        b = lax.rem(z + dz, 4)
        c = 1 - core if flip_core else core
        d = lax.rem(x + dx, 4)
        e = 1 - y_lo if flip_lo else y_lo
        return (a * 8 + b * 2 + c, d * 2 + e)

    sibling = at(flip_core=True)
    z_next, z_prev, z_far = at(dz=1), at(dz=3), at(dz=2)
    y_far = at(flip_hi=True)
    x_next, x_prev, x_far = at(dx=1), at(dx=3), at(dx=2)
    y_near = at(flip_lo=True)
    peers = [sibling, z_next, z_prev, z_far, y_far, x_next, x_prev, x_far, y_near]
    block = y_hi * 4 + z
    lanes = pl.ds(aligned(block, LANES), LANES)

    barrier = pltpu.get_barrier_semaphore()
    for peer in peers:
        pl.semaphore_signal(barrier, inc=1, device_id=peer, device_id_type=MESH)
    pl.semaphore_wait(barrier, len(peers))

    own_rows = pl.ds(aligned(core, ROWS), ROWS)
    other_rows = pl.ds(aligned(1 - core, ROWS), ROWS)
    own_feat = pl.ds(aligned(core, FEATURES), FEATURES)
    other_feat = pl.ds(aligned(1 - core, FEATURES), FEATURES)
    tok_local = pltpu.make_async_copy(tokens.at[own_rows, :], tok.at[tp, :, own_feat], local_sem.at[0])
    tok_local.start()
    remote(tokens.at[other_rows, :], tok.at[tp, :, own_feat], send_sem.at[0], tok_sem.at[CHUNKS], sibling).start()

    def weight_pair(r):
        zi = lax.rem(z + r, 4)
        return in_weight.at[zi], w_in.at[zi, own_feat, :], w_in.at[zi, other_feat, :]

    for r in (2, 1, 3, 0):
        src, dst, _ = weight_pair(r)
        pltpu.make_async_copy(src, dst, local_sem.at[1 + r]).start()
        remote(src, dst, send_sem.at[1], w_sem.at[r], sibling).start()
    pltpu.make_async_copy(out_weight, w_out.at[core], local_sem.at[5]).start()

    seg_index = lax.broadcasted_iota(jnp.int32, (SEGS, LANES), 0)
    seg_next = (seg_index + 1).astype(F32) * float(STEPS)
    for m in range(MODES):
        rate = jnp.broadcast_to(decay_rates[pl.ds(m, 1), lanes], (SEGS, LANES))
        decay_b[m] = jnp.exp(-rate)
        res_b[m] = jnp.broadcast_to(residues[pl.ds(m, 1), lanes], (SEGS, LANES))
        seg_b[m] = jnp.exp(-rate * seg_next)
        for k in range(3):
            scan_b[k, m] = jnp.where(seg_index >= (1 << k), jnp.exp(-rate * float(STEPS << k)), 0.0)

    @pl.when(core == 0)
    def _():
        state_in[0] = jnp.zeros((MODES, LANES), F32)

    tok_local.wait()
    wait_bytes(tok.at[0, :, pl.ds(0, FEATURES)], tok_sem.at[CHUNKS])
    for peer in (y_near, x_next, x_prev, x_far):
        remote(tok.at[tp], tok.at[tp], send_sem.at[0], tok_sem.at[tp], peer).start()
    remote(out_weight, w_out.at[core], send_sem.at[1], wo_sem.at[0], sibling).start()

    near = x * 2 + 1 - y_lo

    def order(i):
        return jnp.where(i == 0, tp, jnp.where(i <= tp, i - 1, i))

    def multiply(jc, r):
        zi = lax.rem(z + r, 4)

        def column(n, carry):
            cols = pl.ds(aligned(n, 256), 256)
            acc = jnp.dot(tok[jc], w_in[zi, :, cols], preferred_element_type=F32)
            part[jc, r, :, cols] = acc.astype(BF16)
            return carry

        lax.fori_loop(0, 3, column, 0)

    first, second = pl.ds(0, QKV), pl.ds(QKV, QKV)

    def project(i):
        jc = order(i)

        @pl.when(jnp.logical_and(i > 0, jc != near))
        def _():
            wait_bytes(tok.at[jc], tok_sem.at[jc])

        for r in (2, 1, 3, 0):

            @pl.when(i == 0)
            def _():
                src, dst, other = weight_pair(r)
                pltpu.make_async_copy(src, dst, local_sem.at[1 + r]).wait()
                wait_bytes(other, w_sem.at[r])

            multiply(jc, r)
            if r == 2:
                remote(part.at[jc, 2, :, first], relay.at[0, jc], send_sem.at[2], relay_sem.at[0, jc], z_next).start()
                remote(part.at[jc, 2, :, second], relay.at[1, jc], send_sem.at[2], relay_sem.at[1, jc], z_prev).start()
            elif r == 1:
                remote(part.at[jc, 1, :, second], direct.at[1, jc], send_sem.at[3], direct_sem.at[1, jc], z_next).start()
            elif r == 3:
                remote(part.at[jc, 3, :, first], direct.at[0, jc], send_sem.at[3], direct_sem.at[0, jc], z_prev).start()

    def pass_on(jc):
        for k, r, cols, peer in ((0, 1, first, z_next), (1, 3, second, z_prev)):
            wait_bytes(relay.at[k, jc], relay_sem.at[k, jc])
            relay[k, jc] = (relay[k, jc].astype(F32) + part[jc, r, :, cols].astype(F32)).astype(BF16)
            remote(relay.at[k, jc], summed.at[k, jc], send_sem.at[4], summed_sem.at[k, jc], peer).start()

    def gather_half(jc, k):
        cols = pl.ds(aligned(k, QKV), QKV)
        return part[jc, 0, :, cols].astype(F32) + direct[k, jc].astype(F32) + summed[k, jc].astype(F32)

    def cross(jc):
        for k in range(2):
            wait_bytes(direct.at[k, jc], direct_sem.at[k, jc])
            wait_bytes(summed.at[k, jc], summed_sem.at[k, jc])
        y_send[jc] = gather_half(jc, 1 - y_hi).astype(BF16)
        remote(y_send.at[jc], y_recv.at[jc], send_sem.at[5], y_sem.at[jc], y_far).start()

    def convolve(j):
        wait_bytes(y_recv.at[j], y_sem.at[j])
        total = gather_half(j, y_hi) + y_recv[j].astype(F32)
        q_scr[...] = total[:, :LANES]
        s_scr[...] = total[:, LANES : 2 * LANES] * total[:, 2 * LANES :]
        decay = [decay_b[m] for m in range(MODES)]
        held = [jnp.zeros((SEGS, LANES), F32)] * MODES
        for i in range(STEPS):
            now = s_scr[pl.ds(i, SEGS, stride=STEPS), :]
            held = [decay[m] * held[m] + now for m in range(MODES)]
        for m in range(MODES):
            total = held[m]
            for k in range(3):
                total = total + scan_b[k, m] * pltpu.roll(total, 1 << k, 0)
            ends[m] = total

        @pl.when(jnp.logical_or(core == 1, j > 0))
        def _():
            wait_bytes(state_in.at[j], state_sem.at[j])

        for m in range(MODES):
            before = jnp.broadcast_to(state_in[j, pl.ds(m, 1), :], (SEGS, LANES))
            full = ends[m] + seg_b[m] * before
            state_out[j, pl.ds(m, 1), :] = full[SEGS - 1 :, :]
            ends[m] = jnp.where(seg_index == 0, before, pltpu.roll(full, 1, 0))

        @pl.when(jnp.logical_or(core == 0, j < CHUNKS - 1))
        def _():
            remote(state_out.at[j], state_in.at[j + core], send_sem.at[6], state_sem.at[j + core], sibling).start()

        held = [ends[m] for m in range(MODES)]
        for i in range(STEPS):
            now = s_scr[pl.ds(i, SEGS, stride=STEPS), :]
            held = [decay_b[m] * held[m] + now for m in range(MODES)]
            terms = [res_b[m] * held[m] for m in range(MODES)]
            while len(terms) > 1:
                terms = [terms[k] + terms[k + 1] for k in range(0, len(terms), 2)]
            y_scr[pl.ds(i, SEGS, stride=STEPS), :] = terms[0]
        gain = skip_gain[:, lanes]
        gath[j, :, lanes] = (q_scr[...] * (y_scr[...] + gain * s_scr[...])).astype(BF16)
        own = gath.at[j, :, lanes]
        for peer in (z_next, z_prev, z_far, y_far):
            remote(own, own, send_sem.at[7], gath_sem.at[block, j], peer).start()

    def forward(j):
        for r in (1, 3, 2):
            b = y_hi * 4 + lax.rem(z + r, 4)
            there = gath.at[j, :, pl.ds(aligned(b, LANES), LANES)]
            wait_bytes(there, gath_sem.at[b, j])
            remote(there, there, send_sem.at[7], gath_sem.at[b, j], y_far).start()

    upper, lower = pl.ds(0, HALF), pl.ds(HALF, HALF)

    def distance(j):
        return lax.rem(j // 2 - x + 4, 4)

    def finish(j):
        for r in range(4):
            b = (1 - y_hi) * 4 + r
            wait_bytes(gath.at[j, :, pl.ds(aligned(b, LANES), LANES)], gath_sem.at[b, j])

        @pl.when(j == 0)
        def _():
            pltpu.make_async_copy(out_weight, w_out.at[core], local_sem.at[5]).wait()
            wait_bytes(w_out.at[1 - core], wo_sem.at[0])

        for h in range(2):

            def column(n, carry):
                cols = pl.ds(aligned(n, 256), 256)
                acc = jnp.dot(gath[j], w_out[h, :, cols], preferred_element_type=F32)
                p_out[j, :, pl.ds(pl.multiple_of(h * FEATURES + n * 256, 256), 256)] = acc.astype(BF16)
                return carry

            lax.fori_loop(0, 2, column, 0)
        dx = distance(j)
        side = lax.rem(j, 2)

        @pl.when(dx == 2)
        def _():
            remote(p_out.at[j, upper], o_relay.at[j], send_sem.at[8], o_relay_sem.at[j], x_next).start()
            remote(p_out.at[j, lower], o_relay.at[j], send_sem.at[8], o_relay_sem.at[j], x_prev).start()

        @pl.when(dx == 1)
        def _():
            remote(p_out.at[j, lower], o_dir.at[1, side], send_sem.at[8], o_dir_sem.at[1, side], x_next).start()

        @pl.when(dx == 3)
        def _():
            remote(p_out.at[j, upper], o_dir.at[0, side], send_sem.at[8], o_dir_sem.at[0, side], x_prev).start()

    def o_pass(j):
        dx = distance(j)
        side = lax.rem(j, 2)
        for want, rows, k, peer in ((1, upper, 0, x_next), (3, lower, 1, x_prev)):

            @pl.when(dx == want)
            def _():
                wait_bytes(o_relay.at[j], o_relay_sem.at[j])
                o_relay[j] = (o_relay[j].astype(F32) + p_out[j, rows, :].astype(F32)).astype(BF16)
                remote(o_relay.at[j], o_sum.at[k, side], send_sem.at[8], o_sum_sem.at[k, side], peer).start()

    def o_cross(j):
        side = lax.rem(j, 2)

        @pl.when(distance(j) == 0)
        def _():
            for k in range(2):
                wait_bytes(o_dir.at[k, side], o_dir_sem.at[k, side])
                wait_bytes(o_sum.at[k, side], o_sum_sem.at[k, side])

            def total(k, rows):
                return p_out[j, rows, :].astype(F32) + o_dir[k, side].astype(F32) + o_sum[k, side].astype(F32)

            @pl.when(side == y_lo)
            def _():
                for k, rows in ((0, upper), (1, lower)):
                    o_acc[rows, :] = total(k, rows)

            @pl.when(side != y_lo)
            def _():
                for k, rows in ((0, upper), (1, lower)):
                    p_out[j, rows, :] = total(k, rows).astype(BF16)
                remote(p_out.at[j], o_y, send_sem.at[8], o_y_sem.at[0], y_near).start()

    def o_last(j):
        @pl.when(j == tp)
        def _():
            wait_bytes(o_y, o_y_sem.at[0])
            mine = pl.ds(aligned(core, FEATURES), FEATURES)
            theirs = pl.ds(aligned(1 - core, FEATURES), FEATURES)
            o_fin[...] = (o_acc[:, theirs] + o_y[:, theirs].astype(F32)).astype(BF16)
            remote(o_fin, out.at[own_rows, :], send_sem.at[8], fin_sem.at[0], sibling).start()
            out[own_rows, :] = (o_acc[:, mine] + o_y[:, mine].astype(F32)).astype(BF16)

    def step(i, carry):
        def stage(lag, body):
            @pl.when(jnp.logical_and(i >= lag, i < lag + CHUNKS))
            def _():
                body(i - lag)

        @pl.when(i == 1)
        def _():
            wait_bytes(tok.at[near], tok_sem.at[near])
            for peer in (x_next, x_prev, x_far):
                remote(tok.at[near], tok.at[near], send_sem.at[0], tok_sem.at[near], peer).start()

        stage(0, project)
        stage(1, lambda k: pass_on(order(k)))
        stage(2, lambda k: cross(order(k)))
        stage(4, convolve)
        stage(5, forward)
        stage(6, finish)
        stage(7, o_pass)
        stage(8, o_cross)
        stage(9, o_last)
        return carry

    lax.fori_loop(0, CHUNKS + 9, step, 0)

    wait_bytes(o_fin, fin_sem.at[0])
    wait_bytes(tok.at[pl.ds(0, 7)], send_sem.at[0])
    wait_bytes(tok.at[0, :, pl.ds(0, FEATURES)], send_sem.at[0])
    wait_bytes(in_weight, send_sem.at[1])
    wait_bytes(out_weight, send_sem.at[1])
    wait_bytes(relay, send_sem.at[2])
    wait_bytes(direct, send_sem.at[3])
    wait_bytes(summed, send_sem.at[4])
    wait_bytes(y_recv, send_sem.at[5])
    wait_bytes(state_out.at[pl.ds(0, CHUNKS - 1)], send_sem.at[6])

    @pl.when(core == 0)
    def _():
        wait_bytes(state_out.at[0], send_sem.at[6])

    wait_bytes(gath.at[pl.ds(0, 7)], send_sem.at[7])
    wait_bytes(p_out.at[pl.ds(0, 7)], send_sem.at[8])
    wait_bytes(o_fin, send_sem.at[8])


def local(tokens, in_weight, residues, decay_rates, skip_gain, out_weight):
    features, _, channels = in_weight.shape
    sorted_weight = in_weight.reshape(features, 3, 2, 4, LANES).transpose(3, 0, 2, 1, 4).reshape(4, features, 2 * QKV)
    vmem = pl.BlockSpec(memory_space=pltpu.VMEM)
    anywhere = pl.BlockSpec(memory_space=pl.ANY)
    dma = pltpu.SemaphoreType.DMA
    scratch = [
        pltpu.VMEM((CHUNKS, ROWS, WIDE), BF16),
        pltpu.VMEM((4, WIDE, 2 * QKV), BF16),
        pltpu.VMEM((2, WIDE, FEATURES), BF16),
        pltpu.VMEM((CHUNKS, 4, ROWS, 2 * QKV), BF16),
        pltpu.VMEM((2, CHUNKS, ROWS, QKV), BF16),
        pltpu.VMEM((2, CHUNKS, ROWS, QKV), BF16),
        pltpu.VMEM((2, CHUNKS, ROWS, QKV), BF16),
        pltpu.VMEM((CHUNKS, ROWS, QKV), BF16),
        pltpu.VMEM((CHUNKS, ROWS, QKV), BF16),
        pltpu.VMEM((ROWS, LANES), F32),
        pltpu.VMEM((ROWS, LANES), F32),
        pltpu.VMEM((ROWS, LANES), F32),
        pltpu.VMEM((MODES, SEGS, LANES), F32),
        pltpu.VMEM((MODES, SEGS, LANES), F32),
        pltpu.VMEM((MODES, SEGS, LANES), F32),
        pltpu.VMEM((3, MODES, SEGS, LANES), F32),
        pltpu.VMEM((MODES, SEGS, LANES), F32),
        pltpu.VMEM((CHUNKS + 1, MODES, LANES), F32),
        pltpu.VMEM((CHUNKS, MODES, LANES), F32),
        pltpu.VMEM((CHUNKS, ROWS, WIDE), BF16),
        pltpu.VMEM((CHUNKS, ROWS, WIDE), BF16),
        pltpu.VMEM((CHUNKS, HALF, WIDE), BF16),
        pltpu.VMEM((2, 2, HALF, WIDE), BF16),
        pltpu.VMEM((2, 2, HALF, WIDE), BF16),
        pltpu.VMEM((ROWS, WIDE), F32),
        pltpu.VMEM((ROWS, WIDE), BF16),
        pltpu.VMEM((ROWS, FEATURES), BF16),
        dma((6,)),
        dma((CHUNKS + 1,)),
        dma((4,)),
        dma((1,)),
        dma((2, CHUNKS)),
        dma((2, CHUNKS)),
        dma((2, CHUNKS)),
        dma((CHUNKS,)),
        dma((CHUNKS + 1,)),
        dma((8, CHUNKS)),
        dma((CHUNKS,)),
        dma((2, 2)),
        dma((2, 2)),
        dma((1,)),
        dma((1,)),
        dma((9,)),
    ]
    return pl.pallas_call(
        kernel,
        out_shape=jax.ShapeDtypeStruct(tokens.shape, BF16),
        in_specs=[anywhere, anywhere, vmem, vmem, vmem, anywhere],
        out_specs=vmem,
        scratch_shapes=scratch,
        compiler_params=pltpu.CompilerParams(
            collective_id=0, has_side_effects=True, vmem_limit_bytes=56 * 2**20
        ),
        name="hyena_block",
    )(tokens, sorted_weight, residues, decay_rates, skip_gain.reshape(1, channels), out_weight)


def solution(mesh):
    in_specs = (
        P("tp", "seq"),
        P("seq", None, "tp"),
        P(None, "tp"),
        P(None, "tp"),
        P("tp"),
        P("tp", "seq"),
    )
    return jax.shard_map(local, mesh=mesh, in_specs=in_specs, out_specs=P("tp", "seq"), check_vma=False)
```

```python
import functools

import jax
import jax.numpy as jnp
from jax import lax
from jax.experimental import pallas as pl
from jax.experimental.pallas import tpu as pltpu
from jax.sharding import PartitionSpec as P

MESH = pl.DeviceIdType.MESH
F32 = jnp.float32
BF16 = jnp.bfloat16
CHUNKS = 8
ROWS = 128
HALF = 64
LANES = 128
MODES = 16
SEGS = 8
STEPS = 16
QKV = 3 * LANES
FEATURES = 512
WIDE = 1024


def remote(src, dst, send_sem, recv_sem, device):
    return pltpu.make_async_remote_copy(
        src_ref=src,
        dst_ref=dst,
        send_sem=send_sem,
        recv_sem=recv_sem,
        device_id=device,
        device_id_type=MESH,
    )


def wait_bytes(ref, sem):
    pltpu.make_async_copy(ref, ref, sem).wait()


def aligned(value, step):
    return pl.multiple_of(value * step, step)


def kernel(
    tokens,
    in_weight,
    residues,
    decay_rates,
    skip_gain,
    out_weight,
    out,
    tok,
    w_in,
    w_out,
    part,
    relay,
    direct,
    summed,
    y_send,
    y_recv,
    s_scr,
    y_scr,
    q_scr,
    decay_b,
    res_b,
    seg_b,
    scan_b,
    ends,
    state_in,
    state_out,
    gath,
    p_out,
    o_relay,
    o_dir,
    o_sum,
    o_acc,
    o_y,
    o_fin,
    local_sem,
    tok_sem,
    w_sem,
    wo_sem,
    relay_sem,
    direct_sem,
    summed_sem,
    y_sem,
    state_sem,
    gath_sem,
    o_relay_sem,
    o_dir_sem,
    o_sum_sem,
    o_y_sem,
    fin_sem,
    send_sem,
):
    seq = lax.axis_index("seq")
    tp = lax.axis_index("tp")
    core = lax.rem(seq, 2)
    z = lax.rem(seq // 2, 4)
    y_hi = seq // 8
    x = tp // 2
    y_lo = lax.rem(tp, 2)

    def at(dx=0, dz=0, flip_hi=False, flip_lo=False, flip_core=False):
        a = 1 - y_hi if flip_hi else y_hi
        b = lax.rem(z + dz, 4)
        c = 1 - core if flip_core else core
        d = lax.rem(x + dx, 4)
        e = 1 - y_lo if flip_lo else y_lo
        return (a * 8 + b * 2 + c, d * 2 + e)

    sibling = at(flip_core=True)
    z_next, z_prev, z_far = at(dz=1), at(dz=3), at(dz=2)
    y_far = at(flip_hi=True)
    x_next, x_prev, x_far = at(dx=1), at(dx=3), at(dx=2)
    y_near = at(flip_lo=True)
    peers = [sibling, z_next, z_prev, z_far, y_far, x_next, x_prev, x_far, y_near]
    block = y_hi * 4 + z
    lanes = pl.ds(aligned(block, LANES), LANES)

    barrier = pltpu.get_barrier_semaphore()
    for peer in peers:
        pl.semaphore_signal(barrier, inc=1, device_id=peer, device_id_type=MESH)
    pl.semaphore_wait(barrier, len(peers))

    own_rows = pl.ds(aligned(core, ROWS), ROWS)
    other_rows = pl.ds(aligned(1 - core, ROWS), ROWS)
    own_feat = pl.ds(aligned(core, FEATURES), FEATURES)
    other_feat = pl.ds(aligned(1 - core, FEATURES), FEATURES)
    tok_local = pltpu.make_async_copy(tokens.at[own_rows, :], tok.at[tp, :, own_feat], local_sem.at[0])
    tok_local.start()
    remote(tokens.at[other_rows, :], tok.at[tp, :, own_feat], send_sem.at[0], tok_sem.at[CHUNKS], sibling).start()

    def own_weight(r):
        return w_in.at[lax.rem(z + r, 4), own_feat, :]

    for r in (2, 1, 3, 0):
        zi = lax.rem(z + r, 4)
        for h in range(2):
            there = pl.ds(aligned(h * 4 + zi, LANES), LANES)
            for k in range(3):
                pltpu.make_async_copy(
                    in_weight.at[k, :, there],
                    w_in.at[zi, own_feat, pl.ds((h * 3 + k) * LANES, LANES)],
                    local_sem.at[1 + r],
                ).start()
    pltpu.make_async_copy(out_weight, w_out.at[core], local_sem.at[5]).start()

    seg_index = lax.broadcasted_iota(jnp.int32, (SEGS, LANES), 0)
    seg_next = (seg_index + 1).astype(F32) * float(STEPS)
    for m in range(MODES):
        rate = jnp.broadcast_to(decay_rates[pl.ds(m, 1), lanes], (SEGS, LANES))
        decay_b[m] = jnp.exp(-rate)
        res_b[m] = jnp.broadcast_to(residues[pl.ds(m, 1), lanes], (SEGS, LANES))
        seg_b[m] = jnp.exp(-rate * seg_next)
        for k in range(3):
            scan_b[k, m] = jnp.where(seg_index >= (1 << k), jnp.exp(-rate * float(STEPS << k)), 0.0)

    @pl.when(core == 0)
    def _():
        state_in[0] = jnp.zeros((MODES, LANES), F32)

    for r in (2, 1, 3, 0):
        wait_bytes(own_weight(r), local_sem.at[1 + r])
        remote(own_weight(r), own_weight(r), send_sem.at[1], w_sem.at[r], sibling).start()
    tok_local.wait()
    wait_bytes(tok.at[0, :, pl.ds(0, FEATURES)], tok_sem.at[CHUNKS])
    for peer in (y_near, x_next, x_prev, x_far):
        remote(tok.at[tp], tok.at[tp], send_sem.at[0], tok_sem.at[tp], peer).start()
    remote(out_weight, w_out.at[core], send_sem.at[1], wo_sem.at[0], sibling).start()

    near = x * 2 + 1 - y_lo

    def order(i):
        return jnp.where(i == 0, tp, jnp.where(i <= tp, i - 1, i))

    def multiply(jc, r):
        zi = lax.rem(z + r, 4)

        part[jc, r] = jnp.dot(tok[jc], w_in[zi], preferred_element_type=F32).astype(BF16)

    first, second = pl.ds(0, QKV), pl.ds(QKV, QKV)

    def project(i):
        jc = order(i)

        @pl.when(jnp.logical_and(i > 0, jc != near))
        def _():
            wait_bytes(tok.at[jc], tok_sem.at[jc])

        for r in (2, 1, 3, 0):

            @pl.when(i == 0)
            def _():
                wait_bytes(w_in.at[0, other_feat, :], w_sem.at[r])

            multiply(jc, r)
            if r == 2:
                remote(part.at[jc, 2, :, first], relay.at[0, jc], send_sem.at[2], relay_sem.at[0, jc], z_next).start()
                remote(part.at[jc, 2, :, second], relay.at[1, jc], send_sem.at[2], relay_sem.at[1, jc], z_prev).start()
            elif r == 1:
                remote(part.at[jc, 1, :, second], direct.at[1, jc], send_sem.at[3], direct_sem.at[1, jc], z_next).start()
            elif r == 3:
                remote(part.at[jc, 3, :, first], direct.at[0, jc], send_sem.at[3], direct_sem.at[0, jc], z_prev).start()

    def pass_on(jc):
        for k, r, cols, peer in ((0, 1, first, z_next), (1, 3, second, z_prev)):
            wait_bytes(relay.at[k, jc], relay_sem.at[k, jc])
            relay[k, jc] = (relay[k, jc].astype(F32) + part[jc, r, :, cols].astype(F32)).astype(BF16)
            remote(relay.at[k, jc], summed.at[k, jc], send_sem.at[4], summed_sem.at[k, jc], peer).start()

    def gather_half(jc, k):
        cols = pl.ds(aligned(k, QKV), QKV)
        return part[jc, 0, :, cols].astype(F32) + direct[k, jc].astype(F32) + summed[k, jc].astype(F32)

    def cross(jc):
        for k in range(2):
            wait_bytes(direct.at[k, jc], direct_sem.at[k, jc])
            wait_bytes(summed.at[k, jc], summed_sem.at[k, jc])
        y_send[jc] = gather_half(jc, 1 - y_hi).astype(BF16)
        remote(y_send.at[jc], y_recv.at[jc], send_sem.at[5], y_sem.at[jc], y_far).start()

    def convolve(j):
        wait_bytes(y_recv.at[j], y_sem.at[j])
        total = gather_half(j, y_hi) + y_recv[j].astype(F32)
        q_scr[...] = total[:, :LANES]
        s_scr[...] = total[:, LANES : 2 * LANES] * total[:, 2 * LANES :]
        decay = [decay_b[m] for m in range(MODES)]
        held = [jnp.zeros((SEGS, LANES), F32)] * MODES
        for i in range(STEPS):
            now = s_scr[pl.ds(i, SEGS, stride=STEPS), :]
            held = [decay[m] * held[m] + now for m in range(MODES)]
        for m in range(MODES):
            total = held[m]
            for k in range(3):
                total = total + scan_b[k, m] * pltpu.roll(total, 1 << k, 0)
            ends[m] = total

        @pl.when(jnp.logical_or(core == 1, j > 0))
        def _():
            wait_bytes(state_in.at[j], state_sem.at[j])

        for m in range(MODES):
            before = jnp.broadcast_to(state_in[j, pl.ds(m, 1), :], (SEGS, LANES))
            full = ends[m] + seg_b[m] * before
            state_out[j, pl.ds(m, 1), :] = full[SEGS - 1 :, :]
            ends[m] = jnp.where(seg_index == 0, before, pltpu.roll(full, 1, 0))

        @pl.when(jnp.logical_or(core == 0, j < CHUNKS - 1))
        def _():
            remote(state_out.at[j], state_in.at[j + core], send_sem.at[6], state_sem.at[j + core], sibling).start()

        held = [ends[m] for m in range(MODES)]
        for i in range(STEPS):
            now = s_scr[pl.ds(i, SEGS, stride=STEPS), :]
            held = [decay_b[m] * held[m] + now for m in range(MODES)]
            terms = [res_b[m] * held[m] for m in range(MODES)]
            while len(terms) > 1:
                terms = [terms[k] + terms[k + 1] for k in range(0, len(terms), 2)]
            y_scr[pl.ds(i, SEGS, stride=STEPS), :] = terms[0]
        gain = skip_gain[:, lanes]
        gath[j, :, lanes] = (q_scr[...] * (y_scr[...] + gain * s_scr[...])).astype(BF16)
        own = gath.at[j, :, lanes]
        for peer in (z_next, z_prev, z_far, y_far):
            remote(own, own, send_sem.at[7], gath_sem.at[block, j], peer).start()

    def forward(j):
        for r in (1, 3, 2):
            b = y_hi * 4 + lax.rem(z + r, 4)
            there = gath.at[j, :, pl.ds(aligned(b, LANES), LANES)]
            wait_bytes(there, gath_sem.at[b, j])
            remote(there, there, send_sem.at[7], gath_sem.at[b, j], y_far).start()

    upper, lower = pl.ds(0, HALF), pl.ds(HALF, HALF)

    def distance(j):
        return lax.rem(j // 2 - x + 4, 4)

    def finish(j):
        for r in range(4):
            b = (1 - y_hi) * 4 + r
            wait_bytes(gath.at[j, :, pl.ds(aligned(b, LANES), LANES)], gath_sem.at[b, j])

        @pl.when(j == 0)
        def _():
            pltpu.make_async_copy(out_weight, w_out.at[core], local_sem.at[5]).wait()
            wait_bytes(w_out.at[1 - core], wo_sem.at[0])

        for h in range(2):
            cols = pl.ds(h * FEATURES, FEATURES)
            p_out[j, :, cols] = jnp.dot(gath[j], w_out[h], preferred_element_type=F32).astype(BF16)
        dx = distance(j)
        side = lax.rem(j, 2)

        @pl.when(dx == 2)
        def _():
            remote(p_out.at[j, upper], o_relay.at[j], send_sem.at[8], o_relay_sem.at[j], x_next).start()
            remote(p_out.at[j, lower], o_relay.at[j], send_sem.at[8], o_relay_sem.at[j], x_prev).start()

        @pl.when(dx == 1)
        def _():
            remote(p_out.at[j, lower], o_dir.at[1, side], send_sem.at[8], o_dir_sem.at[1, side], x_next).start()

        @pl.when(dx == 3)
        def _():
            remote(p_out.at[j, upper], o_dir.at[0, side], send_sem.at[8], o_dir_sem.at[0, side], x_prev).start()

    def o_pass(j):
        dx = distance(j)
        side = lax.rem(j, 2)
        for want, rows, k, peer in ((1, upper, 0, x_next), (3, lower, 1, x_prev)):

            @pl.when(dx == want)
            def _():
                wait_bytes(o_relay.at[j], o_relay_sem.at[j])
                o_relay[j] = (o_relay[j].astype(F32) + p_out[j, rows, :].astype(F32)).astype(BF16)
                remote(o_relay.at[j], o_sum.at[k, side], send_sem.at[8], o_sum_sem.at[k, side], peer).start()

    def o_cross(j):
        side = lax.rem(j, 2)

        @pl.when(distance(j) == 0)
        def _():
            for k in range(2):
                wait_bytes(o_dir.at[k, side], o_dir_sem.at[k, side])
                wait_bytes(o_sum.at[k, side], o_sum_sem.at[k, side])

            def total(k, rows):
                return p_out[j, rows, :].astype(F32) + o_dir[k, side].astype(F32) + o_sum[k, side].astype(F32)

            @pl.when(side == y_lo)
            def _():
                for k, rows in ((0, upper), (1, lower)):
                    o_acc[rows, :] = total(k, rows)

            @pl.when(side != y_lo)
            def _():
                for k, rows in ((0, upper), (1, lower)):
                    p_out[j, rows, :] = total(k, rows).astype(BF16)
                remote(p_out.at[j], o_y, send_sem.at[8], o_y_sem.at[0], y_near).start()

    def o_last(j):
        @pl.when(j == tp)
        def _():
            wait_bytes(o_y, o_y_sem.at[0])
            mine = pl.ds(aligned(core, FEATURES), FEATURES)
            theirs = pl.ds(aligned(1 - core, FEATURES), FEATURES)
            o_fin[...] = (o_acc[:, theirs] + o_y[:, theirs].astype(F32)).astype(BF16)
            remote(o_fin, out.at[own_rows, :], send_sem.at[8], fin_sem.at[0], sibling).start()
            out[own_rows, :] = (o_acc[:, mine] + o_y[:, mine].astype(F32)).astype(BF16)

    def step(i, carry):
        def stage(lag, body):
            @pl.when(jnp.logical_and(i >= lag, i < lag + CHUNKS))
            def _():
                body(i - lag)

        @pl.when(i == 1)
        def _():
            wait_bytes(tok.at[near], tok_sem.at[near])
            for peer in (x_next, x_prev, x_far):
                remote(tok.at[near], tok.at[near], send_sem.at[0], tok_sem.at[near], peer).start()

        stage(0, project)
        stage(1, lambda k: pass_on(order(k)))
        stage(2, lambda k: cross(order(k)))
        stage(4, convolve)
        stage(5, forward)
        stage(6, finish)
        stage(7, o_pass)
        stage(8, o_cross)
        stage(9, o_last)
        return carry

    lax.fori_loop(0, CHUNKS + 9, step, 0)

    wait_bytes(o_fin, fin_sem.at[0])
    wait_bytes(tok.at[pl.ds(0, 7)], send_sem.at[0])
    wait_bytes(tok.at[0, :, pl.ds(0, FEATURES)], send_sem.at[0])
    wait_bytes(w_in.at[:, own_feat, :], send_sem.at[1])
    wait_bytes(out_weight, send_sem.at[1])
    wait_bytes(relay, send_sem.at[2])
    wait_bytes(direct, send_sem.at[3])
    wait_bytes(summed, send_sem.at[4])
    wait_bytes(y_recv, send_sem.at[5])
    wait_bytes(state_out.at[pl.ds(0, CHUNKS - 1)], send_sem.at[6])

    @pl.when(core == 0)
    def _():
        wait_bytes(state_out.at[0], send_sem.at[6])

    wait_bytes(gath.at[pl.ds(0, 7)], send_sem.at[7])
    wait_bytes(p_out.at[pl.ds(0, 7)], send_sem.at[8])
    wait_bytes(o_fin, send_sem.at[8])


def local(tokens, in_weight, residues, decay_rates, skip_gain, out_weight):
    channels = in_weight.shape[2]
    vmem = pl.BlockSpec(memory_space=pltpu.VMEM)
    anywhere = pl.BlockSpec(memory_space=pl.ANY)
    dma = pltpu.SemaphoreType.DMA
    scratch = [
        pltpu.VMEM((CHUNKS, ROWS, WIDE), BF16),
        pltpu.VMEM((4, WIDE, 2 * QKV), BF16),
        pltpu.VMEM((2, WIDE, FEATURES), BF16),
        pltpu.VMEM((CHUNKS, 4, ROWS, 2 * QKV), BF16),
        pltpu.VMEM((2, CHUNKS, ROWS, QKV), BF16),
        pltpu.VMEM((2, CHUNKS, ROWS, QKV), BF16),
        pltpu.VMEM((2, CHUNKS, ROWS, QKV), BF16),
        pltpu.VMEM((CHUNKS, ROWS, QKV), BF16),
        pltpu.VMEM((CHUNKS, ROWS, QKV), BF16),
        pltpu.VMEM((ROWS, LANES), F32),
        pltpu.VMEM((ROWS, LANES), F32),
        pltpu.VMEM((ROWS, LANES), F32),
        pltpu.VMEM((MODES, SEGS, LANES), F32),
        pltpu.VMEM((MODES, SEGS, LANES), F32),
        pltpu.VMEM((MODES, SEGS, LANES), F32),
        pltpu.VMEM((3, MODES, SEGS, LANES), F32),
        pltpu.VMEM((MODES, SEGS, LANES), F32),
        pltpu.VMEM((CHUNKS + 1, MODES, LANES), F32),
        pltpu.VMEM((CHUNKS, MODES, LANES), F32),
        pltpu.VMEM((CHUNKS, ROWS, WIDE), BF16),
        pltpu.VMEM((CHUNKS, ROWS, WIDE), BF16),
        pltpu.VMEM((CHUNKS, HALF, WIDE), BF16),
        pltpu.VMEM((2, 2, HALF, WIDE), BF16),
        pltpu.VMEM((2, 2, HALF, WIDE), BF16),
        pltpu.VMEM((ROWS, WIDE), F32),
        pltpu.VMEM((ROWS, WIDE), BF16),
        pltpu.VMEM((ROWS, FEATURES), BF16),
        dma((6,)),
        dma((CHUNKS + 1,)),
        dma((4,)),
        dma((1,)),
        dma((2, CHUNKS)),
        dma((2, CHUNKS)),
        dma((2, CHUNKS)),
        dma((CHUNKS,)),
        dma((CHUNKS + 1,)),
        dma((8, CHUNKS)),
        dma((CHUNKS,)),
        dma((2, 2)),
        dma((2, 2)),
        dma((1,)),
        dma((1,)),
        dma((9,)),
    ]
    return pl.pallas_call(
        kernel,
        out_shape=jax.ShapeDtypeStruct(tokens.shape, BF16),
        in_specs=[anywhere, anywhere, vmem, vmem, vmem, anywhere],
        out_specs=vmem,
        scratch_shapes=scratch,
        compiler_params=pltpu.CompilerParams(
            collective_id=0, has_side_effects=True, vmem_limit_bytes=56 * 2**20
        ),
        name="hyena_block",
    )(tokens, in_weight.transpose(1, 0, 2), residues, decay_rates, skip_gain.reshape(1, channels), out_weight)


def solution(mesh):
    in_specs = (
        P("tp", "seq"),
        P("seq", None, "tp"),
        P(None, "tp"),
        P(None, "tp"),
        P("tp"),
        P("tp", "seq"),
    )
    return jax.shard_map(local, mesh=mesh, in_specs=in_specs, out_specs=P("tp", "seq"), check_vma=False)
```

```python
import functools

import jax
import jax.numpy as jnp
from jax import lax
from jax.experimental import pallas as pl
from jax.experimental.pallas import tpu as pltpu
from jax.sharding import PartitionSpec as P

MESH = pl.DeviceIdType.MESH
F32 = jnp.float32
BF16 = jnp.bfloat16
CHUNKS = 8
ROWS = 128
HALF = 64
LANES = 128
MODES = 16
SEGS = 8
STEPS = 16
QKV = 3 * LANES
FEATURES = 512
WIDE = 1024
DIRECT = 6
CONVOLVE_AT = (12, 12, 13, 14, 15, 16, 18, 19)
FINISH_AT = (14, 14, 15, 16, 17, 18, 19, 20)
CHUNK_ORDERS = (
    (0, 1, 2, 3, 4, 5, 6, 7),
    (1, 0, 3, 2, 4, 5, 6, 7),
    (2, 3, 0, 1, 4, 5, 6, 7),
    (3, 2, 1, 0, 4, 5, 6, 7),
    (4, 5, 0, 2, 1, 3, 6, 7),
    (5, 4, 1, 2, 0, 3, 6, 7),
    (6, 0, 2, 1, 3, 4, 5, 7),
    (7, 1, 3, 0, 2, 4, 5, 6),
)
ORDERS = tuple(sum(chunk << (3 * k) for k, chunk in enumerate(row)) for row in CHUNK_ORDERS)


def remote(src, dst, send_sem, recv_sem, device):
    return pltpu.make_async_remote_copy(
        src_ref=src,
        dst_ref=dst,
        send_sem=send_sem,
        recv_sem=recv_sem,
        device_id=device,
        device_id_type=MESH,
    )


def wait_bytes(ref, sem):
    pltpu.make_async_copy(ref, ref, sem).wait()


def aligned(value, step):
    return pl.multiple_of(value * step, step)


def kernel(
    tokens,
    in_weight,
    residues,
    decay_rates,
    skip_gain,
    out_weight,
    out,
    tok,
    w_in,
    w_out,
    part,
    relay,
    direct,
    summed,
    y_send,
    y_recv,
    s_scr,
    y_scr,
    q_scr,
    decay_b,
    res_b,
    seg_b,
    scan_b,
    ends,
    state_in,
    state_out,
    gath,
    p_out,
    o_relay,
    o_dir,
    o_sum,
    o_acc,
    o_y,
    o_fin,
    local_sem,
    tok_sem,
    far_sem,
    w_sem,
    wo_sem,
    relay_sem,
    direct_sem,
    summed_sem,
    y_sem,
    state_sem,
    gath_sem,
    o_relay_sem,
    o_dir_sem,
    o_sum_sem,
    o_y_sem,
    fin_sem,
    send_sem,
):
    seq = lax.axis_index("seq")
    tp = lax.axis_index("tp")
    core = lax.rem(seq, 2)
    z = lax.rem(seq // 2, 4)
    y_hi = seq // 8
    x = tp // 2
    y_lo = lax.rem(tp, 2)

    def at(dx=0, dz=0, flip_hi=False, flip_lo=False, flip_core=False):
        a = 1 - y_hi if flip_hi else y_hi
        b = lax.rem(z + dz, 4)
        c = 1 - core if flip_core else core
        d = lax.rem(x + dx, 4)
        e = 1 - y_lo if flip_lo else y_lo
        return (a * 8 + b * 2 + c, d * 2 + e)

    sibling = at(flip_core=True)
    z_next, z_prev, z_far = at(dz=1), at(dz=3), at(dz=2)
    y_far = at(flip_hi=True)
    x_next, x_prev = at(dx=1), at(dx=3)
    y_near = at(flip_lo=True)
    diagonals = [at(dz=r, flip_hi=True) for r in (2, 1, 3)]
    peers = [sibling, z_next, z_prev, z_far, y_far, x_next, x_prev, y_near, *diagonals]
    block = y_hi * 4 + z
    lanes = pl.ds(aligned(block, LANES), LANES)

    barrier = pltpu.get_barrier_semaphore()
    for peer in peers:
        pl.semaphore_signal(barrier, inc=1, device_id=peer, device_id_type=MESH)

    own_rows = pl.ds(aligned(core, ROWS), ROWS)
    other_rows = pl.ds(aligned(1 - core, ROWS), ROWS)
    own_feat = pl.ds(aligned(core, FEATURES), FEATURES)
    other_feat = pl.ds(aligned(1 - core, FEATURES), FEATURES)
    pltpu.make_async_copy(tokens.at[own_rows, :], tok.at[tp, :, own_feat], local_sem.at[0]).start()

    def own_weight(r):
        return w_in.at[lax.rem(z + r, 4), own_feat, :]

    for r in (2, 1, 3, 0):
        zi = lax.rem(z + r, 4)
        for h in range(2):
            there = pl.ds(aligned(h * 4 + zi, LANES), LANES)
            for k in range(3):
                pltpu.make_async_copy(
                    in_weight.at[k, :, there],
                    w_in.at[zi, own_feat, pl.ds((h * 3 + k) * LANES, LANES)],
                    local_sem.at[1 + r],
                ).start()
    pltpu.make_async_copy(out_weight, w_out.at[core], local_sem.at[5]).start()

    pl.semaphore_wait(barrier, len(peers))
    remote(tokens.at[other_rows, :], tok.at[tp, :, own_feat], send_sem.at[0], tok_sem.at[CHUNKS], sibling).start()
    wait_bytes(own_weight(2), local_sem.at[3])
    remote(own_weight(2), own_weight(2), send_sem.at[1], w_sem.at[2], sibling).start()
    wait_bytes(tok.at[0, :, pl.ds(0, FEATURES)], local_sem.at[0])
    wait_bytes(tok.at[0, :, pl.ds(0, FEATURES)], tok_sem.at[CHUNKS])
    for peer in (y_near, x_next, x_prev):
        remote(tok.at[tp], tok.at[tp], send_sem.at[0], tok_sem.at[tp], peer).start()
    for r in (1, 3, 0):
        wait_bytes(own_weight(r), local_sem.at[1 + r])
        remote(own_weight(r), own_weight(r), send_sem.at[1], w_sem.at[r], sibling).start()
    remote(out_weight, w_out.at[core], send_sem.at[1], wo_sem.at[0], sibling).start()

    seg_index = lax.broadcasted_iota(jnp.int32, (SEGS, LANES), 0)
    seg_next = (seg_index + 1).astype(F32) * float(STEPS)
    for m in range(MODES):
        rate = jnp.broadcast_to(decay_rates[pl.ds(m, 1), lanes], (SEGS, LANES))
        decay_b[m] = jnp.exp(-rate)
        res_b[m] = jnp.broadcast_to(residues[pl.ds(m, 1), lanes], (SEGS, LANES))
        seg_b[m] = jnp.exp(-rate * seg_next)
        for k in range(3):
            scan_b[k, m] = jnp.where(seg_index >= (1 << k), jnp.exp(-rate * float(STEPS << k)), 0.0)

    @pl.when(core == 0)
    def _():
        state_in[0] = jnp.zeros((MODES, LANES), F32)

    upper, lower = pl.ds(0, HALF), pl.ds(HALF, HALF)
    near = x * 2 + 1 - y_lo
    code = jnp.int32(ORDERS[0])
    for t in range(1, 8):
        code = jnp.where(tp == t, jnp.int32(ORDERS[t]), code)

    def order(i):
        return lax.shift_right_logical(code, 3 * i) & 7

    def column_chunk(dx, row):
        return lax.rem(x + dx, 4) * 2 + row

    def relay_tokens(row, far):
        after, before = column_chunk(1, row), column_chunk(3, row)
        for chunk in (after, before):
            wait_bytes(tok.at[chunk], tok_sem.at[chunk])
        remote(
            tok.at[before, upper], tok.at[before, upper], send_sem.at[0], far_sem.at[far, 0], x_next
        ).start()
        remote(tok.at[after, lower], tok.at[after, lower], send_sem.at[0], far_sem.at[far, 1], x_prev).start()

    def multiply(jc, r):
        zi = lax.rem(z + r, 4)

        part[jc, r] = jnp.dot(tok[jc], w_in[zi], preferred_element_type=F32).astype(BF16)

    first, second = pl.ds(0, QKV), pl.ds(QKV, QKV)

    def project(i):
        jc = order(i)

        for far, row in ((0, y_lo), (1, 1 - y_lo)):

            @pl.when(jc == column_chunk(2, row))
            def _():
                wait_bytes(tok.at[jc, upper], far_sem.at[far, 0])
                wait_bytes(tok.at[jc, lower], far_sem.at[far, 1])

        for r in (2, 1, 3, 0):

            @pl.when(i == 0)
            def _():
                wait_bytes(w_in.at[0, other_feat, :], w_sem.at[r])

            multiply(jc, r)
            if r == 2:
                remote(part.at[jc, 2, :, first], relay.at[0, jc], send_sem.at[2], relay_sem.at[0, jc], z_next).start()
                remote(part.at[jc, 2, :, second], relay.at[1, jc], send_sem.at[2], relay_sem.at[1, jc], z_prev).start()
            elif r == 1:
                remote(part.at[jc, 1, :, second], direct.at[1, jc], send_sem.at[3], direct_sem.at[1, jc], z_next).start()
            elif r == 3:
                remote(part.at[jc, 3, :, first], direct.at[0, jc], send_sem.at[3], direct_sem.at[0, jc], z_prev).start()

    def pass_on(jc):
        for k, r, cols, peer in ((0, 1, first, z_next), (1, 3, second, z_prev)):
            wait_bytes(relay.at[k, jc], relay_sem.at[k, jc])
            relay[k, jc] = (relay[k, jc].astype(F32) + part[jc, r, :, cols].astype(F32)).astype(BF16)
            remote(relay.at[k, jc], summed.at[k, jc], send_sem.at[4], summed_sem.at[k, jc], peer).start()

    def gather_half(jc, k):
        cols = pl.ds(aligned(k, QKV), QKV)
        return part[jc, 0, :, cols].astype(F32) + direct[k, jc].astype(F32) + summed[k, jc].astype(F32)

    def cross(jc):
        for k in range(2):
            wait_bytes(direct.at[k, jc], direct_sem.at[k, jc])
            wait_bytes(summed.at[k, jc], summed_sem.at[k, jc])
        y_send[jc] = gather_half(jc, 1 - y_hi).astype(BF16)
        remote(y_send.at[jc], y_recv.at[jc], send_sem.at[5], y_sem.at[jc], y_far).start()

    def convolve(j):
        wait_bytes(y_recv.at[j], y_sem.at[j])
        total = gather_half(j, y_hi) + y_recv[j].astype(F32)
        q_scr[...] = total[:, :LANES]
        s_scr[...] = total[:, LANES : 2 * LANES] * total[:, 2 * LANES :]
        decay = [decay_b[m] for m in range(MODES)]
        held = [jnp.zeros((SEGS, LANES), F32)] * MODES
        for i in range(STEPS):
            now = s_scr[pl.ds(i, SEGS, stride=STEPS), :]
            held = [decay[m] * held[m] + now for m in range(MODES)]
        for m in range(MODES):
            total = held[m]
            for k in range(3):
                total = total + scan_b[k, m] * pltpu.roll(total, 1 << k, 0)
            ends[m] = total

        @pl.when(jnp.logical_or(core == 1, j > 0))
        def _():
            wait_bytes(state_in.at[j], state_sem.at[j])

        for m in range(MODES):
            before = jnp.broadcast_to(state_in[j, pl.ds(m, 1), :], (SEGS, LANES))
            full = ends[m] + seg_b[m] * before
            state_out[j, pl.ds(m, 1), :] = full[SEGS - 1 :, :]
            ends[m] = jnp.where(seg_index == 0, before, pltpu.roll(full, 1, 0))

        @pl.when(jnp.logical_or(core == 0, j < CHUNKS - 1))
        def _():
            remote(state_out.at[j], state_in.at[j + core], send_sem.at[6], state_sem.at[j + core], sibling).start()

        held = [ends[m] for m in range(MODES)]
        for i in range(STEPS):
            now = s_scr[pl.ds(i, SEGS, stride=STEPS), :]
            held = [decay_b[m] * held[m] + now for m in range(MODES)]
            terms = [res_b[m] * held[m] for m in range(MODES)]
            while len(terms) > 1:
                terms = [terms[k] + terms[k + 1] for k in range(0, len(terms), 2)]
            y_scr[pl.ds(i, SEGS, stride=STEPS), :] = terms[0]
        gain = skip_gain[:, lanes]
        gath[j, :, lanes] = (q_scr[...] * (y_scr[...] + gain * s_scr[...])).astype(BF16)
        own = gath.at[j, :, lanes]
        for peer in (z_far, z_next, z_prev, y_far):
            remote(own, own, send_sem.at[7], gath_sem.at[block, j], peer).start()

        @pl.when(j >= DIRECT)
        def _():
            for peer in diagonals:
                remote(own, own, send_sem.at[7], gath_sem.at[block, j], peer).start()

    def forward(j):
        for r in (1, 3, 2):
            b = y_hi * 4 + lax.rem(z + r, 4)
            there = gath.at[j, :, pl.ds(aligned(b, LANES), LANES)]
            wait_bytes(there, gath_sem.at[b, j])
            remote(there, there, send_sem.at[7], gath_sem.at[b, j], y_far).start()

    def distance(j):
        return lax.rem(j // 2 - x + 4, 4)

    def finish(j):
        for r in range(4):
            b = (1 - y_hi) * 4 + r
            wait_bytes(gath.at[j, :, pl.ds(aligned(b, LANES), LANES)], gath_sem.at[b, j])

        @pl.when(j >= DIRECT)
        def _():
            for r in (1, 3, 2):
                b = y_hi * 4 + lax.rem(z + r, 4)
                wait_bytes(gath.at[j, :, pl.ds(aligned(b, LANES), LANES)], gath_sem.at[b, j])

        @pl.when(j == 0)
        def _():
            pltpu.make_async_copy(out_weight, w_out.at[core], local_sem.at[5]).wait()
            wait_bytes(w_out.at[1 - core], wo_sem.at[0])

        for h in range(2):
            cols = pl.ds(h * FEATURES, FEATURES)
            p_out[j, :, cols] = jnp.dot(gath[j], w_out[h], preferred_element_type=F32).astype(BF16)
        dx = distance(j)
        side = lax.rem(j, 2)

        @pl.when(dx == 2)
        def _():
            remote(p_out.at[j, upper], o_relay.at[j], send_sem.at[8], o_relay_sem.at[j], x_next).start()
            remote(p_out.at[j, lower], o_relay.at[j], send_sem.at[8], o_relay_sem.at[j], x_prev).start()

        @pl.when(dx == 1)
        def _():
            remote(p_out.at[j, lower], o_dir.at[1, side], send_sem.at[8], o_dir_sem.at[1, side], x_next).start()

        @pl.when(dx == 3)
        def _():
            remote(p_out.at[j, upper], o_dir.at[0, side], send_sem.at[8], o_dir_sem.at[0, side], x_prev).start()

    def o_pass(j):
        dx = distance(j)
        side = lax.rem(j, 2)
        for want, rows, k, peer in ((1, upper, 0, x_next), (3, lower, 1, x_prev)):

            @pl.when(dx == want)
            def _():
                wait_bytes(o_relay.at[j], o_relay_sem.at[j])
                o_relay[j] = (o_relay[j].astype(F32) + p_out[j, rows, :].astype(F32)).astype(BF16)
                remote(o_relay.at[j], o_sum.at[k, side], send_sem.at[8], o_sum_sem.at[k, side], peer).start()

    def o_cross(j):
        side = lax.rem(j, 2)

        @pl.when(distance(j) == 0)
        def _():
            for k in range(2):
                wait_bytes(o_dir.at[k, side], o_dir_sem.at[k, side])
                wait_bytes(o_sum.at[k, side], o_sum_sem.at[k, side])

            def total(k, rows):
                return p_out[j, rows, :].astype(F32) + o_dir[k, side].astype(F32) + o_sum[k, side].astype(F32)

            @pl.when(side == y_lo)
            def _():
                for k, rows in ((0, upper), (1, lower)):
                    o_acc[rows, :] = total(k, rows)

            @pl.when(side != y_lo)
            def _():
                for k, rows in ((0, upper), (1, lower)):
                    p_out[j, rows, :] = total(k, rows).astype(BF16)
                remote(p_out.at[j], o_y, send_sem.at[8], o_y_sem.at[0], y_near).start()

    def o_last(j):
        @pl.when(j == tp)
        def _():
            wait_bytes(o_y, o_y_sem.at[0])
            mine = pl.ds(aligned(core, FEATURES), FEATURES)
            theirs = pl.ds(aligned(1 - core, FEATURES), FEATURES)
            o_fin[...] = (o_acc[:, theirs] + o_y[:, theirs].astype(F32)).astype(BF16)
            remote(o_fin, out.at[own_rows, :], send_sem.at[8], fin_sem.at[0], sibling).start()
            out[own_rows, :] = (o_acc[:, mine] + o_y[:, mine].astype(F32)).astype(BF16)

    def step(n, carry):
        def stage(times, body):
            first_chunk, end_chunk = jnp.int32(0), jnp.int32(0)
            for time in times:
                first_chunk = first_chunk + jnp.where(n > time, 1, 0)
                end_chunk = end_chunk + jnp.where(n >= time, 1, 0)

            def call(j, unused):
                body(j)
                return unused

            lax.fori_loop(first_chunk, end_chunk, call, 0)

        @pl.when(n == 2)
        def _():
            wait_bytes(tok.at[near], tok_sem.at[near])
            relay_tokens(y_lo, 0)
            for peer in (x_next, x_prev):
                remote(tok.at[near], tok.at[near], send_sem.at[0], tok_sem.at[near], peer).start()

        @pl.when(n == 6)
        def _():
            relay_tokens(1 - y_lo, 1)

        stage(range(0, 16, 2), project)
        stage(range(1, 17, 2), lambda k: pass_on(order(k)))
        stage(range(3, 19, 2), lambda k: cross(order(k)))
        stage(CONVOLVE_AT, convolve)
        stage([t + 1 for t in CONVOLVE_AT[:DIRECT]], forward)
        stage(FINISH_AT, finish)
        stage([t + 1 for t in FINISH_AT], o_pass)
        stage([t + 2 for t in FINISH_AT], o_cross)
        stage([t + 3 for t in FINISH_AT], o_last)
        return carry

    lax.fori_loop(0, FINISH_AT[-1] + 4, step, 0)

    wait_bytes(o_fin, fin_sem.at[0])
    wait_bytes(tok.at[pl.ds(0, 7)], send_sem.at[0])
    wait_bytes(tok.at[0, :, pl.ds(0, FEATURES)], send_sem.at[0])
    wait_bytes(w_in.at[:, own_feat, :], send_sem.at[1])
    wait_bytes(out_weight, send_sem.at[1])
    wait_bytes(relay, send_sem.at[2])
    wait_bytes(direct, send_sem.at[3])
    wait_bytes(summed, send_sem.at[4])
    wait_bytes(y_recv, send_sem.at[5])
    wait_bytes(state_out.at[pl.ds(0, CHUNKS - 1)], send_sem.at[6])

    @pl.when(core == 0)
    def _():
        wait_bytes(state_out.at[0], send_sem.at[6])

    wait_bytes(gath.at[pl.ds(0, 7)], send_sem.at[7])
    wait_bytes(p_out.at[pl.ds(0, 7)], send_sem.at[8])
    wait_bytes(o_fin, send_sem.at[8])


def local(tokens, in_weight, residues, decay_rates, skip_gain, out_weight):
    channels = in_weight.shape[2]
    vmem = pl.BlockSpec(memory_space=pltpu.VMEM)
    anywhere = pl.BlockSpec(memory_space=pl.ANY)
    dma = pltpu.SemaphoreType.DMA
    scratch = [
        pltpu.VMEM((CHUNKS, ROWS, WIDE), BF16),
        pltpu.VMEM((4, WIDE, 2 * QKV), BF16),
        pltpu.VMEM((2, WIDE, FEATURES), BF16),
        pltpu.VMEM((CHUNKS, 4, ROWS, 2 * QKV), BF16),
        pltpu.VMEM((2, CHUNKS, ROWS, QKV), BF16),
        pltpu.VMEM((2, CHUNKS, ROWS, QKV), BF16),
        pltpu.VMEM((2, CHUNKS, ROWS, QKV), BF16),
        pltpu.VMEM((CHUNKS, ROWS, QKV), BF16),
        pltpu.VMEM((CHUNKS, ROWS, QKV), BF16),
        pltpu.VMEM((ROWS, LANES), F32),
        pltpu.VMEM((ROWS, LANES), F32),
        pltpu.VMEM((ROWS, LANES), F32),
        pltpu.VMEM((MODES, SEGS, LANES), F32),
        pltpu.VMEM((MODES, SEGS, LANES), F32),
        pltpu.VMEM((MODES, SEGS, LANES), F32),
        pltpu.VMEM((3, MODES, SEGS, LANES), F32),
        pltpu.VMEM((MODES, SEGS, LANES), F32),
        pltpu.VMEM((CHUNKS + 1, MODES, LANES), F32),
        pltpu.VMEM((CHUNKS, MODES, LANES), F32),
        pltpu.VMEM((CHUNKS, ROWS, WIDE), BF16),
        pltpu.VMEM((CHUNKS, ROWS, WIDE), BF16),
        pltpu.VMEM((CHUNKS, HALF, WIDE), BF16),
        pltpu.VMEM((2, 2, HALF, WIDE), BF16),
        pltpu.VMEM((2, 2, HALF, WIDE), BF16),
        pltpu.VMEM((ROWS, WIDE), F32),
        pltpu.VMEM((ROWS, WIDE), BF16),
        pltpu.VMEM((ROWS, FEATURES), BF16),
        dma((6,)),
        dma((CHUNKS + 1,)),
        dma((2, 2)),
        dma((4,)),
        dma((1,)),
        dma((2, CHUNKS)),
        dma((2, CHUNKS)),
        dma((2, CHUNKS)),
        dma((CHUNKS,)),
        dma((CHUNKS + 1,)),
        dma((8, CHUNKS)),
        dma((CHUNKS,)),
        dma((2, 2)),
        dma((2, 2)),
        dma((1,)),
        dma((1,)),
        dma((9,)),
    ]
    return pl.pallas_call(
        kernel,
        out_shape=jax.ShapeDtypeStruct(tokens.shape, BF16),
        in_specs=[anywhere, anywhere, vmem, vmem, vmem, anywhere],
        out_specs=vmem,
        scratch_shapes=scratch,
        compiler_params=pltpu.CompilerParams(
            collective_id=0, has_side_effects=True, vmem_limit_bytes=56 * 2**20
        ),
        name="hyena_block",
    )(tokens, in_weight.transpose(1, 0, 2), residues, decay_rates, skip_gain.reshape(1, channels), out_weight)


def solution(mesh):
    in_specs = (
        P("tp", "seq"),
        P("seq", None, "tp"),
        P(None, "tp"),
        P(None, "tp"),
        P("tp"),
        P("tp", "seq"),
    )
    return jax.shard_map(local, mesh=mesh, in_specs=in_specs, out_specs=P("tp", "seq"), check_vma=False)
```

```python
import functools

import jax
import jax.numpy as jnp
from jax import lax
from jax.experimental import pallas as pl
from jax.experimental.pallas import tpu as pltpu
from jax.sharding import PartitionSpec as P

MESH = pl.DeviceIdType.MESH
F32 = jnp.float32
BF16 = jnp.bfloat16
CHUNKS = 8
ROWS = 128
HALF = 64
QUARTER = 32
LANES = 128
MODES = 16
SEGS = 8
STEPS = 16
QKV = 3 * LANES
FEATURES = 512
WIDE = 1024
DIRECT = 6
CONVOLVE_AT = (12, 12, 13, 14, 15, 16, 18, 19)
FINISH_AT = (14, 14, 15, 16, 17, 18, 19, 20)
CHUNK_ORDERS = (
    (0, 1, 2, 3, 4, 5, 6, 7),
    (1, 0, 3, 2, 4, 5, 6, 7),
    (2, 3, 0, 1, 4, 5, 6, 7),
    (3, 2, 1, 0, 4, 5, 6, 7),
    (4, 5, 0, 2, 1, 3, 6, 7),
    (5, 4, 1, 2, 0, 3, 6, 7),
    (6, 0, 2, 1, 3, 4, 5, 7),
    (7, 1, 3, 0, 2, 4, 5, 6),
)
ORDERS = tuple(sum(chunk << (3 * k) for k, chunk in enumerate(row)) for row in CHUNK_ORDERS)


def remote(src, dst, send_sem, recv_sem, device):
    return pltpu.make_async_remote_copy(
        src_ref=src,
        dst_ref=dst,
        send_sem=send_sem,
        recv_sem=recv_sem,
        device_id=device,
        device_id_type=MESH,
    )


def wait_bytes(ref, sem):
    pltpu.make_async_copy(ref, ref, sem).wait()


def aligned(value, step):
    return pl.multiple_of(value * step, step)


def kernel(
    tokens,
    in_weight,
    residues,
    decay_rates,
    skip_gain,
    out_weight,
    out,
    tok,
    w_in,
    w_out,
    part,
    relay,
    direct,
    summed,
    y_send,
    y_recv,
    s_scr,
    y_scr,
    q_scr,
    decay_b,
    res_b,
    seg_b,
    scan_b,
    ends,
    state_in,
    state_out,
    gath,
    p_out,
    o_relay,
    o_y_in,
    o_in,
    o_sib,
    o_send,
    o_y,
    local_sem,
    tok_sem,
    far_sem,
    w_sem,
    wo_sem,
    relay_sem,
    direct_sem,
    summed_sem,
    y_sem,
    state_sem,
    gath_sem,
    o_relay_sem,
    o_y_in_sem,
    o_in_sem,
    o_sib_sem,
    o_y_sem,
    send_sem,
):
    seq = lax.axis_index("seq")
    tp = lax.axis_index("tp")
    core = lax.rem(seq, 2)
    z = lax.rem(seq // 2, 4)
    y_hi = seq // 8
    x = tp // 2
    y_lo = lax.rem(tp, 2)

    def at(dx=0, dz=0, flip_hi=False, flip_lo=False, flip_core=False):
        a = 1 - y_hi if flip_hi else y_hi
        b = lax.rem(z + dz, 4)
        c = 1 - core if flip_core else core
        d = lax.rem(x + dx, 4)
        e = 1 - y_lo if flip_lo else y_lo
        return (a * 8 + b * 2 + c, d * 2 + e)

    sibling = at(flip_core=True)
    z_next, z_prev, z_far = at(dz=1), at(dz=3), at(dz=2)
    y_far = at(flip_hi=True)
    x_next, x_prev = at(dx=1), at(dx=3)
    y_near = at(flip_lo=True)
    diagonals = [at(dz=r, flip_hi=True) for r in (2, 1, 3)]
    peers = [sibling, z_next, z_prev, z_far, y_far, x_next, x_prev, y_near, *diagonals]
    peers += [at(dx=1, flip_core=True), at(dx=3, flip_core=True)]
    block = y_hi * 4 + z
    lanes = pl.ds(aligned(block, LANES), LANES)

    barrier = pltpu.get_barrier_semaphore()
    for peer in peers:
        pl.semaphore_signal(barrier, inc=1, device_id=peer, device_id_type=MESH)

    own_rows = pl.ds(aligned(core, ROWS), ROWS)
    other_rows = pl.ds(aligned(1 - core, ROWS), ROWS)
    own_feat = pl.ds(aligned(core, FEATURES), FEATURES)
    other_feat = pl.ds(aligned(1 - core, FEATURES), FEATURES)
    pltpu.make_async_copy(tokens.at[own_rows, :], tok.at[tp, :, own_feat], local_sem.at[0]).start()

    def own_weight(r):
        return w_in.at[lax.rem(z + r, 4), own_feat, :]

    for r in (2, 1, 3, 0):
        zi = lax.rem(z + r, 4)
        for h in range(2):
            there = pl.ds(aligned(h * 4 + zi, LANES), LANES)
            for k in range(3):
                pltpu.make_async_copy(
                    in_weight.at[k, :, there],
                    w_in.at[zi, own_feat, pl.ds((h * 3 + k) * LANES, LANES)],
                    local_sem.at[1 + r],
                ).start()
    pltpu.make_async_copy(out_weight, w_out.at[core], local_sem.at[5]).start()

    pl.semaphore_wait(barrier, len(peers))
    remote(tokens.at[other_rows, :], tok.at[tp, :, own_feat], send_sem.at[0], tok_sem.at[CHUNKS], sibling).start()
    wait_bytes(own_weight(2), local_sem.at[3])
    remote(own_weight(2), own_weight(2), send_sem.at[1], w_sem.at[2], sibling).start()
    wait_bytes(tok.at[0, :, pl.ds(0, FEATURES)], local_sem.at[0])
    wait_bytes(tok.at[0, :, pl.ds(0, FEATURES)], tok_sem.at[CHUNKS])
    for peer in (y_near, x_next, x_prev):
        remote(tok.at[tp], tok.at[tp], send_sem.at[0], tok_sem.at[tp], peer).start()
    for r in (1, 3, 0):
        wait_bytes(own_weight(r), local_sem.at[1 + r])
        remote(own_weight(r), own_weight(r), send_sem.at[1], w_sem.at[r], sibling).start()
    remote(out_weight, w_out.at[core], send_sem.at[1], wo_sem.at[0], sibling).start()

    seg_index = lax.broadcasted_iota(jnp.int32, (SEGS, LANES), 0)
    seg_next = (seg_index + 1).astype(F32) * float(STEPS)
    for m in range(MODES):
        rate = jnp.broadcast_to(decay_rates[pl.ds(m, 1), lanes], (SEGS, LANES))
        decay_b[m] = jnp.exp(-rate)
        res_b[m] = jnp.broadcast_to(residues[pl.ds(m, 1), lanes], (SEGS, LANES))
        seg_b[m] = jnp.exp(-rate * seg_next)
        for k in range(3):
            scan_b[k, m] = jnp.where(seg_index >= (1 << k), jnp.exp(-rate * float(STEPS << k)), 0.0)

    @pl.when(core == 0)
    def _():
        state_in[0] = jnp.zeros((MODES, LANES), F32)

    upper, lower = pl.ds(0, HALF), pl.ds(HALF, HALF)
    near = x * 2 + 1 - y_lo
    code = jnp.int32(ORDERS[0])
    for t in range(1, 8):
        code = jnp.where(tp == t, jnp.int32(ORDERS[t]), code)

    def order(i):
        return lax.shift_right_logical(code, 3 * i) & 7

    def column_chunk(dx, row):
        return lax.rem(x + dx, 4) * 2 + row

    def relay_tokens(row, far):
        after, before = column_chunk(1, row), column_chunk(3, row)
        for chunk in (after, before):
            wait_bytes(tok.at[chunk], tok_sem.at[chunk])
        remote(
            tok.at[before, upper], tok.at[before, upper], send_sem.at[0], far_sem.at[far, 0], x_next
        ).start()
        remote(tok.at[after, lower], tok.at[after, lower], send_sem.at[0], far_sem.at[far, 1], x_prev).start()

    def multiply(jc, r):
        zi = lax.rem(z + r, 4)

        part[jc, r] = jnp.dot(tok[jc], w_in[zi], preferred_element_type=F32).astype(BF16)

    first, second = pl.ds(0, QKV), pl.ds(QKV, QKV)

    def project(i):
        jc = order(i)

        for far, row in ((0, y_lo), (1, 1 - y_lo)):

            @pl.when(jc == column_chunk(2, row))
            def _():
                wait_bytes(tok.at[jc, upper], far_sem.at[far, 0])
                wait_bytes(tok.at[jc, lower], far_sem.at[far, 1])

        for r in (2, 1, 3, 0):

            @pl.when(i == 0)
            def _():
                wait_bytes(w_in.at[0, other_feat, :], w_sem.at[r])

            multiply(jc, r)
            if r == 2:
                remote(part.at[jc, 2, :, first], relay.at[0, jc], send_sem.at[2], relay_sem.at[0, jc], z_next).start()
                remote(part.at[jc, 2, :, second], relay.at[1, jc], send_sem.at[2], relay_sem.at[1, jc], z_prev).start()
            elif r == 1:
                remote(part.at[jc, 1, :, second], direct.at[1, jc], send_sem.at[3], direct_sem.at[1, jc], z_next).start()
            elif r == 3:
                remote(part.at[jc, 3, :, first], direct.at[0, jc], send_sem.at[3], direct_sem.at[0, jc], z_prev).start()

    def pass_on(jc):
        for k, r, cols, peer in ((0, 1, first, z_next), (1, 3, second, z_prev)):
            wait_bytes(relay.at[k, jc], relay_sem.at[k, jc])
            relay[k, jc] = (relay[k, jc].astype(F32) + part[jc, r, :, cols].astype(F32)).astype(BF16)
            remote(relay.at[k, jc], summed.at[k, jc], send_sem.at[4], summed_sem.at[k, jc], peer).start()

    def gather_half(jc, k):
        cols = pl.ds(aligned(k, QKV), QKV)
        return part[jc, 0, :, cols].astype(F32) + direct[k, jc].astype(F32) + summed[k, jc].astype(F32)

    def cross(jc):
        for k in range(2):
            wait_bytes(direct.at[k, jc], direct_sem.at[k, jc])
            wait_bytes(summed.at[k, jc], summed_sem.at[k, jc])
        y_send[jc] = gather_half(jc, 1 - y_hi).astype(BF16)
        remote(y_send.at[jc], y_recv.at[jc], send_sem.at[5], y_sem.at[jc], y_far).start()

    def convolve(j):
        wait_bytes(y_recv.at[j], y_sem.at[j])
        total = gather_half(j, y_hi) + y_recv[j].astype(F32)
        q_scr[...] = total[:, :LANES]
        s_scr[...] = total[:, LANES : 2 * LANES] * total[:, 2 * LANES :]
        decay = [decay_b[m] for m in range(MODES)]
        held = [jnp.zeros((SEGS, LANES), F32)] * MODES
        for i in range(STEPS):
            now = s_scr[pl.ds(i, SEGS, stride=STEPS), :]
            held = [decay[m] * held[m] + now for m in range(MODES)]
        for m in range(MODES):
            total = held[m]
            for k in range(3):
                total = total + scan_b[k, m] * pltpu.roll(total, 1 << k, 0)
            ends[m] = total

        @pl.when(jnp.logical_or(core == 1, j > 0))
        def _():
            wait_bytes(state_in.at[j], state_sem.at[j])

        for m in range(MODES):
            before = jnp.broadcast_to(state_in[j, pl.ds(m, 1), :], (SEGS, LANES))
            full = ends[m] + seg_b[m] * before
            state_out[j, pl.ds(m, 1), :] = full[SEGS - 1 :, :]
            ends[m] = jnp.where(seg_index == 0, before, pltpu.roll(full, 1, 0))

        @pl.when(jnp.logical_or(core == 0, j < CHUNKS - 1))
        def _():
            remote(state_out.at[j], state_in.at[j + core], send_sem.at[6], state_sem.at[j + core], sibling).start()

        held = [ends[m] for m in range(MODES)]
        for i in range(STEPS):
            now = s_scr[pl.ds(i, SEGS, stride=STEPS), :]
            held = [decay_b[m] * held[m] + now for m in range(MODES)]
            terms = [res_b[m] * held[m] for m in range(MODES)]
            while len(terms) > 1:
                terms = [terms[k] + terms[k + 1] for k in range(0, len(terms), 2)]
            y_scr[pl.ds(i, SEGS, stride=STEPS), :] = terms[0]
        gain = skip_gain[:, lanes]
        gath[j, :, lanes] = (q_scr[...] * (y_scr[...] + gain * s_scr[...])).astype(BF16)
        own = gath.at[j, :, lanes]
        for peer in (z_far, z_next, z_prev, y_far):
            remote(own, own, send_sem.at[7], gath_sem.at[block, j], peer).start()

        @pl.when(j >= DIRECT)
        def _():
            for peer in diagonals:
                remote(own, own, send_sem.at[7], gath_sem.at[block, j], peer).start()

    def forward(j):
        for r in (1, 3, 2):
            b = y_hi * 4 + lax.rem(z + r, 4)
            there = gath.at[j, :, pl.ds(aligned(b, LANES), LANES)]
            wait_bytes(there, gath_sem.at[b, j])
            remote(there, there, send_sem.at[7], gath_sem.at[b, j], y_far).start()

    def distance(j):
        return lax.rem(j // 2 - x + 4, 4)

    def finish(j):
        for r in range(4):
            b = (1 - y_hi) * 4 + r
            wait_bytes(gath.at[j, :, pl.ds(aligned(b, LANES), LANES)], gath_sem.at[b, j])

        @pl.when(j >= DIRECT)
        def _():
            for r in (1, 3, 2):
                b = y_hi * 4 + lax.rem(z + r, 4)
                wait_bytes(gath.at[j, :, pl.ds(aligned(b, LANES), LANES)], gath_sem.at[b, j])

        @pl.when(j == 0)
        def _():
            pltpu.make_async_copy(out_weight, w_out.at[core], local_sem.at[5]).wait()
            wait_bytes(w_out.at[1 - core], wo_sem.at[0])

        for h in range(2):
            cols = pl.ds(h * FEATURES, FEATURES)
            p_out[j, :, cols] = jnp.dot(gath[j], w_out[h], preferred_element_type=F32).astype(BF16)
        o_begin(j, 0)

        @pl.when(row_of(j) != y_lo)
        def _():
            remote(p_out.at[j, lower], o_y_in.at[j], send_sem.at[8], o_y_in_sem.at[j], y_near).start()

    def row_of(j):
        return lax.rem(j, 2)

    def quarter(part_index, k):
        return pl.ds(part_index * HALF + k * QUARTER, QUARTER)

    def own_columns(flip):
        return pl.ds(aligned(1 - core if flip else core, FEATURES), FEATURES)

    def to_column(src, j, s, kind, k, dx):
        for flip in (False, True):
            remote(
                src.at[:, own_columns(flip)],
                o_in.at[row_of(j), s, kind, k, core],
                send_sem.at[8],
                o_in_sem.at[row_of(j), s],
                at(dx=dx, flip_core=flip),
            ).start()

    def o_begin(j, s):
        dx = distance(j)

        @pl.when(dx == 2)
        def _():
            for k, peer in ((0, x_next), (1, x_prev)):
                remote(
                    p_out.at[j, quarter(s, k)], o_relay.at[s, j], send_sem.at[8], o_relay_sem.at[s, j], peer
                ).start()

        @pl.when(dx == 1)
        def _():
            to_column(p_out.at[j, quarter(s, 1)], j, s, 0, 1, 1)

        @pl.when(dx == 3)
        def _():
            to_column(p_out.at[j, quarter(s, 0)], j, s, 0, 0, 3)

        @pl.when(dx == 0)
        def _():
            rows = pl.ds(s * HALF, HALF)
            remote(
                p_out.at[j, rows, own_columns(True)],
                o_sib.at[row_of(j), s],
                send_sem.at[8],
                o_sib_sem.at[row_of(j), s],
                sibling,
            ).start()

    def o_pass(j, s):
        dx = distance(j)
        for want, k in ((1, 0), (3, 1)):

            @pl.when(dx == want)
            def _():
                wait_bytes(o_relay.at[s, j], o_relay_sem.at[s, j])
                o_relay[s, j] = (o_relay[s, j].astype(F32) + p_out[j, quarter(s, k), :].astype(F32)).astype(BF16)
                to_column(o_relay.at[s, j], j, s, 1, k, want)

    def o_total(j, s, k, mine):
        side = row_of(j)
        source = core if mine else 1 - core
        if mine:
            base = p_out[j, quarter(s, k), own_columns(False)]
        else:
            base = o_sib[side, s, pl.ds(k * QUARTER, QUARTER), :]
        return (
            base.astype(F32) + o_in[side, s, 0, k, source].astype(F32) + o_in[side, s, 1, k, source].astype(F32)
        )

    def o_arrived(j, s):
        wait_bytes(o_in.at[row_of(j), s], o_in_sem.at[row_of(j), s])
        wait_bytes(o_sib.at[row_of(j), s], o_sib_sem.at[row_of(j), s])

    def o_second(j):
        @pl.when(row_of(j) == y_lo)
        def _():
            wait_bytes(o_y_in.at[j], o_y_in_sem.at[j])
            p_out[j, lower, :] = (p_out[j, lower, :].astype(F32) + o_y_in[j].astype(F32)).astype(BF16)
            o_begin(j, 1)

        o_pass(j, 0)

    def o_third(j):
        @pl.when(row_of(j) == y_lo)
        def _():
            o_pass(j, 1)

        @pl.when(jnp.logical_and(distance(j) == 0, row_of(j) != y_lo))
        def _():
            o_arrived(j, 0)
            for k in range(2):
                for mine in (True, False):
                    o_send[core if mine else 1 - core, k] = o_total(j, 0, k, mine).astype(BF16)
            remote(o_send, o_y, send_sem.at[8], o_y_sem.at[0], y_near).start()

    def o_last(j):
        @pl.when(j == tp)
        def _():
            o_arrived(j, 0)
            o_arrived(j, 1)
            for s in (1, 0):
                if s == 0:
                    wait_bytes(o_y, o_y_sem.at[0])
                for k in range(2):
                    for mine in (True, False):
                        source = core if mine else 1 - core
                        total = o_total(j, s, k, mine)
                        if s == 0:
                            total = total + o_y[source, k].astype(F32)
                        start = source * ROWS + s * HALF + k * QUARTER
                        out[pl.ds(pl.multiple_of(start, QUARTER), QUARTER), :] = total.astype(BF16)

    def step(n, carry):
        def stage(times, body):
            first_chunk, end_chunk = jnp.int32(0), jnp.int32(0)
            for time in times:
                first_chunk = first_chunk + jnp.where(n > time, 1, 0)
                end_chunk = end_chunk + jnp.where(n >= time, 1, 0)

            def call(j, unused):
                body(j)
                return unused

            lax.fori_loop(first_chunk, end_chunk, call, 0)

        @pl.when(n == 2)
        def _():
            wait_bytes(tok.at[near], tok_sem.at[near])
            relay_tokens(y_lo, 0)
            for peer in (x_next, x_prev):
                remote(tok.at[near], tok.at[near], send_sem.at[0], tok_sem.at[near], peer).start()

        @pl.when(n == 6)
        def _():
            relay_tokens(1 - y_lo, 1)

        stage(range(0, 16, 2), project)
        stage(range(1, 17, 2), lambda k: pass_on(order(k)))
        stage(range(3, 19, 2), lambda k: cross(order(k)))
        stage(CONVOLVE_AT, convolve)
        stage([t + 1 for t in CONVOLVE_AT[:DIRECT]], forward)
        stage(FINISH_AT, finish)
        stage([t + 1 for t in FINISH_AT], o_second)
        stage([t + 2 for t in FINISH_AT], o_third)
        stage([t + 3 for t in FINISH_AT], o_last)
        return carry

    lax.fori_loop(0, FINISH_AT[-1] + 4, step, 0)

    wait_bytes(tok.at[pl.ds(0, 7)], send_sem.at[0])
    wait_bytes(tok.at[0, :, pl.ds(0, FEATURES)], send_sem.at[0])
    wait_bytes(w_in.at[:, own_feat, :], send_sem.at[1])
    wait_bytes(out_weight, send_sem.at[1])
    wait_bytes(relay, send_sem.at[2])
    wait_bytes(direct, send_sem.at[3])
    wait_bytes(summed, send_sem.at[4])
    wait_bytes(y_recv, send_sem.at[5])
    wait_bytes(state_out.at[pl.ds(0, CHUNKS - 1)], send_sem.at[6])

    @pl.when(core == 0)
    def _():
        wait_bytes(state_out.at[0], send_sem.at[6])

    wait_bytes(gath.at[pl.ds(0, 7)], send_sem.at[7])
    wait_bytes(p_out.at[pl.ds(0, 7)], send_sem.at[8])
    wait_bytes(p_out.at[0, pl.ds(0, 3 * QUARTER)], send_sem.at[8])


def local(tokens, in_weight, residues, decay_rates, skip_gain, out_weight):
    channels = in_weight.shape[2]
    vmem = pl.BlockSpec(memory_space=pltpu.VMEM)
    anywhere = pl.BlockSpec(memory_space=pl.ANY)
    dma = pltpu.SemaphoreType.DMA
    scratch = [
        pltpu.VMEM((CHUNKS, ROWS, WIDE), BF16),
        pltpu.VMEM((4, WIDE, 2 * QKV), BF16),
        pltpu.VMEM((2, WIDE, FEATURES), BF16),
        pltpu.VMEM((CHUNKS, 4, ROWS, 2 * QKV), BF16),
        pltpu.VMEM((2, CHUNKS, ROWS, QKV), BF16),
        pltpu.VMEM((2, CHUNKS, ROWS, QKV), BF16),
        pltpu.VMEM((2, CHUNKS, ROWS, QKV), BF16),
        pltpu.VMEM((CHUNKS, ROWS, QKV), BF16),
        pltpu.VMEM((CHUNKS, ROWS, QKV), BF16),
        pltpu.VMEM((ROWS, LANES), F32),
        pltpu.VMEM((ROWS, LANES), F32),
        pltpu.VMEM((ROWS, LANES), F32),
        pltpu.VMEM((MODES, SEGS, LANES), F32),
        pltpu.VMEM((MODES, SEGS, LANES), F32),
        pltpu.VMEM((MODES, SEGS, LANES), F32),
        pltpu.VMEM((3, MODES, SEGS, LANES), F32),
        pltpu.VMEM((MODES, SEGS, LANES), F32),
        pltpu.VMEM((CHUNKS + 1, MODES, LANES), F32),
        pltpu.VMEM((CHUNKS, MODES, LANES), F32),
        pltpu.VMEM((CHUNKS, ROWS, WIDE), BF16),
        pltpu.VMEM((CHUNKS, ROWS, WIDE), BF16),
        pltpu.VMEM((2, CHUNKS, QUARTER, WIDE), BF16),
        pltpu.VMEM((CHUNKS, HALF, WIDE), BF16),
        pltpu.VMEM((2, 2, 2, 2, 2, QUARTER, FEATURES), BF16),
        pltpu.VMEM((2, 2, HALF, FEATURES), BF16),
        pltpu.VMEM((2, 2, QUARTER, FEATURES), BF16),
        pltpu.VMEM((2, 2, QUARTER, FEATURES), BF16),
        dma((6,)),
        dma((CHUNKS + 1,)),
        dma((2, 2)),
        dma((4,)),
        dma((1,)),
        dma((2, CHUNKS)),
        dma((2, CHUNKS)),
        dma((2, CHUNKS)),
        dma((CHUNKS,)),
        dma((CHUNKS + 1,)),
        dma((8, CHUNKS)),
        dma((2, CHUNKS)),
        dma((CHUNKS,)),
        dma((2, 2)),
        dma((2, 2)),
        dma((1,)),
        dma((9,)),
    ]
    return pl.pallas_call(
        kernel,
        out_shape=jax.ShapeDtypeStruct(tokens.shape, BF16),
        in_specs=[anywhere, anywhere, vmem, vmem, vmem, anywhere],
        out_specs=vmem,
        scratch_shapes=scratch,
        compiler_params=pltpu.CompilerParams(
            collective_id=0, has_side_effects=True, vmem_limit_bytes=56 * 2**20
        ),
        name="hyena_block",
    )(tokens, in_weight.transpose(1, 0, 2), residues, decay_rates, skip_gain.reshape(1, channels), out_weight)


def solution(mesh):
    in_specs = (
        P("tp", "seq"),
        P("seq", None, "tp"),
        P(None, "tp"),
        P(None, "tp"),
        P("tp"),
        P("tp", "seq"),
    )
    return jax.shard_map(local, mesh=mesh, in_specs=in_specs, out_specs=P("tp", "seq"), check_vma=False)
```

```python
import functools

import jax
import jax.numpy as jnp
from jax import lax
from jax.experimental import pallas as pl
from jax.experimental.pallas import tpu as pltpu
from jax.sharding import PartitionSpec as P

MESH = pl.DeviceIdType.MESH
F32 = jnp.float32
BF16 = jnp.bfloat16
CHUNKS = 8
ROWS = 128
HALF = 64
QUARTER = 32
LANES = 128
MODES = 16
SEGS = 8
STEPS = 16
QKV = 3 * LANES
FEATURES = 512
WIDE = 1024
DIRECT = 5
SPLIT = 6
EARLY = 7
LATE = CHUNKS - EARLY
PROJECT_LATE_AT = (9,)
START_LATE_AT = (13,)
CONVOLVE_AT = (12, 12, 13, 14, 14, 16, 16, 17)
FINISH_AT = (14, 14, 15, 16, 16, 17, 17, 18)
CHUNK_ORDERS = (
    (0, 1, 2, 3, 4, 5, 6, 7),
    (1, 0, 3, 2, 4, 5, 6, 7),
    (2, 3, 0, 1, 4, 5, 6, 7),
    (3, 2, 1, 0, 4, 5, 6, 7),
    (4, 5, 0, 2, 1, 3, 6, 7),
    (5, 4, 1, 2, 0, 3, 6, 7),
    (6, 0, 2, 1, 3, 4, 5, 7),
    (7, 1, 3, 0, 2, 4, 5, 6),
)
ORDERS = tuple(sum(chunk << (3 * k) for k, chunk in enumerate(row)) for row in CHUNK_ORDERS)


def remote(src, dst, send_sem, recv_sem, device):
    return pltpu.make_async_remote_copy(
        src_ref=src,
        dst_ref=dst,
        send_sem=send_sem,
        recv_sem=recv_sem,
        device_id=device,
        device_id_type=MESH,
    )


def wait_bytes(ref, sem):
    pltpu.make_async_copy(ref, ref, sem).wait()


def aligned(value, step):
    return pl.multiple_of(value * step, step)


def kernel(
    tokens,
    in_weight,
    residues,
    decay_rates,
    skip_gain,
    out_weight,
    out,
    tok,
    w_in,
    w_out,
    part,
    relay,
    direct,
    summed,
    y_send,
    y_recv,
    crossed,
    relay_l,
    direct_l,
    summed_l,
    s_scr,
    y_scr,
    q_scr,
    decay_b,
    res_b,
    seg_b,
    scan_b,
    ends,
    state_in,
    state_out,
    gath,
    p_out,
    o_relay,
    o_y_in,
    o_in,
    o_sib,
    o_send,
    o_y,
    local_sem,
    tok_sem,
    far_sem,
    w_sem,
    wo_sem,
    relay_sem,
    direct_sem,
    summed_sem,
    y_sem,
    crossed_sem,
    relay_l_sem,
    direct_l_sem,
    summed_l_sem,
    state_sem,
    gath_sem,
    o_relay_sem,
    o_y_in_sem,
    o_in_sem,
    o_sib_sem,
    o_y_sem,
    send_sem,
):
    seq = lax.axis_index("seq")
    tp = lax.axis_index("tp")
    core = lax.rem(seq, 2)
    z = lax.rem(seq // 2, 4)
    y_hi = seq // 8
    x = tp // 2
    y_lo = lax.rem(tp, 2)

    def at(dx=0, dz=0, flip_hi=False, flip_lo=False, flip_core=False):
        a = 1 - y_hi if flip_hi else y_hi
        b = lax.rem(z + dz, 4)
        c = 1 - core if flip_core else core
        d = lax.rem(x + dx, 4)
        e = 1 - y_lo if flip_lo else y_lo
        return (a * 8 + b * 2 + c, d * 2 + e)

    sibling = at(flip_core=True)
    z_next, z_prev, z_far = at(dz=1), at(dz=3), at(dz=2)
    y_far = at(flip_hi=True)
    x_next, x_prev = at(dx=1), at(dx=3)
    y_near = at(flip_lo=True)
    diagonals = [at(dz=r, flip_hi=True) for r in (2, 1, 3)]
    peers = [sibling, z_next, z_prev, z_far, y_far, x_next, x_prev, y_near, *diagonals]
    peers += [at(dx=1, flip_core=True), at(dx=3, flip_core=True)]
    block = y_hi * 4 + z
    lanes = pl.ds(aligned(block, LANES), LANES)

    barrier = pltpu.get_barrier_semaphore()
    for peer in peers:
        pl.semaphore_signal(barrier, inc=1, device_id=peer, device_id_type=MESH)

    own_rows = pl.ds(aligned(core, ROWS), ROWS)
    other_rows = pl.ds(aligned(1 - core, ROWS), ROWS)
    own_feat = pl.ds(aligned(core, FEATURES), FEATURES)
    other_feat = pl.ds(aligned(1 - core, FEATURES), FEATURES)
    pltpu.make_async_copy(tokens.at[own_rows, :], tok.at[tp, :, own_feat], local_sem.at[0]).start()

    def own_weight(r):
        return w_in.at[lax.rem(z + r, 4), own_feat, :]

    for r in (2, 1, 3, 0):
        zi = lax.rem(z + r, 4)
        for h in range(2):
            there = pl.ds(aligned(h * 4 + zi, LANES), LANES)
            for k in range(3):
                pltpu.make_async_copy(
                    in_weight.at[k, :, there],
                    w_in.at[zi, own_feat, pl.ds((h * 3 + k) * LANES, LANES)],
                    local_sem.at[1 + r],
                ).start()
    pltpu.make_async_copy(out_weight, w_out.at[core], local_sem.at[5]).start()

    pl.semaphore_wait(barrier, len(peers))
    remote(tokens.at[other_rows, :], tok.at[tp, :, own_feat], send_sem.at[0], tok_sem.at[CHUNKS], sibling).start()
    wait_bytes(own_weight(2), local_sem.at[3])
    remote(own_weight(2), own_weight(2), send_sem.at[1], w_sem.at[2], sibling).start()
    wait_bytes(tok.at[0, :, pl.ds(0, FEATURES)], local_sem.at[0])
    wait_bytes(tok.at[0, :, pl.ds(0, FEATURES)], tok_sem.at[CHUNKS])
    for peer in (y_near, x_next, x_prev):
        remote(tok.at[tp], tok.at[tp], send_sem.at[0], tok_sem.at[tp], peer).start()
    for r in (1, 3, 0):
        wait_bytes(own_weight(r), local_sem.at[1 + r])
        remote(own_weight(r), own_weight(r), send_sem.at[1], w_sem.at[r], sibling).start()
    remote(out_weight, w_out.at[core], send_sem.at[1], wo_sem.at[0], sibling).start()

    seg_index = lax.broadcasted_iota(jnp.int32, (SEGS, LANES), 0)
    seg_next = (seg_index + 1).astype(F32) * float(STEPS)
    for m in range(MODES):
        rate = jnp.broadcast_to(decay_rates[pl.ds(m, 1), lanes], (SEGS, LANES))
        decay_b[m] = jnp.exp(-rate)
        res_b[m] = jnp.broadcast_to(residues[pl.ds(m, 1), lanes], (SEGS, LANES))
        seg_b[m] = jnp.exp(-rate * seg_next)
        for k in range(3):
            scan_b[k, m] = jnp.where(seg_index >= (1 << k), jnp.exp(-rate * float(STEPS << k)), 0.0)

    @pl.when(core == 0)
    def _():
        state_in[0] = jnp.zeros((MODES, LANES), F32)

    @pl.when(tp >= SPLIT)
    def _():
        o_y[1] = jnp.zeros((2, 2, QUARTER, FEATURES), BF16)

    upper, lower = pl.ds(0, HALF), pl.ds(HALF, HALF)
    near = x * 2 + 1 - y_lo
    code = jnp.int32(ORDERS[0])
    for t in range(1, 8):
        code = jnp.where(tp == t, jnp.int32(ORDERS[t]), code)

    def order(i):
        return lax.shift_right_logical(code, 3 * i) & 7

    def column_chunk(dx, row):
        return lax.rem(x + dx, 4) * 2 + row

    def relay_tokens(row, far):
        after, before = column_chunk(1, row), column_chunk(3, row)
        for chunk in (after, before):
            wait_bytes(tok.at[chunk], tok_sem.at[chunk])
        remote(
            tok.at[before, upper], tok.at[before, upper], send_sem.at[0], far_sem.at[far, 0], x_next
        ).start()
        remote(tok.at[after, lower], tok.at[after, lower], send_sem.at[0], far_sem.at[far, 1], x_prev).start()

    def multiply(jc, r):
        zi = lax.rem(z + r, 4)

        part[jc, r] = jnp.dot(tok[jc], w_in[zi], preferred_element_type=F32).astype(BF16)

    first, second = pl.ds(0, QKV), pl.ds(QKV, QKV)

    def await_tokens(jc):
        for far, row in ((0, y_lo), (1, 1 - y_lo)):

            @pl.when(jc == column_chunk(2, row))
            def _():
                wait_bytes(tok.at[jc, upper], far_sem.at[far, 0])
                wait_bytes(tok.at[jc, lower], far_sem.at[far, 1])

    def project(i):
        jc = order(i)
        await_tokens(jc)

        for r in (2, 1, 3, 0):

            @pl.when(i == 0)
            def _():
                wait_bytes(w_in.at[0, other_feat, :], w_sem.at[r])

            multiply(jc, r)
            if r == 2:
                remote(part.at[jc, 2, :, first], relay.at[0, jc], send_sem.at[2], relay_sem.at[0, jc], z_next).start()
                remote(part.at[jc, 2, :, second], relay.at[1, jc], send_sem.at[2], relay_sem.at[1, jc], z_prev).start()
            elif r == 1:
                remote(part.at[jc, 1, :, second], direct.at[1, jc], send_sem.at[3], direct_sem.at[1, jc], z_next).start()
            elif r == 3:
                remote(part.at[jc, 3, :, first], direct.at[0, jc], send_sem.at[3], direct_sem.at[0, jc], z_prev).start()

    def project_late(u):
        jc = order(EARLY + u)
        await_tokens(jc)
        theirs = pl.ds(aligned(1 - y_hi, QKV), QKV)
        for r in (2, 1, 3, 0):
            multiply(jc, r)
            remote(part.at[jc, r, :, theirs], crossed.at[u, r], send_sem.at[9], crossed_sem.at[u], y_far).start()

    def start_late(u):
        jc = order(EARLY + u)
        mine = pl.ds(aligned(y_hi, QKV), QKV)
        wait_bytes(crossed.at[u], crossed_sem.at[u])
        for r in (2, 1, 3, 0):
            crossed[u, r] = (crossed[u, r].astype(F32) + part[jc, r, :, mine].astype(F32)).astype(BF16)
            if r == 2:
                for k, rows, peer in ((0, upper, z_next), (1, lower, z_prev)):
                    remote(
                        crossed.at[u, 2, rows], relay_l.at[u, k], send_sem.at[10], relay_l_sem.at[u, k], peer
                    ).start()
            elif r == 1:
                remote(
                    crossed.at[u, 1, lower], direct_l.at[u, 1], send_sem.at[10], direct_l_sem.at[u, 1], z_next
                ).start()
            elif r == 3:
                remote(
                    crossed.at[u, 3, upper], direct_l.at[u, 0], send_sem.at[10], direct_l_sem.at[u, 0], z_prev
                ).start()

    def pass_late(u):
        for k, r, rows, peer in ((0, 1, upper, z_next), (1, 3, lower, z_prev)):
            wait_bytes(relay_l.at[u, k], relay_l_sem.at[u, k])
            relay_l[u, k] = (relay_l[u, k].astype(F32) + crossed[u, r, rows].astype(F32)).astype(BF16)
            remote(relay_l.at[u, k], summed_l.at[u, k], send_sem.at[10], summed_l_sem.at[u, k], peer).start()

    def pass_on(jc):
        for k, r, cols, peer in ((0, 1, first, z_next), (1, 3, second, z_prev)):
            wait_bytes(relay.at[k, jc], relay_sem.at[k, jc])
            relay[k, jc] = (relay[k, jc].astype(F32) + part[jc, r, :, cols].astype(F32)).astype(BF16)
            remote(relay.at[k, jc], summed.at[k, jc], send_sem.at[4], summed_sem.at[k, jc], peer).start()

    def gather_half(jc, k):
        cols = pl.ds(aligned(k, QKV), QKV)
        return part[jc, 0, :, cols].astype(F32) + direct[k, jc].astype(F32) + summed[k, jc].astype(F32)

    def cross(jc):
        for k in range(2):
            wait_bytes(direct.at[k, jc], direct_sem.at[k, jc])
            wait_bytes(summed.at[k, jc], summed_sem.at[k, jc])
        y_send[jc] = gather_half(jc, 1 - y_hi).astype(BF16)
        remote(y_send.at[jc], y_recv.at[jc], send_sem.at[5], y_sem.at[jc], y_far).start()

    def convolve(j):
        def keep(rows, total):
            q_scr[rows, :] = total[:, :LANES]
            s_scr[rows, :] = total[:, LANES : 2 * LANES] * total[:, 2 * LANES :]

        late = jnp.int32(-1)
        for u in range(LATE):
            late = jnp.where(order(EARLY + u) == j, u, late)

        @pl.when(late < 0)
        def _():
            wait_bytes(y_recv.at[j], y_sem.at[j])
            keep(pl.ds(0, ROWS), gather_half(j, y_hi) + y_recv[j].astype(F32))

        @pl.when(late >= 0)
        def _():
            for k, rows in ((0, upper), (1, lower)):
                wait_bytes(direct_l.at[late, k], direct_l_sem.at[late, k])
                wait_bytes(summed_l.at[late, k], summed_l_sem.at[late, k])
                keep(
                    rows,
                    crossed[late, 0, rows].astype(F32)
                    + direct_l[late, k].astype(F32)
                    + summed_l[late, k].astype(F32),
                )

        decay = [decay_b[m] for m in range(MODES)]
        held = [jnp.zeros((SEGS, LANES), F32)] * MODES
        for i in range(STEPS):
            now = s_scr[pl.ds(i, SEGS, stride=STEPS), :]
            held = [decay[m] * held[m] + now for m in range(MODES)]
        for m in range(MODES):
            total = held[m]
            for k in range(3):
                total = total + scan_b[k, m] * pltpu.roll(total, 1 << k, 0)
            ends[m] = total

        @pl.when(jnp.logical_or(core == 1, j > 0))
        def _():
            wait_bytes(state_in.at[j], state_sem.at[j])

        for m in range(MODES):
            before = jnp.broadcast_to(state_in[j, pl.ds(m, 1), :], (SEGS, LANES))
            full = ends[m] + seg_b[m] * before
            state_out[j, pl.ds(m, 1), :] = full[SEGS - 1 :, :]
            ends[m] = jnp.where(seg_index == 0, before, pltpu.roll(full, 1, 0))

        @pl.when(jnp.logical_or(core == 0, j < CHUNKS - 1))
        def _():
            remote(state_out.at[j], state_in.at[j + core], send_sem.at[6], state_sem.at[j + core], sibling).start()

        held = [ends[m] for m in range(MODES)]
        for i in range(STEPS):
            now = s_scr[pl.ds(i, SEGS, stride=STEPS), :]
            held = [decay_b[m] * held[m] + now for m in range(MODES)]
            terms = [res_b[m] * held[m] for m in range(MODES)]
            while len(terms) > 1:
                terms = [terms[k] + terms[k + 1] for k in range(0, len(terms), 2)]
            y_scr[pl.ds(i, SEGS, stride=STEPS), :] = terms[0]
        gain = skip_gain[:, lanes]
        gath[j, :, lanes] = (q_scr[...] * (y_scr[...] + gain * s_scr[...])).astype(BF16)
        own = gath.at[j, :, lanes]
        for peer in (z_far, z_next, z_prev, y_far):
            remote(own, own, send_sem.at[7], gath_sem.at[block, j], peer).start()

        @pl.when(j >= DIRECT)
        def _():
            for peer in diagonals:
                remote(own, own, send_sem.at[7], gath_sem.at[block, j], peer).start()

    def forward(j):
        for r in (1, 3, 2):
            b = y_hi * 4 + lax.rem(z + r, 4)
            there = gath.at[j, :, pl.ds(aligned(b, LANES), LANES)]
            wait_bytes(there, gath_sem.at[b, j])
            remote(there, there, send_sem.at[7], gath_sem.at[b, j], y_far).start()

    def distance(j):
        return lax.rem(j // 2 - x + 4, 4)

    def finish(j):
        for r in range(4):
            b = (1 - y_hi) * 4 + r
            wait_bytes(gath.at[j, :, pl.ds(aligned(b, LANES), LANES)], gath_sem.at[b, j])

        @pl.when(j >= DIRECT)
        def _():
            for r in (1, 3, 2):
                b = y_hi * 4 + lax.rem(z + r, 4)
                wait_bytes(gath.at[j, :, pl.ds(aligned(b, LANES), LANES)], gath_sem.at[b, j])

        @pl.when(j == 0)
        def _():
            pltpu.make_async_copy(out_weight, w_out.at[core], local_sem.at[5]).wait()
            wait_bytes(w_out.at[1 - core], wo_sem.at[0])

        for h in range(2):
            cols = pl.ds(h * FEATURES, FEATURES)
            p_out[j, :, cols] = jnp.dot(gath[j], w_out[h], preferred_element_type=F32).astype(BF16)
        o_begin(j, 0)

        @pl.when(j < SPLIT)
        def _():
            o_begin(j, 1)

        @pl.when(jnp.logical_and(j >= SPLIT, row_of(j) != y_lo))
        def _():
            remote(p_out.at[j, lower], o_y_in.at[j], send_sem.at[8], o_y_in_sem.at[j], y_near).start()

    def row_of(j):
        return lax.rem(j, 2)

    def quarter(part_index, k):
        return pl.ds(part_index * HALF + k * QUARTER, QUARTER)

    def own_columns(flip):
        return pl.ds(aligned(1 - core if flip else core, FEATURES), FEATURES)

    def to_column(src, j, s, kind, k, dx):
        for flip in (False, True):
            remote(
                src.at[:, own_columns(flip)],
                o_in.at[row_of(j), s, kind, k, core],
                send_sem.at[8],
                o_in_sem.at[row_of(j), s],
                at(dx=dx, flip_core=flip),
            ).start()

    def o_begin(j, s):
        dx = distance(j)

        @pl.when(dx == 2)
        def _():
            for k, peer in ((0, x_next), (1, x_prev)):
                remote(
                    p_out.at[j, quarter(s, k)], o_relay.at[s, j], send_sem.at[8], o_relay_sem.at[s, j], peer
                ).start()

        @pl.when(dx == 1)
        def _():
            to_column(p_out.at[j, quarter(s, 1)], j, s, 0, 1, 1)

        @pl.when(dx == 3)
        def _():
            to_column(p_out.at[j, quarter(s, 0)], j, s, 0, 0, 3)

        @pl.when(dx == 0)
        def _():
            rows = pl.ds(s * HALF, HALF)
            remote(
                p_out.at[j, rows, own_columns(True)],
                o_sib.at[row_of(j), s],
                send_sem.at[8],
                o_sib_sem.at[row_of(j), s],
                sibling,
            ).start()

    def o_pass(j, s):
        dx = distance(j)
        for want, k in ((1, 0), (3, 1)):

            @pl.when(dx == want)
            def _():
                wait_bytes(o_relay.at[s, j], o_relay_sem.at[s, j])
                o_relay[s, j] = (o_relay[s, j].astype(F32) + p_out[j, quarter(s, k), :].astype(F32)).astype(BF16)
                to_column(o_relay.at[s, j], j, s, 1, k, want)

    def o_total(j, s, k, mine):
        side = row_of(j)
        source = core if mine else 1 - core
        if mine:
            base = p_out[j, quarter(s, k), own_columns(False)]
        else:
            base = o_sib[side, s, pl.ds(k * QUARTER, QUARTER), :]
        return (
            base.astype(F32) + o_in[side, s, 0, k, source].astype(F32) + o_in[side, s, 1, k, source].astype(F32)
        )

    def o_arrived(j, s):
        wait_bytes(o_in.at[row_of(j), s], o_in_sem.at[row_of(j), s])
        wait_bytes(o_sib.at[row_of(j), s], o_sib_sem.at[row_of(j), s])

    def o_second(j):
        @pl.when(jnp.logical_and(j >= SPLIT, row_of(j) == y_lo))
        def _():
            wait_bytes(o_y_in.at[j], o_y_in_sem.at[j])
            p_out[j, lower, :] = (p_out[j, lower, :].astype(F32) + o_y_in[j].astype(F32)).astype(BF16)
            o_begin(j, 1)

        o_pass(j, 0)

        @pl.when(j < SPLIT)
        def _():
            o_pass(j, 1)

    def o_over(j, s):
        o_arrived(j, s)
        for k in range(2):
            for mine in (True, False):
                o_send[s, core if mine else 1 - core, k] = o_total(j, s, k, mine).astype(BF16)
        remote(o_send.at[s], o_y.at[s], send_sem.at[8], o_y_sem.at[s], y_near).start()

    def o_third(j):
        @pl.when(jnp.logical_and(j >= SPLIT, row_of(j) == y_lo))
        def _():
            o_pass(j, 1)

        @pl.when(jnp.logical_and(distance(j) == 0, row_of(j) != y_lo))
        def _():
            o_over(j, 0)

            @pl.when(j < SPLIT)
            def _():
                o_over(j, 1)

    def o_last(j):
        @pl.when(j == tp)
        def _():
            for s in (1, 0):
                o_arrived(j, s)
                if s == 0:
                    wait_bytes(o_y.at[0], o_y_sem.at[0])
                else:

                    @pl.when(j < SPLIT)
                    def _():
                        wait_bytes(o_y.at[1], o_y_sem.at[1])

                for k in range(2):
                    for mine in (True, False):
                        source = core if mine else 1 - core
                        total = o_total(j, s, k, mine) + o_y[s, source, k].astype(F32)
                        start = source * ROWS + s * HALF + k * QUARTER
                        out[pl.ds(pl.multiple_of(start, QUARTER), QUARTER), :] = total.astype(BF16)

    def step(n, carry):
        def stage(times, body):
            first_chunk, end_chunk = jnp.int32(0), jnp.int32(0)
            for time in times:
                first_chunk = first_chunk + jnp.where(n > time, 1, 0)
                end_chunk = end_chunk + jnp.where(n >= time, 1, 0)

            def call(j, unused):
                body(j)
                return unused

            lax.fori_loop(first_chunk, end_chunk, call, 0)

        @pl.when(n == 2)
        def _():
            wait_bytes(tok.at[near], tok_sem.at[near])
            relay_tokens(y_lo, 0)
            for peer in (x_next, x_prev):
                remote(tok.at[near], tok.at[near], send_sem.at[0], tok_sem.at[near], peer).start()

        @pl.when(n == 6)
        def _():
            relay_tokens(1 - y_lo, 1)

        stage(range(0, 2 * EARLY, 2), project)
        stage(START_LATE_AT, start_late)
        stage(range(1, 2 * EARLY, 2), lambda k: pass_on(order(k)))
        stage([t + 1 for t in START_LATE_AT], pass_late)
        stage(range(3, 2 * EARLY + 2, 2), lambda k: cross(order(k)))
        stage(PROJECT_LATE_AT, project_late)
        stage(CONVOLVE_AT, convolve)
        stage([t + 1 for t in CONVOLVE_AT[:DIRECT]], forward)
        stage(FINISH_AT, finish)
        stage([t + 1 for t in FINISH_AT], o_second)
        stage([t + 2 for t in FINISH_AT], o_third)
        stage([t + 3 for t in FINISH_AT], o_last)
        return carry

    lax.fori_loop(0, FINISH_AT[-1] + 4, step, 0)

    wait_bytes(tok.at[pl.ds(0, 7)], send_sem.at[0])
    wait_bytes(tok.at[0, :, pl.ds(0, FEATURES)], send_sem.at[0])
    wait_bytes(w_in.at[:, own_feat, :], send_sem.at[1])
    wait_bytes(out_weight, send_sem.at[1])
    early = pl.ds(0, EARLY)
    wait_bytes(relay.at[:, early], send_sem.at[2])
    wait_bytes(direct.at[:, early], send_sem.at[3])
    wait_bytes(summed.at[:, early], send_sem.at[4])
    wait_bytes(y_recv.at[early], send_sem.at[5])
    wait_bytes(crossed, send_sem.at[9])
    for arrived in (relay_l, direct_l, summed_l):
        wait_bytes(arrived, send_sem.at[10])
    wait_bytes(state_out.at[pl.ds(0, CHUNKS - 1)], send_sem.at[6])

    @pl.when(core == 0)
    def _():
        wait_bytes(state_out.at[0], send_sem.at[6])

    wait_bytes(gath.at[pl.ds(0, 7)], send_sem.at[7])
    wait_bytes(p_out.at[pl.ds(0, 7)], send_sem.at[8])
    wait_bytes(p_out.at[0, pl.ds(0, 3 * QUARTER)], send_sem.at[8])

    @pl.when(tp < SPLIT)
    def _():
        wait_bytes(p_out.at[0, pl.ds(0, QUARTER)], send_sem.at[8])


def local(tokens, in_weight, residues, decay_rates, skip_gain, out_weight):
    channels = in_weight.shape[2]
    vmem = pl.BlockSpec(memory_space=pltpu.VMEM)
    anywhere = pl.BlockSpec(memory_space=pl.ANY)
    dma = pltpu.SemaphoreType.DMA
    scratch = [
        pltpu.VMEM((CHUNKS, ROWS, WIDE), BF16),
        pltpu.VMEM((4, WIDE, 2 * QKV), BF16),
        pltpu.VMEM((2, WIDE, FEATURES), BF16),
        pltpu.VMEM((CHUNKS, 4, ROWS, 2 * QKV), BF16),
        pltpu.VMEM((2, CHUNKS, ROWS, QKV), BF16),
        pltpu.VMEM((2, CHUNKS, ROWS, QKV), BF16),
        pltpu.VMEM((2, CHUNKS, ROWS, QKV), BF16),
        pltpu.VMEM((CHUNKS, ROWS, QKV), BF16),
        pltpu.VMEM((CHUNKS, ROWS, QKV), BF16),
        pltpu.VMEM((LATE, 4, ROWS, QKV), BF16),
        pltpu.VMEM((LATE, 2, HALF, QKV), BF16),
        pltpu.VMEM((LATE, 2, HALF, QKV), BF16),
        pltpu.VMEM((LATE, 2, HALF, QKV), BF16),
        pltpu.VMEM((ROWS, LANES), F32),
        pltpu.VMEM((ROWS, LANES), F32),
        pltpu.VMEM((ROWS, LANES), F32),
        pltpu.VMEM((MODES, SEGS, LANES), F32),
        pltpu.VMEM((MODES, SEGS, LANES), F32),
        pltpu.VMEM((MODES, SEGS, LANES), F32),
        pltpu.VMEM((3, MODES, SEGS, LANES), F32),
        pltpu.VMEM((MODES, SEGS, LANES), F32),
        pltpu.VMEM((CHUNKS + 1, MODES, LANES), F32),
        pltpu.VMEM((CHUNKS, MODES, LANES), F32),
        pltpu.VMEM((CHUNKS, ROWS, WIDE), BF16),
        pltpu.VMEM((CHUNKS, ROWS, WIDE), BF16),
        pltpu.VMEM((2, CHUNKS, QUARTER, WIDE), BF16),
        pltpu.VMEM((CHUNKS, HALF, WIDE), BF16),
        pltpu.VMEM((2, 2, 2, 2, 2, QUARTER, FEATURES), BF16),
        pltpu.VMEM((2, 2, HALF, FEATURES), BF16),
        pltpu.VMEM((2, 2, 2, QUARTER, FEATURES), BF16),
        pltpu.VMEM((2, 2, 2, QUARTER, FEATURES), BF16),
        dma((6,)),
        dma((CHUNKS + 1,)),
        dma((2, 2)),
        dma((4,)),
        dma((1,)),
        dma((2, CHUNKS)),
        dma((2, CHUNKS)),
        dma((2, CHUNKS)),
        dma((CHUNKS,)),
        dma((LATE,)),
        dma((LATE, 2)),
        dma((LATE, 2)),
        dma((LATE, 2)),
        dma((CHUNKS + 1,)),
        dma((8, CHUNKS)),
        dma((2, CHUNKS)),
        dma((CHUNKS,)),
        dma((2, 2)),
        dma((2, 2)),
        dma((2,)),
        dma((11,)),
    ]
    return pl.pallas_call(
        kernel,
        out_shape=jax.ShapeDtypeStruct(tokens.shape, BF16),
        in_specs=[anywhere, anywhere, vmem, vmem, vmem, anywhere],
        out_specs=vmem,
        scratch_shapes=scratch,
        compiler_params=pltpu.CompilerParams(
            collective_id=0, has_side_effects=True, vmem_limit_bytes=56 * 2**20
        ),
        name="hyena_block",
    )(tokens, in_weight.transpose(1, 0, 2), residues, decay_rates, skip_gain.reshape(1, channels), out_weight)


def solution(mesh):
    in_specs = (
        P("tp", "seq"),
        P("seq", None, "tp"),
        P(None, "tp"),
        P(None, "tp"),
        P("tp"),
        P("tp", "seq"),
    )
    return jax.shard_map(local, mesh=mesh, in_specs=in_specs, out_specs=P("tp", "seq"), check_vma=False)
```

```python
import functools

import jax
import jax.numpy as jnp
from jax import lax
from jax.experimental import pallas as pl
from jax.experimental.pallas import tpu as pltpu
from jax.sharding import PartitionSpec as P

MESH = pl.DeviceIdType.MESH
F32 = jnp.float32
BF16 = jnp.bfloat16
CHUNKS = 8
ROWS = 128
HALF = 64
QUARTER = 32
LANES = 128
MODES = 16
SEGS = 8
STEPS = 16
QKV = 3 * LANES
FEATURES = 512
WIDE = 1024
DIRECT = 5
SPLIT = 6
EARLY = 7
LATE = CHUNKS - EARLY
PROJECT_LATE_AT = (9,)
START_LATE_AT = (13,)
CONVOLVE_AT = (12, 12, 13, 14, 14, 16, 16, 16)
FINISH_AT = (15, 15, 15, 16, 16, 17, 17, 17)
CHUNK_ORDERS = (
    (0, 1, 2, 3, 4, 5, 6, 7),
    (1, 0, 3, 2, 4, 5, 6, 7),
    (2, 3, 0, 1, 4, 5, 6, 7),
    (3, 2, 1, 0, 4, 5, 6, 7),
    (4, 5, 0, 2, 1, 3, 6, 7),
    (5, 4, 1, 2, 0, 3, 6, 7),
    (6, 0, 2, 1, 3, 4, 5, 7),
    (7, 1, 3, 0, 2, 4, 5, 6),
)
ORDERS = tuple(sum(chunk << (3 * k) for k, chunk in enumerate(row)) for row in CHUNK_ORDERS)


def remote(src, dst, send_sem, recv_sem, device):
    return pltpu.make_async_remote_copy(
        src_ref=src,
        dst_ref=dst,
        send_sem=send_sem,
        recv_sem=recv_sem,
        device_id=device,
        device_id_type=MESH,
    )


def wait_bytes(ref, sem):
    pltpu.make_async_copy(ref, ref, sem).wait()


def aligned(value, step):
    return pl.multiple_of(value * step, step)


def kernel(
    tokens,
    in_weight,
    residues_in,
    decay_rates_in,
    skip_gain_in,
    out_weight,
    out,
    residues,
    decay_rates,
    skip_gain,
    tok,
    w_in,
    w_out,
    part,
    relay,
    direct,
    summed,
    y_send,
    y_recv,
    crossed,
    relay_l,
    direct_l,
    summed_l,
    s_scr,
    y_scr,
    q_scr,
    decay_b,
    res_b,
    seg_b,
    scan_b,
    ends,
    state_in,
    state_out,
    gath,
    p_out,
    o_relay,
    o_y_in,
    o_in,
    o_sib,
    o_send,
    o_y,
    local_sem,
    tok_sem,
    far_sem,
    w_sem,
    wo_sem,
    relay_sem,
    direct_sem,
    summed_sem,
    y_sem,
    crossed_sem,
    relay_l_sem,
    direct_l_sem,
    summed_l_sem,
    state_sem,
    gath_sem,
    o_relay_sem,
    o_y_in_sem,
    o_in_sem,
    o_sib_sem,
    o_y_sem,
    send_sem,
):
    seq = lax.axis_index("seq")
    tp = lax.axis_index("tp")
    core = lax.rem(seq, 2)
    z = lax.rem(seq // 2, 4)
    y_hi = seq // 8
    x = tp // 2
    y_lo = lax.rem(tp, 2)

    def at(dx=0, dz=0, flip_hi=False, flip_lo=False, flip_core=False):
        a = 1 - y_hi if flip_hi else y_hi
        b = lax.rem(z + dz, 4)
        c = 1 - core if flip_core else core
        d = lax.rem(x + dx, 4)
        e = 1 - y_lo if flip_lo else y_lo
        return (a * 8 + b * 2 + c, d * 2 + e)

    sibling = at(flip_core=True)
    z_next, z_prev, z_far = at(dz=1), at(dz=3), at(dz=2)
    y_far = at(flip_hi=True)
    x_next, x_prev = at(dx=1), at(dx=3)
    y_near = at(flip_lo=True)
    diagonals = [at(dz=r, flip_hi=True) for r in (2, 1, 3)]
    peers = [sibling, z_next, z_prev, z_far, y_far, x_next, x_prev, y_near, *diagonals]
    peers += [at(dx=1, flip_core=True), at(dx=3, flip_core=True)]
    block = y_hi * 4 + z
    lanes = pl.ds(aligned(block, LANES), LANES)

    barrier = pltpu.get_barrier_semaphore()
    for peer in peers:
        pl.semaphore_signal(barrier, inc=1, device_id=peer, device_id_type=MESH)

    own_rows = pl.ds(aligned(core, ROWS), ROWS)
    other_rows = pl.ds(aligned(1 - core, ROWS), ROWS)
    own_feat = pl.ds(aligned(core, FEATURES), FEATURES)
    other_feat = pl.ds(aligned(1 - core, FEATURES), FEATURES)
    pltpu.make_async_copy(tokens.at[own_rows, :], tok.at[tp, :, own_feat], local_sem.at[0]).start()

    def own_weight(r):
        return w_in.at[lax.rem(z + r, 4), own_feat, :]

    for r in (2, 1, 3, 0):
        zi = lax.rem(z + r, 4)
        for h in range(2):
            there = pl.ds(aligned(h * 4 + zi, LANES), LANES)
            for k in range(3):
                pltpu.make_async_copy(
                    in_weight.at[k, :, there],
                    w_in.at[zi, own_feat, pl.ds((h * 3 + k) * LANES, LANES)],
                    local_sem.at[1 + r],
                ).start()
    pltpu.make_async_copy(out_weight, w_out.at[core], local_sem.at[5]).start()
    small = [
        pltpu.make_async_copy(whole.at[:, lanes], piece, local_sem.at[6 + k])
        for k, (whole, piece) in enumerate(
            ((residues_in, residues), (decay_rates_in, decay_rates), (skip_gain_in, skip_gain))
        )
    ]
    for copy in small:
        copy.start()

    pl.semaphore_wait(barrier, len(peers))
    remote(tokens.at[other_rows, :], tok.at[tp, :, own_feat], send_sem.at[0], tok_sem.at[CHUNKS], sibling).start()
    wait_bytes(own_weight(2), local_sem.at[3])
    remote(own_weight(2), own_weight(2), send_sem.at[1], w_sem.at[2], sibling).start()
    wait_bytes(tok.at[0, :, pl.ds(0, FEATURES)], local_sem.at[0])
    wait_bytes(tok.at[0, :, pl.ds(0, FEATURES)], tok_sem.at[CHUNKS])
    for peer in (y_near, x_next, x_prev):
        remote(tok.at[tp], tok.at[tp], send_sem.at[0], tok_sem.at[tp], peer).start()
    for r in (1, 3, 0):
        wait_bytes(own_weight(r), local_sem.at[1 + r])
        remote(own_weight(r), own_weight(r), send_sem.at[1], w_sem.at[r], sibling).start()
    remote(out_weight, w_out.at[core], send_sem.at[1], wo_sem.at[0], sibling).start()

    for copy in small:
        copy.wait()
    seg_index = lax.broadcasted_iota(jnp.int32, (SEGS, LANES), 0)
    seg_next = (seg_index + 1).astype(F32) * float(STEPS)
    for m in range(MODES):
        rate = jnp.broadcast_to(decay_rates[pl.ds(m, 1), :], (SEGS, LANES))
        decay_b[m] = jnp.exp(-rate)
        res_b[m] = jnp.broadcast_to(residues[pl.ds(m, 1), :], (SEGS, LANES))
        seg_b[m] = jnp.exp(-rate * seg_next)
        for k in range(3):
            scan_b[k, m] = jnp.where(seg_index >= (1 << k), jnp.exp(-rate * float(STEPS << k)), 0.0)

    @pl.when(core == 0)
    def _():
        state_in[0] = jnp.zeros((MODES, LANES), F32)

    @pl.when(tp >= SPLIT)
    def _():
        o_y[1] = jnp.zeros((2, 2, QUARTER, FEATURES), BF16)

    upper, lower = pl.ds(0, HALF), pl.ds(HALF, HALF)
    near = x * 2 + 1 - y_lo
    code = jnp.int32(ORDERS[0])
    for t in range(1, 8):
        code = jnp.where(tp == t, jnp.int32(ORDERS[t]), code)

    def order(i):
        return lax.shift_right_logical(code, 3 * i) & 7

    def column_chunk(dx, row):
        return lax.rem(x + dx, 4) * 2 + row

    def relay_tokens(row, far):
        after, before = column_chunk(1, row), column_chunk(3, row)
        for chunk in (after, before):
            wait_bytes(tok.at[chunk], tok_sem.at[chunk])
        remote(
            tok.at[before, upper], tok.at[before, upper], send_sem.at[0], far_sem.at[far, 0], x_next
        ).start()
        remote(tok.at[after, lower], tok.at[after, lower], send_sem.at[0], far_sem.at[far, 1], x_prev).start()

    def multiply(jc, r):
        zi = lax.rem(z + r, 4)

        part[jc, r] = jnp.dot(tok[jc], w_in[zi], preferred_element_type=F32).astype(BF16)

    first, second = pl.ds(0, QKV), pl.ds(QKV, QKV)

    def await_tokens(jc):
        for far, row in ((0, y_lo), (1, 1 - y_lo)):

            @pl.when(jc == column_chunk(2, row))
            def _():
                wait_bytes(tok.at[jc, upper], far_sem.at[far, 0])
                wait_bytes(tok.at[jc, lower], far_sem.at[far, 1])

    def project(i):
        jc = order(i)
        await_tokens(jc)

        for r in (2, 1, 3, 0):

            @pl.when(i == 0)
            def _():
                wait_bytes(w_in.at[0, other_feat, :], w_sem.at[r])

            multiply(jc, r)
            if r == 2:
                remote(part.at[jc, 2, :, first], relay.at[0, jc], send_sem.at[2], relay_sem.at[0, jc], z_next).start()
                remote(part.at[jc, 2, :, second], relay.at[1, jc], send_sem.at[2], relay_sem.at[1, jc], z_prev).start()
            elif r == 1:
                remote(part.at[jc, 1, :, second], direct.at[1, jc], send_sem.at[3], direct_sem.at[1, jc], z_next).start()
            elif r == 3:
                remote(part.at[jc, 3, :, first], direct.at[0, jc], send_sem.at[3], direct_sem.at[0, jc], z_prev).start()

    def project_late(u):
        jc = order(EARLY + u)
        await_tokens(jc)
        theirs = pl.ds(aligned(1 - y_hi, QKV), QKV)
        for r in (2, 1, 3, 0):
            multiply(jc, r)
            remote(part.at[jc, r, :, theirs], crossed.at[u, r], send_sem.at[9], crossed_sem.at[u], y_far).start()

    def start_late(u):
        jc = order(EARLY + u)
        mine = pl.ds(aligned(y_hi, QKV), QKV)
        wait_bytes(crossed.at[u], crossed_sem.at[u])
        for r in (2, 1, 3, 0):
            crossed[u, r] = (crossed[u, r].astype(F32) + part[jc, r, :, mine].astype(F32)).astype(BF16)
            if r == 2:
                for k, rows, peer in ((0, upper, z_next), (1, lower, z_prev)):
                    remote(
                        crossed.at[u, 2, rows], relay_l.at[u, k], send_sem.at[10], relay_l_sem.at[u, k], peer
                    ).start()
            elif r == 1:
                remote(
                    crossed.at[u, 1, lower], direct_l.at[u, 1], send_sem.at[10], direct_l_sem.at[u, 1], z_next
                ).start()
            elif r == 3:
                remote(
                    crossed.at[u, 3, upper], direct_l.at[u, 0], send_sem.at[10], direct_l_sem.at[u, 0], z_prev
                ).start()

    def pass_late(u):
        for k, r, rows, peer in ((0, 1, upper, z_next), (1, 3, lower, z_prev)):
            wait_bytes(relay_l.at[u, k], relay_l_sem.at[u, k])
            relay_l[u, k] = (relay_l[u, k].astype(F32) + crossed[u, r, rows].astype(F32)).astype(BF16)
            remote(relay_l.at[u, k], summed_l.at[u, k], send_sem.at[10], summed_l_sem.at[u, k], peer).start()

    def pass_on(jc):
        for k, r, cols, peer in ((0, 1, first, z_next), (1, 3, second, z_prev)):
            wait_bytes(relay.at[k, jc], relay_sem.at[k, jc])
            relay[k, jc] = (relay[k, jc].astype(F32) + part[jc, r, :, cols].astype(F32)).astype(BF16)
            remote(relay.at[k, jc], summed.at[k, jc], send_sem.at[4], summed_sem.at[k, jc], peer).start()

    def gather_half(jc, k):
        cols = pl.ds(aligned(k, QKV), QKV)
        return part[jc, 0, :, cols].astype(F32) + direct[k, jc].astype(F32) + summed[k, jc].astype(F32)

    def cross(jc):
        for k in range(2):
            wait_bytes(direct.at[k, jc], direct_sem.at[k, jc])
            wait_bytes(summed.at[k, jc], summed_sem.at[k, jc])
        y_send[jc] = gather_half(jc, 1 - y_hi).astype(BF16)
        remote(y_send.at[jc], y_recv.at[jc], send_sem.at[5], y_sem.at[jc], y_far).start()

    def convolve(j):
        def keep(rows, total):
            q_scr[rows, :] = total[:, :LANES]
            s_scr[rows, :] = total[:, LANES : 2 * LANES] * total[:, 2 * LANES :]

        late = jnp.int32(-1)
        for u in range(LATE):
            late = jnp.where(order(EARLY + u) == j, u, late)

        @pl.when(late < 0)
        def _():
            wait_bytes(y_recv.at[j], y_sem.at[j])
            keep(pl.ds(0, ROWS), gather_half(j, y_hi) + y_recv[j].astype(F32))

        @pl.when(late >= 0)
        def _():
            for k, rows in ((0, upper), (1, lower)):
                wait_bytes(direct_l.at[late, k], direct_l_sem.at[late, k])
                wait_bytes(summed_l.at[late, k], summed_l_sem.at[late, k])
                keep(
                    rows,
                    crossed[late, 0, rows].astype(F32)
                    + direct_l[late, k].astype(F32)
                    + summed_l[late, k].astype(F32),
                )

        decay = [decay_b[m] for m in range(MODES)]
        held = [jnp.zeros((SEGS, LANES), F32)] * MODES
        for i in range(STEPS):
            now = s_scr[pl.ds(i, SEGS, stride=STEPS), :]
            held = [decay[m] * held[m] + now for m in range(MODES)]
        for m in range(MODES):
            total = held[m]
            for k in range(3):
                total = total + scan_b[k, m] * pltpu.roll(total, 1 << k, 0)
            ends[m] = total

        @pl.when(jnp.logical_or(core == 1, j > 0))
        def _():
            wait_bytes(state_in.at[j], state_sem.at[j])

        for m in range(MODES):
            before = jnp.broadcast_to(state_in[j, pl.ds(m, 1), :], (SEGS, LANES))
            full = ends[m] + seg_b[m] * before
            state_out[j, pl.ds(m, 1), :] = full[SEGS - 1 :, :]
            ends[m] = jnp.where(seg_index == 0, before, pltpu.roll(full, 1, 0))

        @pl.when(jnp.logical_or(core == 0, j < CHUNKS - 1))
        def _():
            remote(state_out.at[j], state_in.at[j + core], send_sem.at[6], state_sem.at[j + core], sibling).start()

        held = [ends[m] for m in range(MODES)]
        for i in range(STEPS):
            now = s_scr[pl.ds(i, SEGS, stride=STEPS), :]
            held = [decay_b[m] * held[m] + now for m in range(MODES)]
            terms = [res_b[m] * held[m] for m in range(MODES)]
            while len(terms) > 1:
                terms = [terms[k] + terms[k + 1] for k in range(0, len(terms), 2)]
            y_scr[pl.ds(i, SEGS, stride=STEPS), :] = terms[0]
        gain = skip_gain[...]
        gath[j, :, lanes] = (q_scr[...] * (y_scr[...] + gain * s_scr[...])).astype(BF16)
        own = gath.at[j, :, lanes]
        for peer in (z_far, z_next, z_prev, y_far):
            remote(own, own, send_sem.at[7], gath_sem.at[block, j], peer).start()

        @pl.when(j >= DIRECT)
        def _():
            for peer in diagonals:
                remote(own, own, send_sem.at[7], gath_sem.at[block, j], peer).start()

    def forward(j):
        for r in (1, 3, 2):
            b = y_hi * 4 + lax.rem(z + r, 4)
            there = gath.at[j, :, pl.ds(aligned(b, LANES), LANES)]
            wait_bytes(there, gath_sem.at[b, j])
            remote(there, there, send_sem.at[7], gath_sem.at[b, j], y_far).start()

    def distance(j):
        return lax.rem(j // 2 - x + 4, 4)

    def finish(j):
        for r in range(4):
            b = (1 - y_hi) * 4 + r
            wait_bytes(gath.at[j, :, pl.ds(aligned(b, LANES), LANES)], gath_sem.at[b, j])

        @pl.when(j >= DIRECT)
        def _():
            for r in (1, 3, 2):
                b = y_hi * 4 + lax.rem(z + r, 4)
                wait_bytes(gath.at[j, :, pl.ds(aligned(b, LANES), LANES)], gath_sem.at[b, j])

        @pl.when(j == 0)
        def _():
            pltpu.make_async_copy(out_weight, w_out.at[core], local_sem.at[5]).wait()
            wait_bytes(w_out.at[1 - core], wo_sem.at[0])

        for h in range(2):
            cols = pl.ds(h * FEATURES, FEATURES)
            p_out[j, :, cols] = jnp.dot(gath[j], w_out[h], preferred_element_type=F32).astype(BF16)
        o_begin(j, 0)

        @pl.when(j < SPLIT)
        def _():
            o_begin(j, 1)

        @pl.when(jnp.logical_and(j >= SPLIT, row_of(j) != y_lo))
        def _():
            remote(p_out.at[j, lower], o_y_in.at[j], send_sem.at[8], o_y_in_sem.at[j], y_near).start()

    def row_of(j):
        return lax.rem(j, 2)

    def quarter(part_index, k):
        return pl.ds(part_index * HALF + k * QUARTER, QUARTER)

    def own_columns(flip):
        return pl.ds(aligned(1 - core if flip else core, FEATURES), FEATURES)

    def to_column(src, j, s, kind, k, dx):
        for flip in (False, True):
            remote(
                src.at[:, own_columns(flip)],
                o_in.at[row_of(j), s, kind, k, core],
                send_sem.at[8],
                o_in_sem.at[row_of(j), s],
                at(dx=dx, flip_core=flip),
            ).start()

    def o_begin(j, s):
        dx = distance(j)

        @pl.when(dx == 2)
        def _():
            for k, peer in ((0, x_next), (1, x_prev)):
                remote(
                    p_out.at[j, quarter(s, k)], o_relay.at[s, j], send_sem.at[8], o_relay_sem.at[s, j], peer
                ).start()

        @pl.when(dx == 1)
        def _():
            to_column(p_out.at[j, quarter(s, 1)], j, s, 0, 1, 1)

        @pl.when(dx == 3)
        def _():
            to_column(p_out.at[j, quarter(s, 0)], j, s, 0, 0, 3)

        @pl.when(dx == 0)
        def _():
            rows = pl.ds(s * HALF, HALF)
            remote(
                p_out.at[j, rows, own_columns(True)],
                o_sib.at[row_of(j), s],
                send_sem.at[8],
                o_sib_sem.at[row_of(j), s],
                sibling,
            ).start()

    def o_pass(j, s):
        dx = distance(j)
        for want, k in ((1, 0), (3, 1)):

            @pl.when(dx == want)
            def _():
                wait_bytes(o_relay.at[s, j], o_relay_sem.at[s, j])
                o_relay[s, j] = (o_relay[s, j].astype(F32) + p_out[j, quarter(s, k), :].astype(F32)).astype(BF16)
                to_column(o_relay.at[s, j], j, s, 1, k, want)

    def o_total(j, s, k, mine):
        side = row_of(j)
        source = core if mine else 1 - core
        if mine:
            base = p_out[j, quarter(s, k), own_columns(False)]
        else:
            base = o_sib[side, s, pl.ds(k * QUARTER, QUARTER), :]
        return (
            base.astype(F32) + o_in[side, s, 0, k, source].astype(F32) + o_in[side, s, 1, k, source].astype(F32)
        )

    def o_arrived(j, s):
        wait_bytes(o_in.at[row_of(j), s], o_in_sem.at[row_of(j), s])
        wait_bytes(o_sib.at[row_of(j), s], o_sib_sem.at[row_of(j), s])

    def o_second(j):
        @pl.when(jnp.logical_and(j >= SPLIT, row_of(j) == y_lo))
        def _():
            wait_bytes(o_y_in.at[j], o_y_in_sem.at[j])
            p_out[j, lower, :] = (p_out[j, lower, :].astype(F32) + o_y_in[j].astype(F32)).astype(BF16)
            o_begin(j, 1)

        o_pass(j, 0)

        @pl.when(j < SPLIT)
        def _():
            o_pass(j, 1)

    def o_over(j, s):
        o_arrived(j, s)
        for k in range(2):
            for mine in (True, False):
                o_send[s, core if mine else 1 - core, k] = o_total(j, s, k, mine).astype(BF16)
        remote(o_send.at[s], o_y.at[s], send_sem.at[8], o_y_sem.at[s], y_near).start()

    def o_third(j):
        @pl.when(jnp.logical_and(j >= SPLIT, row_of(j) == y_lo))
        def _():
            o_pass(j, 1)

        @pl.when(jnp.logical_and(distance(j) == 0, row_of(j) != y_lo))
        def _():
            o_over(j, 0)

            @pl.when(j < SPLIT)
            def _():
                o_over(j, 1)

    def o_last(j):
        @pl.when(j == tp)
        def _():
            for s in (1, 0):
                o_arrived(j, s)
                if s == 0:
                    wait_bytes(o_y.at[0], o_y_sem.at[0])
                else:

                    @pl.when(j < SPLIT)
                    def _():
                        wait_bytes(o_y.at[1], o_y_sem.at[1])

                for k in range(2):
                    for mine in (True, False):
                        source = core if mine else 1 - core
                        total = o_total(j, s, k, mine) + o_y[s, source, k].astype(F32)
                        start = source * ROWS + s * HALF + k * QUARTER
                        out[pl.ds(pl.multiple_of(start, QUARTER), QUARTER), :] = total.astype(BF16)

    def step(n, carry):
        def stage(times, body):
            first_chunk, end_chunk = jnp.int32(0), jnp.int32(0)
            for time in times:
                first_chunk = first_chunk + jnp.where(n > time, 1, 0)
                end_chunk = end_chunk + jnp.where(n >= time, 1, 0)

            def call(j, unused):
                body(j)
                return unused

            lax.fori_loop(first_chunk, end_chunk, call, 0)

        @pl.when(n == 2)
        def _():
            wait_bytes(tok.at[near], tok_sem.at[near])
            relay_tokens(y_lo, 0)
            for peer in (x_next, x_prev):
                remote(tok.at[near], tok.at[near], send_sem.at[0], tok_sem.at[near], peer).start()

        @pl.when(n == 6)
        def _():
            relay_tokens(1 - y_lo, 1)

        stage(range(0, 2 * EARLY, 2), project)
        stage(START_LATE_AT, start_late)
        stage(range(1, 2 * EARLY, 2), lambda k: pass_on(order(k)))
        stage([t + 1 for t in START_LATE_AT], pass_late)
        stage(range(3, 2 * EARLY + 2, 2), lambda k: cross(order(k)))
        stage(PROJECT_LATE_AT, project_late)
        stage(CONVOLVE_AT, convolve)
        stage([t + 1 for t in CONVOLVE_AT[:DIRECT]], forward)
        stage(FINISH_AT, finish)
        stage([t + 1 for t in FINISH_AT], o_second)
        stage([t + 2 for t in FINISH_AT], o_third)
        stage([t + 3 for t in FINISH_AT], o_last)
        return carry

    lax.fori_loop(0, FINISH_AT[-1] + 4, step, 0)

    wait_bytes(tok.at[pl.ds(0, 7)], send_sem.at[0])
    wait_bytes(tok.at[0, :, pl.ds(0, FEATURES)], send_sem.at[0])
    wait_bytes(w_in.at[:, own_feat, :], send_sem.at[1])
    wait_bytes(out_weight, send_sem.at[1])
    early = pl.ds(0, EARLY)
    wait_bytes(relay.at[:, early], send_sem.at[2])
    wait_bytes(direct.at[:, early], send_sem.at[3])
    wait_bytes(summed.at[:, early], send_sem.at[4])
    wait_bytes(y_recv.at[early], send_sem.at[5])
    wait_bytes(crossed, send_sem.at[9])
    for arrived in (relay_l, direct_l, summed_l):
        wait_bytes(arrived, send_sem.at[10])
    wait_bytes(state_out.at[pl.ds(0, CHUNKS - 1)], send_sem.at[6])

    @pl.when(core == 0)
    def _():
        wait_bytes(state_out.at[0], send_sem.at[6])

    wait_bytes(gath.at[pl.ds(0, 7)], send_sem.at[7])
    wait_bytes(p_out.at[pl.ds(0, 7)], send_sem.at[8])
    wait_bytes(p_out.at[0, pl.ds(0, 3 * QUARTER)], send_sem.at[8])

    @pl.when(tp < SPLIT)
    def _():
        wait_bytes(p_out.at[0, pl.ds(0, QUARTER)], send_sem.at[8])


def local(tokens, in_weight, residues, decay_rates, skip_gain, out_weight):
    channels = in_weight.shape[2]
    vmem = pl.BlockSpec(memory_space=pltpu.VMEM)
    anywhere = pl.BlockSpec(memory_space=pl.ANY)
    dma = pltpu.SemaphoreType.DMA
    scratch = [
        pltpu.VMEM((MODES, LANES), F32),
        pltpu.VMEM((MODES, LANES), F32),
        pltpu.VMEM((1, LANES), F32),
        pltpu.VMEM((CHUNKS, ROWS, WIDE), BF16),
        pltpu.VMEM((4, WIDE, 2 * QKV), BF16),
        pltpu.VMEM((2, WIDE, FEATURES), BF16),
        pltpu.VMEM((CHUNKS, 4, ROWS, 2 * QKV), BF16),
        pltpu.VMEM((2, CHUNKS, ROWS, QKV), BF16),
        pltpu.VMEM((2, CHUNKS, ROWS, QKV), BF16),
        pltpu.VMEM((2, CHUNKS, ROWS, QKV), BF16),
        pltpu.VMEM((CHUNKS, ROWS, QKV), BF16),
        pltpu.VMEM((CHUNKS, ROWS, QKV), BF16),
        pltpu.VMEM((LATE, 4, ROWS, QKV), BF16),
        pltpu.VMEM((LATE, 2, HALF, QKV), BF16),
        pltpu.VMEM((LATE, 2, HALF, QKV), BF16),
        pltpu.VMEM((LATE, 2, HALF, QKV), BF16),
        pltpu.VMEM((ROWS, LANES), F32),
        pltpu.VMEM((ROWS, LANES), F32),
        pltpu.VMEM((ROWS, LANES), F32),
        pltpu.VMEM((MODES, SEGS, LANES), F32),
        pltpu.VMEM((MODES, SEGS, LANES), F32),
        pltpu.VMEM((MODES, SEGS, LANES), F32),
        pltpu.VMEM((3, MODES, SEGS, LANES), F32),
        pltpu.VMEM((MODES, SEGS, LANES), F32),
        pltpu.VMEM((CHUNKS + 1, MODES, LANES), F32),
        pltpu.VMEM((CHUNKS, MODES, LANES), F32),
        pltpu.VMEM((CHUNKS, ROWS, WIDE), BF16),
        pltpu.VMEM((CHUNKS, ROWS, WIDE), BF16),
        pltpu.VMEM((2, CHUNKS, QUARTER, WIDE), BF16),
        pltpu.VMEM((CHUNKS, HALF, WIDE), BF16),
        pltpu.VMEM((2, 2, 2, 2, 2, QUARTER, FEATURES), BF16),
        pltpu.VMEM((2, 2, HALF, FEATURES), BF16),
        pltpu.VMEM((2, 2, 2, QUARTER, FEATURES), BF16),
        pltpu.VMEM((2, 2, 2, QUARTER, FEATURES), BF16),
        dma((9,)),
        dma((CHUNKS + 1,)),
        dma((2, 2)),
        dma((4,)),
        dma((1,)),
        dma((2, CHUNKS)),
        dma((2, CHUNKS)),
        dma((2, CHUNKS)),
        dma((CHUNKS,)),
        dma((LATE,)),
        dma((LATE, 2)),
        dma((LATE, 2)),
        dma((LATE, 2)),
        dma((CHUNKS + 1,)),
        dma((8, CHUNKS)),
        dma((2, CHUNKS)),
        dma((CHUNKS,)),
        dma((2, 2)),
        dma((2, 2)),
        dma((2,)),
        dma((11,)),
    ]
    return pl.pallas_call(
        kernel,
        out_shape=pltpu.VMEM(tokens.shape, BF16),
        in_specs=[anywhere] * 6,
        out_specs=vmem,
        scratch_shapes=scratch,
        compiler_params=pltpu.CompilerParams(
            collective_id=0, has_side_effects=True, vmem_limit_bytes=56 * 2**20
        ),
        name="hyena_block",
    )(tokens, in_weight.transpose(1, 0, 2), residues, decay_rates, skip_gain.reshape(1, channels), out_weight)


def solution(mesh):
    in_specs = (
        P("tp", "seq"),
        P("seq", None, "tp"),
        P(None, "tp"),
        P(None, "tp"),
        P("tp"),
        P("tp", "seq"),
    )
    return jax.shard_map(local, mesh=mesh, in_specs=in_specs, out_specs=P("tp", "seq"), check_vma=False)
```

```python
import functools

import jax
import jax.numpy as jnp
from jax import lax
from jax.experimental import pallas as pl
from jax.experimental.pallas import tpu as pltpu
from jax.sharding import PartitionSpec as P

MESH = pl.DeviceIdType.MESH
F32 = jnp.float32
BF16 = jnp.bfloat16
CHUNKS = 8
ROWS = 128
HALF = 64
QUARTER = 32
LANES = 128
MODES = 16
SEGS = 8
STEPS = 16
QKV = 3 * LANES
FEATURES = 512
WIDE = 1024
DIRECT = 5
SPLIT = 5
EARLY = 7
LATE = CHUNKS - EARLY
PROJECT_LATE_AT = (8,)
START_LATE_AT = (14,)
CONVOLVE_AT = (12, 12, 13, 14, 14, 16, 16, 16)
FORWARD_AT = (13, 13, 14, 15, 15)
FINISH_AT = (15, 15, 15, 16, 16, 17, 17, 17)
CHUNK_ORDERS = (
    (0, 1, 2, 3, 4, 5, 6, 7),
    (1, 0, 3, 2, 4, 5, 6, 7),
    (2, 3, 0, 1, 4, 5, 6, 7),
    (3, 2, 1, 0, 4, 5, 6, 7),
    (4, 5, 0, 2, 1, 3, 6, 7),
    (5, 4, 1, 2, 0, 3, 6, 7),
    (6, 0, 2, 1, 3, 4, 5, 7),
    (7, 1, 3, 0, 2, 4, 5, 6),
)
ORDERS = tuple(sum(chunk << (3 * k) for k, chunk in enumerate(row)) for row in CHUNK_ORDERS)


def remote(src, dst, send_sem, recv_sem, device):
    return pltpu.make_async_remote_copy(
        src_ref=src,
        dst_ref=dst,
        send_sem=send_sem,
        recv_sem=recv_sem,
        device_id=device,
        device_id_type=MESH,
    )


def wait_bytes(ref, sem):
    pltpu.make_async_copy(ref, ref, sem).wait()


def aligned(value, step):
    return pl.multiple_of(value * step, step)


def kernel(
    tokens,
    in_weight,
    residues_in,
    decay_rates_in,
    skip_gain_in,
    out_weight,
    out,
    residues,
    decay_rates,
    skip_gain,
    tok,
    w_in,
    w_out,
    part,
    relay,
    direct,
    summed,
    y_send,
    y_recv,
    crossed,
    relay_l,
    direct_l,
    summed_l,
    s_scr,
    y_scr,
    q_scr,
    decay_b,
    res_b,
    seg_b,
    scan_b,
    ends,
    state_in,
    state_out,
    carry,
    start,
    span,
    gath,
    p_out,
    o_relay,
    o_y_in,
    o_in,
    o_sib,
    o_send,
    o_y,
    local_sem,
    tok_sem,
    far_sem,
    w_sem,
    wo_sem,
    relay_sem,
    direct_sem,
    summed_sem,
    y_sem,
    crossed_sem,
    relay_l_sem,
    direct_l_sem,
    summed_l_sem,
    state_sem,
    gath_sem,
    o_relay_sem,
    o_y_in_sem,
    o_in_sem,
    o_sib_sem,
    o_y_sem,
    send_sem,
):
    seq = lax.axis_index("seq")
    tp = lax.axis_index("tp")
    core = lax.rem(seq, 2)
    z = lax.rem(seq // 2, 4)
    y_hi = seq // 8
    x = tp // 2
    y_lo = lax.rem(tp, 2)

    def at(dx=0, dz=0, flip_hi=False, flip_lo=False, flip_core=False):
        a = 1 - y_hi if flip_hi else y_hi
        b = lax.rem(z + dz, 4)
        c = 1 - core if flip_core else core
        d = lax.rem(x + dx, 4)
        e = 1 - y_lo if flip_lo else y_lo
        return (a * 8 + b * 2 + c, d * 2 + e)

    sibling = at(flip_core=True)
    z_next, z_prev, z_far = at(dz=1), at(dz=3), at(dz=2)
    y_far = at(flip_hi=True)
    x_next, x_prev = at(dx=1), at(dx=3)
    y_near = at(flip_lo=True)
    diagonals = [at(dz=r, flip_hi=True) for r in (2, 1, 3)]
    peers = [sibling, z_next, z_prev, z_far, y_far, x_next, x_prev, y_near, *diagonals]
    peers += [at(dx=1, flip_core=True), at(dx=3, flip_core=True)]
    block = y_hi * 4 + z
    lanes = pl.ds(aligned(block, LANES), LANES)

    barrier = pltpu.get_barrier_semaphore()
    for peer in peers:
        pl.semaphore_signal(barrier, inc=1, device_id=peer, device_id_type=MESH)

    own_rows = pl.ds(aligned(core, ROWS), ROWS)
    other_rows = pl.ds(aligned(1 - core, ROWS), ROWS)
    own_feat = pl.ds(aligned(core, FEATURES), FEATURES)
    other_feat = pl.ds(aligned(1 - core, FEATURES), FEATURES)
    pltpu.make_async_copy(tokens.at[own_rows, :], tok.at[tp, :, own_feat], local_sem.at[0]).start()

    def own_weight(r):
        return w_in.at[lax.rem(z + r, 4), own_feat, :]

    for r in (2, 1, 3, 0):
        zi = lax.rem(z + r, 4)
        for h in range(2):
            there = pl.ds(aligned(h * 4 + zi, LANES), LANES)
            for k in range(3):
                pltpu.make_async_copy(
                    in_weight.at[k, :, there],
                    w_in.at[zi, own_feat, pl.ds((h * 3 + k) * LANES, LANES)],
                    local_sem.at[1 + r],
                ).start()
    pltpu.make_async_copy(out_weight, w_out.at[core], local_sem.at[5]).start()
    small = [
        pltpu.make_async_copy(whole.at[:, lanes], piece, local_sem.at[6 + k])
        for k, (whole, piece) in enumerate(
            ((residues_in, residues), (decay_rates_in, decay_rates), (skip_gain_in, skip_gain))
        )
    ]
    for copy in small:
        copy.start()

    pl.semaphore_wait(barrier, len(peers))
    remote(tokens.at[other_rows, :], tok.at[tp, :, own_feat], send_sem.at[0], tok_sem.at[CHUNKS], sibling).start()
    wait_bytes(own_weight(2), local_sem.at[3])
    remote(own_weight(2), own_weight(2), send_sem.at[1], w_sem.at[2], sibling).start()
    wait_bytes(tok.at[0, :, pl.ds(0, FEATURES)], local_sem.at[0])
    wait_bytes(tok.at[0, :, pl.ds(0, FEATURES)], tok_sem.at[CHUNKS])
    for peer in (y_near, x_next, x_prev):
        remote(tok.at[tp], tok.at[tp], send_sem.at[0], tok_sem.at[tp], peer).start()
    for r in (1, 3, 0):
        wait_bytes(own_weight(r), local_sem.at[1 + r])
        remote(own_weight(r), own_weight(r), send_sem.at[1], w_sem.at[r], sibling).start()
    remote(out_weight, w_out.at[core], send_sem.at[1], wo_sem.at[0], sibling).start()

    for copy in small:
        copy.wait()
    seg_index = lax.broadcasted_iota(jnp.int32, (SEGS, LANES), 0)
    seg_next = (seg_index + 1).astype(F32) * float(STEPS)
    for m in range(MODES):
        rate = jnp.broadcast_to(decay_rates[pl.ds(m, 1), :], (SEGS, LANES))
        decay_b[m] = jnp.exp(-rate)
        res_b[m] = jnp.broadcast_to(residues[pl.ds(m, 1), :], (SEGS, LANES))
        seg_b[m] = jnp.exp(-rate * seg_next)
        for k in range(3):
            scan_b[k, m] = jnp.where(seg_index >= (1 << k), jnp.exp(-rate * float(STEPS << k)), 0.0)

    carry[...] = jnp.zeros((MODES, LANES), F32)
    start[...] = jnp.zeros((MODES, LANES), F32)
    span[...] = jnp.exp(-decay_rates[...] * float(ROWS))

    @pl.when(tp >= SPLIT)
    def _():
        o_y[1] = jnp.zeros((2, 2, QUARTER, FEATURES), BF16)

    upper, lower = pl.ds(0, HALF), pl.ds(HALF, HALF)
    near = x * 2 + 1 - y_lo
    code = jnp.int32(ORDERS[0])
    for t in range(1, 8):
        code = jnp.where(tp == t, jnp.int32(ORDERS[t]), code)

    def order(i):
        return lax.shift_right_logical(code, 3 * i) & 7

    def column_chunk(dx, row):
        return lax.rem(x + dx, 4) * 2 + row

    def relay_tokens(row, far):
        after, before = column_chunk(1, row), column_chunk(3, row)
        for chunk in (after, before):
            wait_bytes(tok.at[chunk], tok_sem.at[chunk])
        remote(
            tok.at[before, upper], tok.at[before, upper], send_sem.at[0], far_sem.at[far, 0], x_next
        ).start()
        remote(tok.at[after, lower], tok.at[after, lower], send_sem.at[0], far_sem.at[far, 1], x_prev).start()

    def multiply(jc, r):
        zi = lax.rem(z + r, 4)

        part[jc, r] = jnp.dot(tok[jc], w_in[zi], preferred_element_type=F32).astype(BF16)

    first, second = pl.ds(0, QKV), pl.ds(QKV, QKV)

    def await_tokens(jc):
        for far, row in ((0, y_lo), (1, 1 - y_lo)):

            @pl.when(jc == column_chunk(2, row))
            def _():
                wait_bytes(tok.at[jc, upper], far_sem.at[far, 0])
                wait_bytes(tok.at[jc, lower], far_sem.at[far, 1])

    def project(i):
        jc = order(i)
        await_tokens(jc)

        for r in (2, 1, 3, 0):

            @pl.when(i == 0)
            def _():
                wait_bytes(w_in.at[0, other_feat, :], w_sem.at[r])

            multiply(jc, r)
            if r == 2:
                remote(part.at[jc, 2, :, first], relay.at[0, jc], send_sem.at[2], relay_sem.at[0, jc], z_next).start()
                remote(part.at[jc, 2, :, second], relay.at[1, jc], send_sem.at[2], relay_sem.at[1, jc], z_prev).start()
            elif r == 1:
                remote(part.at[jc, 1, :, second], direct.at[1, jc], send_sem.at[3], direct_sem.at[1, jc], z_next).start()
            elif r == 3:
                remote(part.at[jc, 3, :, first], direct.at[0, jc], send_sem.at[3], direct_sem.at[0, jc], z_prev).start()

    def project_late(u):
        jc = order(EARLY + u)
        await_tokens(jc)
        theirs = pl.ds(aligned(1 - y_hi, QKV), QKV)
        for r in (2, 1, 3, 0):
            multiply(jc, r)
            remote(part.at[jc, r, :, theirs], crossed.at[u, r], send_sem.at[9], crossed_sem.at[u], y_far).start()

    def start_late(u):
        jc = order(EARLY + u)
        mine = pl.ds(aligned(y_hi, QKV), QKV)
        wait_bytes(crossed.at[u], crossed_sem.at[u])
        for r in (2, 1, 3, 0):
            crossed[u, r] = (crossed[u, r].astype(F32) + part[jc, r, :, mine].astype(F32)).astype(BF16)
            if r == 2:
                for k, rows, peer in ((0, upper, z_next), (1, lower, z_prev)):
                    remote(
                        crossed.at[u, 2, rows], relay_l.at[u, k], send_sem.at[10], relay_l_sem.at[u, k], peer
                    ).start()
            elif r == 1:
                remote(
                    crossed.at[u, 1, lower], direct_l.at[u, 1], send_sem.at[10], direct_l_sem.at[u, 1], z_next
                ).start()
            elif r == 3:
                remote(
                    crossed.at[u, 3, upper], direct_l.at[u, 0], send_sem.at[10], direct_l_sem.at[u, 0], z_prev
                ).start()

    def pass_late(u):
        for k, r, rows, peer in ((0, 1, upper, z_next), (1, 3, lower, z_prev)):
            wait_bytes(relay_l.at[u, k], relay_l_sem.at[u, k])
            relay_l[u, k] = (relay_l[u, k].astype(F32) + crossed[u, r, rows].astype(F32)).astype(BF16)
            remote(relay_l.at[u, k], summed_l.at[u, k], send_sem.at[10], summed_l_sem.at[u, k], peer).start()

    def pass_on(jc):
        for k, r, cols, peer in ((0, 1, first, z_next), (1, 3, second, z_prev)):
            wait_bytes(relay.at[k, jc], relay_sem.at[k, jc])
            relay[k, jc] = (relay[k, jc].astype(F32) + part[jc, r, :, cols].astype(F32)).astype(BF16)
            remote(relay.at[k, jc], summed.at[k, jc], send_sem.at[4], summed_sem.at[k, jc], peer).start()

    def gather_half(jc, k):
        cols = pl.ds(aligned(k, QKV), QKV)
        return part[jc, 0, :, cols].astype(F32) + direct[k, jc].astype(F32) + summed[k, jc].astype(F32)

    def cross(jc):
        for k in range(2):
            wait_bytes(direct.at[k, jc], direct_sem.at[k, jc])
            wait_bytes(summed.at[k, jc], summed_sem.at[k, jc])
        y_send[jc] = gather_half(jc, 1 - y_hi).astype(BF16)
        remote(y_send.at[jc], y_recv.at[jc], send_sem.at[5], y_sem.at[jc], y_far).start()

    def convolve(j):
        def keep(rows, total):
            q_scr[rows, :] = total[:, :LANES]
            s_scr[rows, :] = total[:, LANES : 2 * LANES] * total[:, 2 * LANES :]

        late = jnp.int32(-1)
        for u in range(LATE):
            late = jnp.where(order(EARLY + u) == j, u, late)

        @pl.when(late < 0)
        def _():
            wait_bytes(y_recv.at[j], y_sem.at[j])
            keep(pl.ds(0, ROWS), gather_half(j, y_hi) + y_recv[j].astype(F32))

        @pl.when(late >= 0)
        def _():
            for k, rows in ((0, upper), (1, lower)):
                wait_bytes(direct_l.at[late, k], direct_l_sem.at[late, k])
                wait_bytes(summed_l.at[late, k], summed_l_sem.at[late, k])
                keep(
                    rows,
                    crossed[late, 0, rows].astype(F32)
                    + direct_l[late, k].astype(F32)
                    + summed_l[late, k].astype(F32),
                )

        decay = [decay_b[m] for m in range(MODES)]
        held = [jnp.zeros((SEGS, LANES), F32)] * MODES
        for i in range(STEPS):
            now = s_scr[pl.ds(i, SEGS, stride=STEPS), :]
            held = [decay[m] * held[m] + now for m in range(MODES)]
        for m in range(MODES):
            total = held[m]
            for k in range(3):
                total = total + scan_b[k, m] * pltpu.roll(total, 1 << k, 0)
            ends[m] = total
            state_out[j, pl.ds(m, 1), :] = total[SEGS - 1 :, :]

        @pl.when(jnp.logical_or(core == 0, j < CHUNKS - 1))
        def _():
            remote(state_out.at[j], state_in.at[j], send_sem.at[6], state_sem.at[j], sibling).start()

        @pl.when(core == 1)
        def _():
            wait_bytes(state_in.at[j], state_sem.at[j])
            before = span[...] * carry[...] + state_in[j]
            start[...] = before
            carry[...] = span[...] * before + state_out[j]

        @pl.when(jnp.logical_and(core == 0, j > 0))
        def _():
            wait_bytes(state_in.at[j - 1], state_sem.at[j - 1])
            before = span[...] * (span[...] * carry[...] + state_out[j - 1]) + state_in[j - 1]
            start[...] = before
            carry[...] = before

        for m in range(MODES):
            before = jnp.broadcast_to(start[pl.ds(m, 1), :], (SEGS, LANES))
            full = ends[m] + seg_b[m] * before
            ends[m] = jnp.where(seg_index == 0, before, pltpu.roll(full, 1, 0))

        held = [ends[m] for m in range(MODES)]
        for i in range(STEPS):
            now = s_scr[pl.ds(i, SEGS, stride=STEPS), :]
            held = [decay_b[m] * held[m] + now for m in range(MODES)]
            terms = [res_b[m] * held[m] for m in range(MODES)]
            while len(terms) > 1:
                terms = [terms[k] + terms[k + 1] for k in range(0, len(terms), 2)]
            y_scr[pl.ds(i, SEGS, stride=STEPS), :] = terms[0]
        gain = skip_gain[...]
        gath[j, :, lanes] = (q_scr[...] * (y_scr[...] + gain * s_scr[...])).astype(BF16)
        own = gath.at[j, :, lanes]
        for peer in (z_far, z_next, z_prev, y_far):
            remote(own, own, send_sem.at[7], gath_sem.at[block, j], peer).start()

        @pl.when(j >= DIRECT)
        def _():
            for peer in diagonals:
                remote(own, own, send_sem.at[7], gath_sem.at[block, j], peer).start()

    def forward(j):
        for r in (1, 3, 2):
            b = y_hi * 4 + lax.rem(z + r, 4)
            there = gath.at[j, :, pl.ds(aligned(b, LANES), LANES)]
            wait_bytes(there, gath_sem.at[b, j])
            remote(there, there, send_sem.at[7], gath_sem.at[b, j], y_far).start()

    def distance(j):
        return lax.rem(j // 2 - x + 4, 4)

    def finish(j):
        for r in range(4):
            b = (1 - y_hi) * 4 + r
            wait_bytes(gath.at[j, :, pl.ds(aligned(b, LANES), LANES)], gath_sem.at[b, j])

        @pl.when(j >= DIRECT)
        def _():
            for r in (1, 3, 2):
                b = y_hi * 4 + lax.rem(z + r, 4)
                wait_bytes(gath.at[j, :, pl.ds(aligned(b, LANES), LANES)], gath_sem.at[b, j])

        @pl.when(j == 0)
        def _():
            pltpu.make_async_copy(out_weight, w_out.at[core], local_sem.at[5]).wait()
            wait_bytes(w_out.at[1 - core], wo_sem.at[0])

        for h in range(2):
            cols = pl.ds(h * FEATURES, FEATURES)
            p_out[j, :, cols] = jnp.dot(gath[j], w_out[h], preferred_element_type=F32).astype(BF16)
        o_begin(j, 0)

        @pl.when(j < SPLIT)
        def _():
            o_begin(j, 1)

        @pl.when(jnp.logical_and(j >= SPLIT, row_of(j) != y_lo))
        def _():
            remote(p_out.at[j, lower], o_y_in.at[j], send_sem.at[8], o_y_in_sem.at[j], y_near).start()

    def row_of(j):
        return lax.rem(j, 2)

    def quarter(part_index, k):
        return pl.ds(part_index * HALF + k * QUARTER, QUARTER)

    def own_columns(flip):
        return pl.ds(aligned(1 - core if flip else core, FEATURES), FEATURES)

    def to_column(src, j, s, kind, k, dx):
        for flip in (False, True):
            remote(
                src.at[:, own_columns(flip)],
                o_in.at[row_of(j), s, kind, k, core],
                send_sem.at[8],
                o_in_sem.at[row_of(j), s],
                at(dx=dx, flip_core=flip),
            ).start()

    def o_begin(j, s):
        dx = distance(j)

        @pl.when(dx == 2)
        def _():
            for k, peer in ((0, x_next), (1, x_prev)):
                remote(
                    p_out.at[j, quarter(s, k)], o_relay.at[s, j], send_sem.at[8], o_relay_sem.at[s, j], peer
                ).start()

        @pl.when(dx == 1)
        def _():
            to_column(p_out.at[j, quarter(s, 1)], j, s, 0, 1, 1)

        @pl.when(dx == 3)
        def _():
            to_column(p_out.at[j, quarter(s, 0)], j, s, 0, 0, 3)

        @pl.when(dx == 0)
        def _():
            rows = pl.ds(s * HALF, HALF)
            remote(
                p_out.at[j, rows, own_columns(True)],
                o_sib.at[row_of(j), s],
                send_sem.at[8],
                o_sib_sem.at[row_of(j), s],
                sibling,
            ).start()

    def o_pass(j, s):
        dx = distance(j)
        for want, k in ((1, 0), (3, 1)):

            @pl.when(dx == want)
            def _():
                wait_bytes(o_relay.at[s, j], o_relay_sem.at[s, j])
                o_relay[s, j] = (o_relay[s, j].astype(F32) + p_out[j, quarter(s, k), :].astype(F32)).astype(BF16)
                to_column(o_relay.at[s, j], j, s, 1, k, want)

    def o_total(j, s, k, mine):
        side = row_of(j)
        source = core if mine else 1 - core
        if mine:
            base = p_out[j, quarter(s, k), own_columns(False)]
        else:
            base = o_sib[side, s, pl.ds(k * QUARTER, QUARTER), :]
        return (
            base.astype(F32) + o_in[side, s, 0, k, source].astype(F32) + o_in[side, s, 1, k, source].astype(F32)
        )

    def o_arrived(j, s):
        wait_bytes(o_in.at[row_of(j), s], o_in_sem.at[row_of(j), s])
        wait_bytes(o_sib.at[row_of(j), s], o_sib_sem.at[row_of(j), s])

    def o_second(j):
        @pl.when(jnp.logical_and(j >= SPLIT, row_of(j) == y_lo))
        def _():
            wait_bytes(o_y_in.at[j], o_y_in_sem.at[j])
            p_out[j, lower, :] = (p_out[j, lower, :].astype(F32) + o_y_in[j].astype(F32)).astype(BF16)
            o_begin(j, 1)

        o_pass(j, 0)

        @pl.when(j < SPLIT)
        def _():
            o_pass(j, 1)

    def o_over(j, s):
        o_arrived(j, s)
        for k in range(2):
            for mine in (True, False):
                o_send[s, core if mine else 1 - core, k] = o_total(j, s, k, mine).astype(BF16)
        remote(o_send.at[s], o_y.at[s], send_sem.at[8], o_y_sem.at[s], y_near).start()

    def o_third(j):
        @pl.when(jnp.logical_and(j >= SPLIT, row_of(j) == y_lo))
        def _():
            o_pass(j, 1)

        @pl.when(jnp.logical_and(distance(j) == 0, row_of(j) != y_lo))
        def _():
            o_over(j, 0)

            @pl.when(j < SPLIT)
            def _():
                o_over(j, 1)

    def o_last(j):
        @pl.when(j == tp)
        def _():
            for s in (1, 0):
                o_arrived(j, s)
                if s == 0:
                    wait_bytes(o_y.at[0], o_y_sem.at[0])
                else:

                    @pl.when(j < SPLIT)
                    def _():
                        wait_bytes(o_y.at[1], o_y_sem.at[1])

                for k in range(2):
                    for mine in (True, False):
                        source = core if mine else 1 - core
                        total = o_total(j, s, k, mine) + o_y[s, source, k].astype(F32)
                        start = source * ROWS + s * HALF + k * QUARTER
                        out[pl.ds(pl.multiple_of(start, QUARTER), QUARTER), :] = total.astype(BF16)

    def step(n, carry):
        def stage(times, body):
            first_chunk, end_chunk = jnp.int32(0), jnp.int32(0)
            for time in times:
                first_chunk = first_chunk + jnp.where(n > time, 1, 0)
                end_chunk = end_chunk + jnp.where(n >= time, 1, 0)

            def call(j, unused):
                body(j)
                return unused

            lax.fori_loop(first_chunk, end_chunk, call, 0)

        @pl.when(n == 2)
        def _():
            wait_bytes(tok.at[near], tok_sem.at[near])
            relay_tokens(y_lo, 0)
            for peer in (x_next, x_prev):
                remote(tok.at[near], tok.at[near], send_sem.at[0], tok_sem.at[near], peer).start()

        @pl.when(n == 6)
        def _():
            relay_tokens(1 - y_lo, 1)

        stage(range(0, 2 * EARLY, 2), project)
        stage(START_LATE_AT, start_late)
        stage(range(1, 2 * EARLY, 2), lambda k: pass_on(order(k)))
        stage([t + 1 for t in START_LATE_AT], pass_late)
        stage(range(3, 2 * EARLY + 2, 2), lambda k: cross(order(k)))
        stage(PROJECT_LATE_AT, project_late)
        stage(CONVOLVE_AT, convolve)
        stage(FORWARD_AT, forward)
        stage(FINISH_AT, finish)
        stage([t + 1 for t in FINISH_AT], o_second)
        stage([t + 2 for t in FINISH_AT], o_third)
        stage([t + 3 for t in FINISH_AT], o_last)
        return carry

    lax.fori_loop(0, FINISH_AT[-1] + 4, step, 0)

    wait_bytes(tok.at[pl.ds(0, 7)], send_sem.at[0])
    wait_bytes(tok.at[0, :, pl.ds(0, FEATURES)], send_sem.at[0])
    wait_bytes(w_in.at[:, own_feat, :], send_sem.at[1])
    wait_bytes(out_weight, send_sem.at[1])
    early = pl.ds(0, EARLY)
    wait_bytes(relay.at[:, early], send_sem.at[2])
    wait_bytes(direct.at[:, early], send_sem.at[3])
    wait_bytes(summed.at[:, early], send_sem.at[4])
    wait_bytes(y_recv.at[early], send_sem.at[5])
    wait_bytes(crossed, send_sem.at[9])
    for arrived in (relay_l, direct_l, summed_l):
        wait_bytes(arrived, send_sem.at[10])
    wait_bytes(state_out.at[pl.ds(0, CHUNKS - 1)], send_sem.at[6])

    @pl.when(core == 0)
    def _():
        wait_bytes(state_out.at[0], send_sem.at[6])

    wait_bytes(gath.at[pl.ds(0, 7)], send_sem.at[7])
    wait_bytes(p_out.at[pl.ds(0, 7)], send_sem.at[8])
    wait_bytes(p_out.at[0, pl.ds(0, 3 * QUARTER)], send_sem.at[8])

    @pl.when(near < SPLIT)
    def _():
        wait_bytes(p_out.at[0, pl.ds(0, QUARTER)], send_sem.at[8])


def local(tokens, in_weight, residues, decay_rates, skip_gain, out_weight):
    channels = in_weight.shape[2]
    vmem = pl.BlockSpec(memory_space=pltpu.VMEM)
    anywhere = pl.BlockSpec(memory_space=pl.ANY)
    dma = pltpu.SemaphoreType.DMA
    scratch = [
        pltpu.VMEM((MODES, LANES), F32),
        pltpu.VMEM((MODES, LANES), F32),
        pltpu.VMEM((1, LANES), F32),
        pltpu.VMEM((CHUNKS, ROWS, WIDE), BF16),
        pltpu.VMEM((4, WIDE, 2 * QKV), BF16),
        pltpu.VMEM((2, WIDE, FEATURES), BF16),
        pltpu.VMEM((CHUNKS, 4, ROWS, 2 * QKV), BF16),
        pltpu.VMEM((2, CHUNKS, ROWS, QKV), BF16),
        pltpu.VMEM((2, CHUNKS, ROWS, QKV), BF16),
        pltpu.VMEM((2, CHUNKS, ROWS, QKV), BF16),
        pltpu.VMEM((CHUNKS, ROWS, QKV), BF16),
        pltpu.VMEM((CHUNKS, ROWS, QKV), BF16),
        pltpu.VMEM((LATE, 4, ROWS, QKV), BF16),
        pltpu.VMEM((LATE, 2, HALF, QKV), BF16),
        pltpu.VMEM((LATE, 2, HALF, QKV), BF16),
        pltpu.VMEM((LATE, 2, HALF, QKV), BF16),
        pltpu.VMEM((ROWS, LANES), F32),
        pltpu.VMEM((ROWS, LANES), F32),
        pltpu.VMEM((ROWS, LANES), F32),
        pltpu.VMEM((MODES, SEGS, LANES), F32),
        pltpu.VMEM((MODES, SEGS, LANES), F32),
        pltpu.VMEM((MODES, SEGS, LANES), F32),
        pltpu.VMEM((3, MODES, SEGS, LANES), F32),
        pltpu.VMEM((MODES, SEGS, LANES), F32),
        pltpu.VMEM((CHUNKS + 1, MODES, LANES), F32),
        pltpu.VMEM((CHUNKS, MODES, LANES), F32),
        pltpu.VMEM((MODES, LANES), F32),
        pltpu.VMEM((MODES, LANES), F32),
        pltpu.VMEM((MODES, LANES), F32),
        pltpu.VMEM((CHUNKS, ROWS, WIDE), BF16),
        pltpu.VMEM((CHUNKS, ROWS, WIDE), BF16),
        pltpu.VMEM((2, CHUNKS, QUARTER, WIDE), BF16),
        pltpu.VMEM((CHUNKS, HALF, WIDE), BF16),
        pltpu.VMEM((2, 2, 2, 2, 2, QUARTER, FEATURES), BF16),
        pltpu.VMEM((2, 2, HALF, FEATURES), BF16),
        pltpu.VMEM((2, 2, 2, QUARTER, FEATURES), BF16),
        pltpu.VMEM((2, 2, 2, QUARTER, FEATURES), BF16),
        dma((9,)),
        dma((CHUNKS + 1,)),
        dma((2, 2)),
        dma((4,)),
        dma((1,)),
        dma((2, CHUNKS)),
        dma((2, CHUNKS)),
        dma((2, CHUNKS)),
        dma((CHUNKS,)),
        dma((LATE,)),
        dma((LATE, 2)),
        dma((LATE, 2)),
        dma((LATE, 2)),
        dma((CHUNKS + 1,)),
        dma((8, CHUNKS)),
        dma((2, CHUNKS)),
        dma((CHUNKS,)),
        dma((2, 2)),
        dma((2, 2)),
        dma((2,)),
        dma((11,)),
    ]
    return pl.pallas_call(
        kernel,
        out_shape=pltpu.VMEM(tokens.shape, BF16),
        in_specs=[anywhere] * 6,
        out_specs=vmem,
        scratch_shapes=scratch,
        compiler_params=pltpu.CompilerParams(
            collective_id=0, has_side_effects=True, vmem_limit_bytes=56 * 2**20
        ),
        name="hyena_block",
    )(tokens, in_weight.transpose(1, 0, 2), residues, decay_rates, skip_gain.reshape(1, channels), out_weight)


def solution(mesh):
    in_specs = (
        P("tp", "seq"),
        P("seq", None, "tp"),
        P(None, "tp"),
        P(None, "tp"),
        P("tp"),
        P("tp", "seq"),
    )
    return jax.shard_map(local, mesh=mesh, in_specs=in_specs, out_specs=P("tp", "seq"), check_vma=False)
```

```python
import functools

import jax
import jax.numpy as jnp
from jax import lax
from jax.experimental import pallas as pl
from jax.experimental.pallas import tpu as pltpu
from jax.sharding import PartitionSpec as P

MESH = pl.DeviceIdType.MESH
F32 = jnp.float32
BF16 = jnp.bfloat16
CHUNKS = 8
ROWS = 128
HALF = 64
QUARTER = 32
LANES = 128
MODES = 16
SEGS = 8
STEPS = 16
QKV = 3 * LANES
FEATURES = 512
WIDE = 1024
DIRECT = 5
SPLIT = 5
EARLY = 7
LATE = CHUNKS - EARLY
PROJECT_LATE_AT = (8,)
START_LATE_AT = (14,)
CONVOLVE_AT = (12, 12, 13, 14, 14, 16, 16, 16)
FORWARD_AT = (13, 13, 14, 15, 15)
FINISH_AT = (15, 15, 15, 16, 16, 17, 17, 17)
CHUNK_ORDERS = (
    (0, 1, 2, 3, 4, 5, 6, 7),
    (1, 0, 3, 2, 4, 5, 6, 7),
    (2, 3, 0, 1, 4, 5, 6, 7),
    (3, 2, 1, 0, 4, 5, 6, 7),
    (4, 5, 0, 2, 1, 3, 6, 7),
    (5, 4, 1, 2, 0, 3, 6, 7),
    (6, 0, 2, 1, 3, 4, 5, 7),
    (7, 1, 3, 0, 2, 4, 5, 6),
)
ORDERS = tuple(sum(chunk << (3 * k) for k, chunk in enumerate(row)) for row in CHUNK_ORDERS)


def remote(src, dst, send_sem, recv_sem, device):
    return pltpu.make_async_remote_copy(
        src_ref=src,
        dst_ref=dst,
        send_sem=send_sem,
        recv_sem=recv_sem,
        device_id=device,
        device_id_type=MESH,
    )


def wait_bytes(ref, sem):
    pltpu.make_async_copy(ref, ref, sem).wait()


def aligned(value, step):
    return pl.multiple_of(value * step, step)


def kernel(
    tokens,
    in_weight,
    residues_in,
    decay_rates_in,
    skip_gain_in,
    out_weight,
    out,
    residues,
    decay_rates,
    skip_gain,
    tok,
    w_in,
    w_out,
    part,
    relay,
    direct,
    summed,
    y_send,
    y_recv,
    crossed,
    relay_l,
    direct_l,
    summed_l,
    s_scr,
    y_scr,
    q_scr,
    decay_b,
    res_b,
    seg_b,
    scan_b,
    ends,
    state_in,
    state_out,
    carry,
    start,
    span,
    gath,
    p_out,
    o_relay,
    o_y_in,
    o_in,
    o_sib,
    o_send,
    o_y,
    local_sem,
    tok_sem,
    far_sem,
    w_sem,
    wo_sem,
    relay_sem,
    direct_sem,
    summed_sem,
    y_sem,
    crossed_sem,
    relay_l_sem,
    direct_l_sem,
    summed_l_sem,
    state_sem,
    gath_sem,
    o_relay_sem,
    o_y_in_sem,
    o_in_sem,
    o_sib_sem,
    o_y_sem,
    send_sem,
):
    seq = lax.axis_index("seq")
    tp = lax.axis_index("tp")
    core = lax.rem(seq, 2)
    z = lax.rem(seq // 2, 4)
    y_hi = seq // 8
    x = tp // 2
    y_lo = lax.rem(tp, 2)

    def at(dx=0, dz=0, flip_hi=False, flip_lo=False, flip_core=False):
        a = 1 - y_hi if flip_hi else y_hi
        b = lax.rem(z + dz, 4)
        c = 1 - core if flip_core else core
        d = lax.rem(x + dx, 4)
        e = 1 - y_lo if flip_lo else y_lo
        return (a * 8 + b * 2 + c, d * 2 + e)

    sibling = at(flip_core=True)
    z_next, z_prev, z_far = at(dz=1), at(dz=3), at(dz=2)
    y_far = at(flip_hi=True)
    x_next, x_prev = at(dx=1), at(dx=3)
    y_near = at(flip_lo=True)
    diagonals = [at(dz=r, flip_hi=True) for r in (2, 1, 3)]
    peers = [sibling, z_next, z_prev, z_far, y_far, x_next, x_prev, y_near, *diagonals]
    peers += [at(dx=1, flip_core=True), at(dx=3, flip_core=True)]
    block = y_hi * 4 + z
    lanes = pl.ds(aligned(block, LANES), LANES)

    barrier = pltpu.get_barrier_semaphore()
    for peer in peers:
        pl.semaphore_signal(barrier, inc=1, device_id=peer, device_id_type=MESH)

    own_rows = pl.ds(aligned(core, ROWS), ROWS)
    other_rows = pl.ds(aligned(1 - core, ROWS), ROWS)
    own_feat = pl.ds(aligned(core, FEATURES), FEATURES)
    other_feat = pl.ds(aligned(1 - core, FEATURES), FEATURES)
    pltpu.make_async_copy(tokens.at[own_rows, :], tok.at[tp, :, own_feat], local_sem.at[0]).start()

    def own_weight(r):
        return w_in.at[lax.rem(z + r, 4), own_feat, :]

    for r in (2, 1, 3, 0):
        zi = lax.rem(z + r, 4)
        for h in range(2):
            there = pl.ds(aligned(h * 4 + zi, LANES), LANES)
            for k in range(3):
                pltpu.make_async_copy(
                    in_weight.at[k, :, there],
                    w_in.at[zi, own_feat, pl.ds((h * 3 + k) * LANES, LANES)],
                    local_sem.at[1 + r],
                ).start()
    pltpu.make_async_copy(out_weight, w_out.at[core], local_sem.at[5]).start()
    small = [
        pltpu.make_async_copy(whole.at[:, lanes], piece, local_sem.at[6 + k])
        for k, (whole, piece) in enumerate(
            ((residues_in, residues), (decay_rates_in, decay_rates), (skip_gain_in, skip_gain))
        )
    ]
    for copy in small:
        copy.start()

    pl.semaphore_wait(barrier, len(peers))
    remote(tokens.at[other_rows, :], tok.at[tp, :, own_feat], send_sem.at[0], tok_sem.at[CHUNKS], sibling).start()
    wait_bytes(own_weight(2), local_sem.at[3])
    remote(own_weight(2), own_weight(2), send_sem.at[1], w_sem.at[2], sibling).start()
    wait_bytes(tok.at[0, :, pl.ds(0, FEATURES)], local_sem.at[0])
    wait_bytes(tok.at[0, :, pl.ds(0, FEATURES)], tok_sem.at[CHUNKS])
    for peer in (y_near, x_next, x_prev):
        remote(tok.at[tp], tok.at[tp], send_sem.at[0], tok_sem.at[tp], peer).start()
    for r in (1, 3, 0):
        wait_bytes(own_weight(r), local_sem.at[1 + r])
        remote(own_weight(r), own_weight(r), send_sem.at[1], w_sem.at[r], sibling).start()
    remote(out_weight, w_out.at[core], send_sem.at[1], wo_sem.at[0], sibling).start()

    for copy in small:
        copy.wait()
    seg_index = lax.broadcasted_iota(jnp.int32, (SEGS, LANES), 0)
    seg_next = (seg_index + 1).astype(F32) * float(STEPS)
    for m in range(MODES):
        rate = jnp.broadcast_to(decay_rates[pl.ds(m, 1), :], (SEGS, LANES))
        decay_b[m] = jnp.exp(-rate)
        res_b[m] = jnp.broadcast_to(residues[pl.ds(m, 1), :], (SEGS, LANES))
        seg_b[m] = jnp.exp(-rate * seg_next)
        for k in range(3):
            scan_b[k, m] = jnp.where(seg_index >= (1 << k), jnp.exp(-rate * float(STEPS << k)), 0.0)

    carry[...] = jnp.zeros((MODES, LANES), F32)
    start[...] = jnp.zeros((MODES, LANES), F32)
    span[...] = jnp.exp(-decay_rates[...] * float(ROWS))

    @pl.when(tp >= SPLIT)
    def _():
        o_y[1] = jnp.zeros((2, 2, QUARTER, FEATURES), BF16)

    upper, lower = pl.ds(0, HALF), pl.ds(HALF, HALF)
    near = x * 2 + 1 - y_lo
    code = jnp.int32(ORDERS[0])
    for t in range(1, 8):
        code = jnp.where(tp == t, jnp.int32(ORDERS[t]), code)

    def order(i):
        return lax.shift_right_logical(code, 3 * i) & 7

    def column_chunk(dx, row):
        return lax.rem(x + dx, 4) * 2 + row

    def relay_tokens(row, far):
        after, before = column_chunk(1, row), column_chunk(3, row)
        for chunk in (after, before):
            wait_bytes(tok.at[chunk], tok_sem.at[chunk])
        remote(
            tok.at[before, upper], tok.at[before, upper], send_sem.at[0], far_sem.at[far, 0], x_next
        ).start()
        remote(tok.at[after, lower], tok.at[after, lower], send_sem.at[0], far_sem.at[far, 1], x_prev).start()

    def multiply(jc, r):
        zi = lax.rem(z + r, 4)

        part[jc, r] = jnp.dot(tok[jc], w_in[zi], preferred_element_type=F32).astype(BF16)

    first, second = pl.ds(0, QKV), pl.ds(QKV, QKV)

    def await_tokens(jc):
        for far, row in ((0, y_lo), (1, 1 - y_lo)):

            @pl.when(jc == column_chunk(2, row))
            def _():
                wait_bytes(tok.at[jc, upper], far_sem.at[far, 0])
                wait_bytes(tok.at[jc, lower], far_sem.at[far, 1])

    def project(i):
        jc = order(i)
        await_tokens(jc)

        for r in (2, 1, 3, 0):

            @pl.when(i == 0)
            def _():
                wait_bytes(w_in.at[0, other_feat, :], w_sem.at[r])

            multiply(jc, r)
            if r == 2:
                remote(part.at[jc, 2, :, first], relay.at[0, jc], send_sem.at[2], relay_sem.at[0, jc], z_next).start()
                remote(part.at[jc, 2, :, second], relay.at[1, jc], send_sem.at[2], relay_sem.at[1, jc], z_prev).start()
            elif r == 1:
                remote(part.at[jc, 1, :, second], direct.at[1, jc], send_sem.at[3], direct_sem.at[1, jc], z_next).start()
            elif r == 3:
                remote(part.at[jc, 3, :, first], direct.at[0, jc], send_sem.at[3], direct_sem.at[0, jc], z_prev).start()

    def project_late(u):
        jc = order(EARLY + u)
        await_tokens(jc)
        theirs = pl.ds(aligned(1 - y_hi, QKV), QKV)
        for r in (2, 1, 3, 0):
            multiply(jc, r)
            remote(part.at[jc, r, :, theirs], crossed.at[u, r], send_sem.at[9], crossed_sem.at[u], y_far).start()

    def start_late(u):
        jc = order(EARLY + u)
        mine = pl.ds(aligned(y_hi, QKV), QKV)
        wait_bytes(crossed.at[u], crossed_sem.at[u])
        for r in (2, 1, 3, 0):
            crossed[u, r] = (crossed[u, r].astype(F32) + part[jc, r, :, mine].astype(F32)).astype(BF16)
            if r == 2:
                for k, rows, peer in ((0, upper, z_next), (1, lower, z_prev)):
                    remote(
                        crossed.at[u, 2, rows], relay_l.at[u, k], send_sem.at[10], relay_l_sem.at[u, k], peer
                    ).start()
            elif r == 1:
                remote(
                    crossed.at[u, 1, lower], direct_l.at[u, 1], send_sem.at[10], direct_l_sem.at[u, 1], z_next
                ).start()
            elif r == 3:
                remote(
                    crossed.at[u, 3, upper], direct_l.at[u, 0], send_sem.at[10], direct_l_sem.at[u, 0], z_prev
                ).start()

    def pass_late(u):
        for k, r, rows, peer in ((0, 1, upper, z_next), (1, 3, lower, z_prev)):
            wait_bytes(relay_l.at[u, k], relay_l_sem.at[u, k])
            relay_l[u, k] = (relay_l[u, k].astype(F32) + crossed[u, r, rows].astype(F32)).astype(BF16)
            remote(relay_l.at[u, k], summed_l.at[u, k], send_sem.at[10], summed_l_sem.at[u, k], peer).start()

    def pass_on(jc):
        for k, r, cols, peer in ((0, 1, first, z_next), (1, 3, second, z_prev)):
            wait_bytes(relay.at[k, jc], relay_sem.at[k, jc])
            relay[k, jc] = (relay[k, jc].astype(F32) + part[jc, r, :, cols].astype(F32)).astype(BF16)
            remote(relay.at[k, jc], summed.at[k, jc], send_sem.at[4], summed_sem.at[k, jc], peer).start()

    def gather_half(jc, k):
        cols = pl.ds(aligned(k, QKV), QKV)
        return part[jc, 0, :, cols].astype(F32) + direct[k, jc].astype(F32) + summed[k, jc].astype(F32)

    def cross(jc):
        for k in range(2):
            wait_bytes(direct.at[k, jc], direct_sem.at[k, jc])
            wait_bytes(summed.at[k, jc], summed_sem.at[k, jc])
        y_send[jc] = gather_half(jc, 1 - y_hi).astype(BF16)
        remote(y_send.at[jc], y_recv.at[jc], send_sem.at[5], y_sem.at[jc], y_far).start()

    def convolve(j):
        def keep(rows, total):
            q_scr[rows, :] = total[:, :LANES]
            s_scr[rows, :] = total[:, LANES : 2 * LANES] * total[:, 2 * LANES :]

        late = jnp.int32(-1)
        for u in range(LATE):
            late = jnp.where(order(EARLY + u) == j, u, late)

        @pl.when(late < 0)
        def _():
            wait_bytes(y_recv.at[j], y_sem.at[j])
            keep(pl.ds(0, ROWS), gather_half(j, y_hi) + y_recv[j].astype(F32))

        @pl.when(late >= 0)
        def _():
            for k, rows in ((0, upper), (1, lower)):
                wait_bytes(direct_l.at[late, k], direct_l_sem.at[late, k])
                wait_bytes(summed_l.at[late, k], summed_l_sem.at[late, k])
                keep(
                    rows,
                    crossed[late, 0, rows].astype(F32)
                    + direct_l[late, k].astype(F32)
                    + summed_l[late, k].astype(F32),
                )

        decay = [decay_b[m] for m in range(MODES)]
        held = [jnp.zeros((SEGS, LANES), F32)] * MODES
        for i in range(STEPS):
            now = s_scr[pl.ds(i, SEGS, stride=STEPS), :]
            held = [decay[m] * held[m] + now for m in range(MODES)]
        for m in range(MODES):
            total = held[m]
            for k in range(3):
                total = total + scan_b[k, m] * pltpu.roll(total, 1 << k, 0)
            ends[m] = total
            state_out[j, pl.ds(m, 1), :] = total[SEGS - 1 :, :]

        @pl.when(jnp.logical_or(core == 0, j < CHUNKS - 1))
        def _():
            remote(state_out.at[j], state_in.at[j], send_sem.at[6], state_sem.at[j], sibling).start()

        @pl.when(core == 1)
        def _():
            wait_bytes(state_in.at[j], state_sem.at[j])
            before = span[...] * carry[...] + state_in[j]
            start[...] = before
            carry[...] = span[...] * before + state_out[j]

        @pl.when(jnp.logical_and(core == 0, j > 0))
        def _():
            wait_bytes(state_in.at[j - 1], state_sem.at[j - 1])
            before = span[...] * (span[...] * carry[...] + state_out[j - 1]) + state_in[j - 1]
            start[...] = before
            carry[...] = before

        for m in range(MODES):
            before = jnp.broadcast_to(start[pl.ds(m, 1), :], (SEGS, LANES))
            full = ends[m] + seg_b[m] * before
            ends[m] = jnp.where(seg_index == 0, before, pltpu.roll(full, 1, 0))

        held = [ends[m] for m in range(MODES)]
        for i in range(STEPS):
            now = s_scr[pl.ds(i, SEGS, stride=STEPS), :]
            held = [decay_b[m] * held[m] + now for m in range(MODES)]
            terms = [res_b[m] * held[m] for m in range(MODES)]
            while len(terms) > 1:
                terms = [terms[k] + terms[k + 1] for k in range(0, len(terms), 2)]
            y_scr[pl.ds(i, SEGS, stride=STEPS), :] = terms[0]
        gain = skip_gain[...]
        gath[j, :, lanes] = (q_scr[...] * (y_scr[...] + gain * s_scr[...])).astype(BF16)
        own = gath.at[j, :, lanes]
        @pl.when(j >= DIRECT)
        def _():
            for peer in diagonals:
                remote(own, own, send_sem.at[7], gath_sem.at[block, j], peer).start()

        for peer in (z_far, z_next, z_prev, y_far):
            remote(own, own, send_sem.at[7], gath_sem.at[block, j], peer).start()

    def forward(j):
        for r in (1, 3, 2):
            b = y_hi * 4 + lax.rem(z + r, 4)
            there = gath.at[j, :, pl.ds(aligned(b, LANES), LANES)]
            wait_bytes(there, gath_sem.at[b, j])
            remote(there, there, send_sem.at[7], gath_sem.at[b, j], y_far).start()

    def distance(j):
        return lax.rem(j // 2 - x + 4, 4)

    def finish(j):
        for r in range(4):
            b = (1 - y_hi) * 4 + r
            wait_bytes(gath.at[j, :, pl.ds(aligned(b, LANES), LANES)], gath_sem.at[b, j])

        @pl.when(j >= DIRECT)
        def _():
            for r in (1, 3, 2):
                b = y_hi * 4 + lax.rem(z + r, 4)
                wait_bytes(gath.at[j, :, pl.ds(aligned(b, LANES), LANES)], gath_sem.at[b, j])

        @pl.when(j == 0)
        def _():
            pltpu.make_async_copy(out_weight, w_out.at[core], local_sem.at[5]).wait()
            wait_bytes(w_out.at[1 - core], wo_sem.at[0])

        for h in range(2):
            cols = pl.ds(h * FEATURES, FEATURES)
            p_out[j, :, cols] = jnp.dot(gath[j], w_out[h], preferred_element_type=F32).astype(BF16)
        o_begin(j, 0)

        @pl.when(j < SPLIT)
        def _():
            o_begin(j, 1)

        @pl.when(jnp.logical_and(j >= SPLIT, row_of(j) != y_lo))
        def _():
            remote(p_out.at[j, lower], o_y_in.at[j], send_sem.at[8], o_y_in_sem.at[j], y_near).start()

    def row_of(j):
        return lax.rem(j, 2)

    def quarter(part_index, k):
        return pl.ds(part_index * HALF + k * QUARTER, QUARTER)

    def own_columns(flip):
        return pl.ds(aligned(1 - core if flip else core, FEATURES), FEATURES)

    def to_column(src, j, s, kind, k, dx):
        for flip in (False, True):
            remote(
                src.at[:, own_columns(flip)],
                o_in.at[row_of(j), s, kind, k, core],
                send_sem.at[8],
                o_in_sem.at[row_of(j), s],
                at(dx=dx, flip_core=flip),
            ).start()

    def o_begin(j, s):
        dx = distance(j)

        @pl.when(dx == 2)
        def _():
            for k, peer in ((0, x_next), (1, x_prev)):
                remote(
                    p_out.at[j, quarter(s, k)], o_relay.at[s, j], send_sem.at[8], o_relay_sem.at[s, j], peer
                ).start()

        @pl.when(dx == 1)
        def _():
            to_column(p_out.at[j, quarter(s, 1)], j, s, 0, 1, 1)

        @pl.when(dx == 3)
        def _():
            to_column(p_out.at[j, quarter(s, 0)], j, s, 0, 0, 3)

        @pl.when(dx == 0)
        def _():
            rows = pl.ds(s * HALF, HALF)
            remote(
                p_out.at[j, rows, own_columns(True)],
                o_sib.at[row_of(j), s],
                send_sem.at[8],
                o_sib_sem.at[row_of(j), s],
                sibling,
            ).start()

    def o_pass(j, s):
        dx = distance(j)
        for want, k in ((1, 0), (3, 1)):

            @pl.when(dx == want)
            def _():
                wait_bytes(o_relay.at[s, j], o_relay_sem.at[s, j])
                o_relay[s, j] = (o_relay[s, j].astype(F32) + p_out[j, quarter(s, k), :].astype(F32)).astype(BF16)
                to_column(o_relay.at[s, j], j, s, 1, k, want)

    def o_total(j, s, k, mine):
        side = row_of(j)
        source = core if mine else 1 - core
        if mine:
            base = p_out[j, quarter(s, k), own_columns(False)]
        else:
            base = o_sib[side, s, pl.ds(k * QUARTER, QUARTER), :]
        return (
            base.astype(F32) + o_in[side, s, 0, k, source].astype(F32) + o_in[side, s, 1, k, source].astype(F32)
        )

    def o_arrived(j, s):
        wait_bytes(o_in.at[row_of(j), s], o_in_sem.at[row_of(j), s])
        wait_bytes(o_sib.at[row_of(j), s], o_sib_sem.at[row_of(j), s])

    def o_second_x(j):
        o_pass(j, 0)

        @pl.when(j < SPLIT)
        def _():
            o_pass(j, 1)

    def o_second_y(j):
        @pl.when(jnp.logical_and(j >= SPLIT, row_of(j) == y_lo))
        def _():
            wait_bytes(o_y_in.at[j], o_y_in_sem.at[j])
            p_out[j, lower, :] = (p_out[j, lower, :].astype(F32) + o_y_in[j].astype(F32)).astype(BF16)
            o_begin(j, 1)

    def o_over(j, s):
        o_arrived(j, s)
        for k in range(2):
            for mine in (True, False):
                o_send[s, core if mine else 1 - core, k] = o_total(j, s, k, mine).astype(BF16)
        remote(o_send.at[s], o_y.at[s], send_sem.at[8], o_y_sem.at[s], y_near).start()

    def o_third_x(j):
        @pl.when(jnp.logical_and(j >= SPLIT, row_of(j) == y_lo))
        def _():
            o_pass(j, 1)

    def o_third_y(j):
        @pl.when(jnp.logical_and(distance(j) == 0, row_of(j) != y_lo))
        def _():
            o_over(j, 0)

            @pl.when(j < SPLIT)
            def _():
                o_over(j, 1)

    def o_last(j):
        @pl.when(j == tp)
        def _():
            for s in (1, 0):
                o_arrived(j, s)
                if s == 0:
                    wait_bytes(o_y.at[0], o_y_sem.at[0])
                else:

                    @pl.when(j < SPLIT)
                    def _():
                        wait_bytes(o_y.at[1], o_y_sem.at[1])

                for k in range(2):
                    for mine in (True, False):
                        source = core if mine else 1 - core
                        total = o_total(j, s, k, mine) + o_y[s, source, k].astype(F32)
                        start = source * ROWS + s * HALF + k * QUARTER
                        out[pl.ds(pl.multiple_of(start, QUARTER), QUARTER), :] = total.astype(BF16)

    def step(n, carry):
        def stage(times, body):
            first_chunk, end_chunk = jnp.int32(0), jnp.int32(0)
            for time in times:
                first_chunk = first_chunk + jnp.where(n > time, 1, 0)
                end_chunk = end_chunk + jnp.where(n >= time, 1, 0)

            def call(j, unused):
                body(j)
                return unused

            lax.fori_loop(first_chunk, end_chunk, call, 0)

        @pl.when(n == 2)
        def _():
            wait_bytes(tok.at[near], tok_sem.at[near])
            relay_tokens(y_lo, 0)
            for peer in (x_next, x_prev):
                remote(tok.at[near], tok.at[near], send_sem.at[0], tok_sem.at[near], peer).start()

        @pl.when(n == 6)
        def _():
            relay_tokens(1 - y_lo, 1)

        stage(range(0, 2 * EARLY, 2), project)
        stage(START_LATE_AT, start_late)
        stage(range(1, 2 * EARLY, 2), lambda k: pass_on(order(k)))
        stage(range(3, 2 * EARLY + 2, 2), lambda k: cross(order(k)))
        stage([t + 1 for t in START_LATE_AT], pass_late)
        stage(PROJECT_LATE_AT, project_late)
        stage(CONVOLVE_AT, convolve)
        stage(FORWARD_AT, forward)
        stage(FINISH_AT, finish)
        stage([t + 1 for t in FINISH_AT], o_second_x)
        stage([t + 1 for t in FINISH_AT], o_second_y)
        stage([t + 2 for t in FINISH_AT], o_third_x)
        stage([t + 2 for t in FINISH_AT], o_third_y)
        stage([t + 3 for t in FINISH_AT], o_last)
        return carry

    lax.fori_loop(0, FINISH_AT[-1] + 4, step, 0)

    wait_bytes(tok.at[pl.ds(0, 7)], send_sem.at[0])
    wait_bytes(tok.at[0, :, pl.ds(0, FEATURES)], send_sem.at[0])
    wait_bytes(w_in.at[:, own_feat, :], send_sem.at[1])
    wait_bytes(out_weight, send_sem.at[1])
    early = pl.ds(0, EARLY)
    wait_bytes(relay.at[:, early], send_sem.at[2])
    wait_bytes(direct.at[:, early], send_sem.at[3])
    wait_bytes(summed.at[:, early], send_sem.at[4])
    wait_bytes(y_recv.at[early], send_sem.at[5])
    wait_bytes(crossed, send_sem.at[9])
    for arrived in (relay_l, direct_l, summed_l):
        wait_bytes(arrived, send_sem.at[10])
    wait_bytes(state_out.at[pl.ds(0, CHUNKS - 1)], send_sem.at[6])

    @pl.when(core == 0)
    def _():
        wait_bytes(state_out.at[0], send_sem.at[6])

    wait_bytes(gath.at[pl.ds(0, 7)], send_sem.at[7])
    wait_bytes(p_out.at[pl.ds(0, 7)], send_sem.at[8])
    wait_bytes(p_out.at[0, pl.ds(0, 3 * QUARTER)], send_sem.at[8])

    @pl.when(near < SPLIT)
    def _():
        wait_bytes(p_out.at[0, pl.ds(0, QUARTER)], send_sem.at[8])


def local(tokens, in_weight, residues, decay_rates, skip_gain, out_weight):
    channels = in_weight.shape[2]
    vmem = pl.BlockSpec(memory_space=pltpu.VMEM)
    anywhere = pl.BlockSpec(memory_space=pl.ANY)
    dma = pltpu.SemaphoreType.DMA
    scratch = [
        pltpu.VMEM((MODES, LANES), F32),
        pltpu.VMEM((MODES, LANES), F32),
        pltpu.VMEM((1, LANES), F32),
        pltpu.VMEM((CHUNKS, ROWS, WIDE), BF16),
        pltpu.VMEM((4, WIDE, 2 * QKV), BF16),
        pltpu.VMEM((2, WIDE, FEATURES), BF16),
        pltpu.VMEM((CHUNKS, 4, ROWS, 2 * QKV), BF16),
        pltpu.VMEM((2, CHUNKS, ROWS, QKV), BF16),
        pltpu.VMEM((2, CHUNKS, ROWS, QKV), BF16),
        pltpu.VMEM((2, CHUNKS, ROWS, QKV), BF16),
        pltpu.VMEM((CHUNKS, ROWS, QKV), BF16),
        pltpu.VMEM((CHUNKS, ROWS, QKV), BF16),
        pltpu.VMEM((LATE, 4, ROWS, QKV), BF16),
        pltpu.VMEM((LATE, 2, HALF, QKV), BF16),
        pltpu.VMEM((LATE, 2, HALF, QKV), BF16),
        pltpu.VMEM((LATE, 2, HALF, QKV), BF16),
        pltpu.VMEM((ROWS, LANES), F32),
        pltpu.VMEM((ROWS, LANES), F32),
        pltpu.VMEM((ROWS, LANES), F32),
        pltpu.VMEM((MODES, SEGS, LANES), F32),
        pltpu.VMEM((MODES, SEGS, LANES), F32),
        pltpu.VMEM((MODES, SEGS, LANES), F32),
        pltpu.VMEM((3, MODES, SEGS, LANES), F32),
        pltpu.VMEM((MODES, SEGS, LANES), F32),
        pltpu.VMEM((CHUNKS + 1, MODES, LANES), F32),
        pltpu.VMEM((CHUNKS, MODES, LANES), F32),
        pltpu.VMEM((MODES, LANES), F32),
        pltpu.VMEM((MODES, LANES), F32),
        pltpu.VMEM((MODES, LANES), F32),
        pltpu.VMEM((CHUNKS, ROWS, WIDE), BF16),
        pltpu.VMEM((CHUNKS, ROWS, WIDE), BF16),
        pltpu.VMEM((2, CHUNKS, QUARTER, WIDE), BF16),
        pltpu.VMEM((CHUNKS, HALF, WIDE), BF16),
        pltpu.VMEM((2, 2, 2, 2, 2, QUARTER, FEATURES), BF16),
        pltpu.VMEM((2, 2, HALF, FEATURES), BF16),
        pltpu.VMEM((2, 2, 2, QUARTER, FEATURES), BF16),
        pltpu.VMEM((2, 2, 2, QUARTER, FEATURES), BF16),
        dma((9,)),
        dma((CHUNKS + 1,)),
        dma((2, 2)),
        dma((4,)),
        dma((1,)),
        dma((2, CHUNKS)),
        dma((2, CHUNKS)),
        dma((2, CHUNKS)),
        dma((CHUNKS,)),
        dma((LATE,)),
        dma((LATE, 2)),
        dma((LATE, 2)),
        dma((LATE, 2)),
        dma((CHUNKS + 1,)),
        dma((8, CHUNKS)),
        dma((2, CHUNKS)),
        dma((CHUNKS,)),
        dma((2, 2)),
        dma((2, 2)),
        dma((2,)),
        dma((11,)),
    ]
    return pl.pallas_call(
        kernel,
        out_shape=pltpu.VMEM(tokens.shape, BF16),
        in_specs=[anywhere] * 6,
        out_specs=vmem,
        scratch_shapes=scratch,
        compiler_params=pltpu.CompilerParams(
            collective_id=0, has_side_effects=True, vmem_limit_bytes=56 * 2**20
        ),
        name="hyena_block",
    )(tokens, in_weight.transpose(1, 0, 2), residues, decay_rates, skip_gain.reshape(1, channels), out_weight)


def solution(mesh):
    in_specs = (
        P("tp", "seq"),
        P("seq", None, "tp"),
        P(None, "tp"),
        P(None, "tp"),
        P("tp"),
        P("tp", "seq"),
    )
    return jax.shard_map(local, mesh=mesh, in_specs=in_specs, out_specs=P("tp", "seq"), check_vma=False)
```

```python
import functools

import jax
import jax.numpy as jnp
from jax import lax
from jax.experimental import pallas as pl
from jax.experimental.pallas import tpu as pltpu
from jax.sharding import PartitionSpec as P

MESH = pl.DeviceIdType.MESH
F32 = jnp.float32
BF16 = jnp.bfloat16
CHUNKS = 8
ROWS = 128
HALF = 64
QUARTER = 32
LANES = 128
MODES = 16
SEGS = 8
STEPS = 16
QKV = 3 * LANES
FEATURES = 512
WIDE = 1024
DIRECT = 5
SPLIT = 5
EARLY = 7
LATE = CHUNKS - EARLY
PROJECT_LATE_AT = (8,)
START_LATE_AT = (14,)
CONVOLVE_AT = (12, 12, 13, 14, 14, 16, 16, 16)
FORWARD_AT = (13, 13, 14, 15, 15)
FINISH_AT = (15, 15, 15, 16, 16, 17, 17, 17)
CHUNK_ORDERS = (
    (0, 1, 2, 3, 4, 5, 6, 7),
    (1, 0, 3, 2, 4, 5, 6, 7),
    (2, 3, 0, 1, 4, 5, 6, 7),
    (3, 2, 1, 0, 4, 5, 6, 7),
    (4, 5, 0, 2, 1, 3, 6, 7),
    (5, 4, 1, 2, 0, 3, 6, 7),
    (6, 0, 2, 1, 3, 4, 5, 7),
    (7, 1, 3, 0, 2, 4, 5, 6),
)
ORDERS = tuple(sum(chunk << (3 * k) for k, chunk in enumerate(row)) for row in CHUNK_ORDERS)


def remote(src, dst, send_sem, recv_sem, device):
    return pltpu.make_async_remote_copy(
        src_ref=src,
        dst_ref=dst,
        send_sem=send_sem,
        recv_sem=recv_sem,
        device_id=device,
        device_id_type=MESH,
    )


def wait_bytes(ref, sem):
    pltpu.make_async_copy(ref, ref, sem).wait()


def aligned(value, step):
    return pl.multiple_of(value * step, step)


def kernel(
    tokens,
    in_weight,
    residues_in,
    decay_rates_in,
    skip_gain_in,
    out_weight,
    out,
    residues,
    decay_rates,
    skip_gain,
    tok,
    w_in,
    w_out,
    part,
    relay,
    direct,
    summed,
    y_send,
    y_recv,
    crossed,
    relay_l,
    direct_l,
    summed_l,
    s_scr,
    y_scr,
    q_scr,
    decay_b,
    res_b,
    seg_b,
    scan_b,
    ends,
    state_in,
    state_out,
    carry,
    start,
    span,
    gath,
    p_out,
    o_relay,
    o_y_in,
    o_in,
    o_sib,
    o_send,
    o_y,
    local_sem,
    tok_sem,
    far_sem,
    w_sem,
    wo_sem,
    relay_sem,
    direct_sem,
    summed_sem,
    y_sem,
    crossed_sem,
    relay_l_sem,
    direct_l_sem,
    summed_l_sem,
    state_sem,
    gath_sem,
    o_relay_sem,
    o_y_in_sem,
    o_in_sem,
    o_sib_sem,
    o_y_sem,
    send_sem,
):
    seq = lax.axis_index("seq")
    tp = lax.axis_index("tp")
    core = lax.rem(seq, 2)
    z = lax.rem(seq // 2, 4)
    y_hi = seq // 8
    x = tp // 2
    y_lo = lax.rem(tp, 2)

    def at(dx=0, dz=0, flip_hi=False, flip_lo=False, flip_core=False):
        a = 1 - y_hi if flip_hi else y_hi
        b = lax.rem(z + dz, 4)
        c = 1 - core if flip_core else core
        d = lax.rem(x + dx, 4)
        e = 1 - y_lo if flip_lo else y_lo
        return (a * 8 + b * 2 + c, d * 2 + e)

    sibling = at(flip_core=True)
    z_next, z_prev, z_far = at(dz=1), at(dz=3), at(dz=2)
    y_far = at(flip_hi=True)
    x_next, x_prev = at(dx=1), at(dx=3)
    y_near = at(flip_lo=True)
    diagonals = [at(dz=r, flip_hi=True) for r in (2, 1, 3)]
    peers = [sibling, z_next, z_prev, z_far, y_far, x_next, x_prev, y_near, *diagonals]
    peers += [at(dx=1, flip_core=True), at(dx=3, flip_core=True)]
    block = y_hi * 4 + z
    lanes = pl.ds(aligned(block, LANES), LANES)

    barrier = pltpu.get_barrier_semaphore()
    for peer in peers:
        pl.semaphore_signal(barrier, inc=1, device_id=peer, device_id_type=MESH)

    own_rows = pl.ds(aligned(core, ROWS), ROWS)
    other_rows = pl.ds(aligned(1 - core, ROWS), ROWS)
    own_feat = pl.ds(aligned(core, FEATURES), FEATURES)
    other_feat = pl.ds(aligned(1 - core, FEATURES), FEATURES)
    pltpu.make_async_copy(tokens.at[own_rows, :], tok.at[tp, :, own_feat], local_sem.at[0]).start()

    def own_weight(r):
        return w_in.at[lax.rem(z + r, 4), own_feat, :]

    for r in (2, 1, 3, 0):
        zi = lax.rem(z + r, 4)
        for h in range(2):
            there = pl.ds(aligned(h * 4 + zi, LANES), LANES)
            for k in range(3):
                pltpu.make_async_copy(
                    in_weight.at[k, :, there],
                    w_in.at[zi, own_feat, pl.ds((h * 3 + k) * LANES, LANES)],
                    local_sem.at[1 + r],
                ).start()
    pltpu.make_async_copy(out_weight, w_out.at[core], local_sem.at[5]).start()
    small = [
        pltpu.make_async_copy(whole.at[:, lanes], piece, local_sem.at[6 + k])
        for k, (whole, piece) in enumerate(
            ((residues_in, residues), (decay_rates_in, decay_rates), (skip_gain_in, skip_gain))
        )
    ]
    for copy in small:
        copy.start()

    pl.semaphore_wait(barrier, len(peers))
    remote(tokens.at[other_rows, :], tok.at[tp, :, own_feat], send_sem.at[0], tok_sem.at[CHUNKS], sibling).start()
    wait_bytes(own_weight(2), local_sem.at[3])
    for k in range(2):
        piece = w_in.at[lax.rem(z + 2, 4), own_feat, pl.ds(k * QKV, QKV)]
        remote(piece, piece, send_sem.at[1], w_sem.at[2 + 2 * k], sibling).start()
    wait_bytes(tok.at[0, :, pl.ds(0, FEATURES)], local_sem.at[0])
    wait_bytes(tok.at[0, :, pl.ds(0, FEATURES)], tok_sem.at[CHUNKS])
    for peer in (y_near, x_next, x_prev):
        remote(tok.at[tp], tok.at[tp], send_sem.at[0], tok_sem.at[tp], peer).start()
    for r in (1, 3, 0):
        wait_bytes(own_weight(r), local_sem.at[1 + r])
        remote(own_weight(r), own_weight(r), send_sem.at[1], w_sem.at[r], sibling).start()
    remote(out_weight, w_out.at[core], send_sem.at[1], wo_sem.at[0], sibling).start()

    for copy in small:
        copy.wait()
    seg_index = lax.broadcasted_iota(jnp.int32, (SEGS, LANES), 0)
    seg_next = (seg_index + 1).astype(F32) * float(STEPS)
    for m in range(MODES):
        rate = jnp.broadcast_to(decay_rates[pl.ds(m, 1), :], (SEGS, LANES))
        decay_b[m] = jnp.exp(-rate)
        res_b[m] = jnp.broadcast_to(residues[pl.ds(m, 1), :], (SEGS, LANES))
        seg_b[m] = jnp.exp(-rate * seg_next)
        for k in range(3):
            scan_b[k, m] = jnp.where(seg_index >= (1 << k), jnp.exp(-rate * float(STEPS << k)), 0.0)

    carry[...] = jnp.zeros((MODES, LANES), F32)
    start[...] = jnp.zeros((MODES, LANES), F32)
    span[...] = jnp.exp(-decay_rates[...] * float(ROWS))

    @pl.when(tp >= SPLIT)
    def _():
        o_y[1] = jnp.zeros((2, 2, QUARTER, FEATURES), BF16)

    upper, lower = pl.ds(0, HALF), pl.ds(HALF, HALF)
    near = x * 2 + 1 - y_lo
    code = jnp.int32(ORDERS[0])
    for t in range(1, 8):
        code = jnp.where(tp == t, jnp.int32(ORDERS[t]), code)

    def order(i):
        return lax.shift_right_logical(code, 3 * i) & 7

    def column_chunk(dx, row):
        return lax.rem(x + dx, 4) * 2 + row

    def relay_tokens(row, far):
        after, before = column_chunk(1, row), column_chunk(3, row)
        for chunk in (after, before):
            wait_bytes(tok.at[chunk], tok_sem.at[chunk])
        remote(
            tok.at[before, upper], tok.at[before, upper], send_sem.at[0], far_sem.at[far, 0], x_next
        ).start()
        remote(tok.at[after, lower], tok.at[after, lower], send_sem.at[0], far_sem.at[far, 1], x_prev).start()

    def multiply(jc, r, cols=pl.ds(0, 2 * QKV)):
        zi = lax.rem(z + r, 4)
        part[jc, r, :, cols] = jnp.dot(tok[jc], w_in[zi, :, cols], preferred_element_type=F32).astype(BF16)

    first, second = pl.ds(0, QKV), pl.ds(QKV, QKV)

    def await_tokens(jc):
        for far, row in ((0, y_lo), (1, 1 - y_lo)):

            @pl.when(jc == column_chunk(2, row))
            def _():
                wait_bytes(tok.at[jc, upper], far_sem.at[far, 0])
                wait_bytes(tok.at[jc, lower], far_sem.at[far, 1])

    def project(i):
        jc = order(i)
        await_tokens(jc)

        for k, cols, peer in ((0, first, z_next), (1, second, z_prev)):

            @pl.when(i == 0)
            def _():
                wait_bytes(w_in.at[0, other_feat, cols], w_sem.at[2 + 2 * k])

            multiply(jc, 2, cols)
            remote(part.at[jc, 2, :, cols], relay.at[k, jc], send_sem.at[2], relay_sem.at[k, jc], peer).start()

        for r in (1, 3, 0):

            @pl.when(i == 0)
            def _():
                wait_bytes(w_in.at[0, other_feat, :], w_sem.at[r])

            multiply(jc, r)
            if r == 1:
                remote(part.at[jc, 1, :, second], direct.at[1, jc], send_sem.at[3], direct_sem.at[1, jc], z_next).start()
            elif r == 3:
                remote(part.at[jc, 3, :, first], direct.at[0, jc], send_sem.at[3], direct_sem.at[0, jc], z_prev).start()

    def project_late(u):
        jc = order(EARLY + u)
        await_tokens(jc)
        theirs = pl.ds(aligned(1 - y_hi, QKV), QKV)
        for r in (2, 1, 3, 0):
            multiply(jc, r)
            remote(part.at[jc, r, :, theirs], crossed.at[u, r], send_sem.at[9], crossed_sem.at[u], y_far).start()

    def start_late(u):
        jc = order(EARLY + u)
        mine = pl.ds(aligned(y_hi, QKV), QKV)
        wait_bytes(crossed.at[u], crossed_sem.at[u])
        for r in (2, 1, 3, 0):
            crossed[u, r] = (crossed[u, r].astype(F32) + part[jc, r, :, mine].astype(F32)).astype(BF16)
            if r == 2:
                for k, rows, peer in ((0, upper, z_next), (1, lower, z_prev)):
                    remote(
                        crossed.at[u, 2, rows], relay_l.at[u, k], send_sem.at[10], relay_l_sem.at[u, k], peer
                    ).start()
            elif r == 1:
                remote(
                    crossed.at[u, 1, lower], direct_l.at[u, 1], send_sem.at[10], direct_l_sem.at[u, 1], z_next
                ).start()
            elif r == 3:
                remote(
                    crossed.at[u, 3, upper], direct_l.at[u, 0], send_sem.at[10], direct_l_sem.at[u, 0], z_prev
                ).start()

    def pass_late(u):
        for k, r, rows, peer in ((0, 1, upper, z_next), (1, 3, lower, z_prev)):
            wait_bytes(relay_l.at[u, k], relay_l_sem.at[u, k])
            relay_l[u, k] = (relay_l[u, k].astype(F32) + crossed[u, r, rows].astype(F32)).astype(BF16)
            remote(relay_l.at[u, k], summed_l.at[u, k], send_sem.at[10], summed_l_sem.at[u, k], peer).start()

    def pass_on(jc):
        for k, r, cols, peer in ((0, 1, first, z_next), (1, 3, second, z_prev)):
            wait_bytes(relay.at[k, jc], relay_sem.at[k, jc])
            relay[k, jc] = (relay[k, jc].astype(F32) + part[jc, r, :, cols].astype(F32)).astype(BF16)
            remote(relay.at[k, jc], summed.at[k, jc], send_sem.at[4], summed_sem.at[k, jc], peer).start()

    def gather_half(jc, k):
        cols = pl.ds(aligned(k, QKV), QKV)
        return part[jc, 0, :, cols].astype(F32) + direct[k, jc].astype(F32) + summed[k, jc].astype(F32)

    def cross(jc):
        for k in range(2):
            wait_bytes(direct.at[k, jc], direct_sem.at[k, jc])
            wait_bytes(summed.at[k, jc], summed_sem.at[k, jc])
        y_send[jc] = gather_half(jc, 1 - y_hi).astype(BF16)
        remote(y_send.at[jc], y_recv.at[jc], send_sem.at[5], y_sem.at[jc], y_far).start()

    def convolve(j):
        def keep(rows, total):
            q_scr[rows, :] = total[:, :LANES]
            s_scr[rows, :] = total[:, LANES : 2 * LANES] * total[:, 2 * LANES :]

        late = jnp.int32(-1)
        for u in range(LATE):
            late = jnp.where(order(EARLY + u) == j, u, late)

        @pl.when(late < 0)
        def _():
            wait_bytes(y_recv.at[j], y_sem.at[j])
            keep(pl.ds(0, ROWS), gather_half(j, y_hi) + y_recv[j].astype(F32))

        @pl.when(late >= 0)
        def _():
            for k, rows in ((0, upper), (1, lower)):
                wait_bytes(direct_l.at[late, k], direct_l_sem.at[late, k])
                wait_bytes(summed_l.at[late, k], summed_l_sem.at[late, k])
                keep(
                    rows,
                    crossed[late, 0, rows].astype(F32)
                    + direct_l[late, k].astype(F32)
                    + summed_l[late, k].astype(F32),
                )

        decay = [decay_b[m] for m in range(MODES)]
        held = [jnp.zeros((SEGS, LANES), F32)] * MODES
        for i in range(STEPS):
            now = s_scr[pl.ds(i, SEGS, stride=STEPS), :]
            held = [decay[m] * held[m] + now for m in range(MODES)]
        for m in range(MODES):
            total = held[m]
            for k in range(3):
                total = total + scan_b[k, m] * pltpu.roll(total, 1 << k, 0)
            ends[m] = total
            state_out[j, pl.ds(m, 1), :] = total[SEGS - 1 :, :]

        @pl.when(jnp.logical_or(core == 0, j < CHUNKS - 1))
        def _():
            remote(state_out.at[j], state_in.at[j], send_sem.at[6], state_sem.at[j], sibling).start()

        @pl.when(core == 1)
        def _():
            wait_bytes(state_in.at[j], state_sem.at[j])
            before = span[...] * carry[...] + state_in[j]
            start[...] = before
            carry[...] = span[...] * before + state_out[j]

        @pl.when(jnp.logical_and(core == 0, j > 0))
        def _():
            wait_bytes(state_in.at[j - 1], state_sem.at[j - 1])
            before = span[...] * (span[...] * carry[...] + state_out[j - 1]) + state_in[j - 1]
            start[...] = before
            carry[...] = before

        for m in range(MODES):
            before = jnp.broadcast_to(start[pl.ds(m, 1), :], (SEGS, LANES))
            full = ends[m] + seg_b[m] * before
            ends[m] = jnp.where(seg_index == 0, before, pltpu.roll(full, 1, 0))

        held = [ends[m] for m in range(MODES)]
        for i in range(STEPS):
            now = s_scr[pl.ds(i, SEGS, stride=STEPS), :]
            held = [decay_b[m] * held[m] + now for m in range(MODES)]
            terms = [res_b[m] * held[m] for m in range(MODES)]
            while len(terms) > 1:
                terms = [terms[k] + terms[k + 1] for k in range(0, len(terms), 2)]
            y_scr[pl.ds(i, SEGS, stride=STEPS), :] = terms[0]
        gain = skip_gain[...]
        gath[j, :, lanes] = (q_scr[...] * (y_scr[...] + gain * s_scr[...])).astype(BF16)
        own = gath.at[j, :, lanes]
        @pl.when(j >= DIRECT)
        def _():
            for peer in diagonals:
                remote(own, own, send_sem.at[7], gath_sem.at[block, j], peer).start()

        for peer in (z_far, z_next, z_prev, y_far):
            remote(own, own, send_sem.at[7], gath_sem.at[block, j], peer).start()

    def forward(j):
        for r in (1, 3, 2):
            b = y_hi * 4 + lax.rem(z + r, 4)
            there = gath.at[j, :, pl.ds(aligned(b, LANES), LANES)]
            wait_bytes(there, gath_sem.at[b, j])
            remote(there, there, send_sem.at[7], gath_sem.at[b, j], y_far).start()

    def distance(j):
        return lax.rem(j // 2 - x + 4, 4)

    def finish(j):
        for r in range(4):
            b = (1 - y_hi) * 4 + r
            wait_bytes(gath.at[j, :, pl.ds(aligned(b, LANES), LANES)], gath_sem.at[b, j])

        @pl.when(j >= DIRECT)
        def _():
            for r in (1, 3, 2):
                b = y_hi * 4 + lax.rem(z + r, 4)
                wait_bytes(gath.at[j, :, pl.ds(aligned(b, LANES), LANES)], gath_sem.at[b, j])

        @pl.when(j == 0)
        def _():
            pltpu.make_async_copy(out_weight, w_out.at[core], local_sem.at[5]).wait()
            wait_bytes(w_out.at[1 - core], wo_sem.at[0])

        for h in range(2):
            cols = pl.ds(h * FEATURES, FEATURES)
            p_out[j, :, cols] = jnp.dot(gath[j], w_out[h], preferred_element_type=F32).astype(BF16)
        o_begin(j, 0)

        @pl.when(j < SPLIT)
        def _():
            o_begin(j, 1)

        @pl.when(jnp.logical_and(j >= SPLIT, row_of(j) != y_lo))
        def _():
            remote(p_out.at[j, lower], o_y_in.at[j], send_sem.at[8], o_y_in_sem.at[j], y_near).start()

    def row_of(j):
        return lax.rem(j, 2)

    def quarter(part_index, k):
        return pl.ds(part_index * HALF + k * QUARTER, QUARTER)

    def own_columns(flip):
        return pl.ds(aligned(1 - core if flip else core, FEATURES), FEATURES)

    def to_column(src, j, s, kind, k, dx):
        for flip in (False, True):
            remote(
                src.at[:, own_columns(flip)],
                o_in.at[row_of(j), s, kind, k, core],
                send_sem.at[8],
                o_in_sem.at[row_of(j), s],
                at(dx=dx, flip_core=flip),
            ).start()

    def o_begin(j, s):
        dx = distance(j)

        @pl.when(dx == 2)
        def _():
            for k, peer in ((0, x_next), (1, x_prev)):
                remote(
                    p_out.at[j, quarter(s, k)], o_relay.at[s, j], send_sem.at[8], o_relay_sem.at[s, j], peer
                ).start()

        @pl.when(dx == 1)
        def _():
            to_column(p_out.at[j, quarter(s, 1)], j, s, 0, 1, 1)

        @pl.when(dx == 3)
        def _():
            to_column(p_out.at[j, quarter(s, 0)], j, s, 0, 0, 3)

        @pl.when(dx == 0)
        def _():
            rows = pl.ds(s * HALF, HALF)
            remote(
                p_out.at[j, rows, own_columns(True)],
                o_sib.at[row_of(j), s],
                send_sem.at[8],
                o_sib_sem.at[row_of(j), s],
                sibling,
            ).start()

    def o_pass(j, s):
        dx = distance(j)
        for want, k in ((1, 0), (3, 1)):

            @pl.when(dx == want)
            def _():
                wait_bytes(o_relay.at[s, j], o_relay_sem.at[s, j])
                o_relay[s, j] = (o_relay[s, j].astype(F32) + p_out[j, quarter(s, k), :].astype(F32)).astype(BF16)
                to_column(o_relay.at[s, j], j, s, 1, k, want)

    def o_total(j, s, k, mine):
        side = row_of(j)
        source = core if mine else 1 - core
        if mine:
            base = p_out[j, quarter(s, k), own_columns(False)]
        else:
            base = o_sib[side, s, pl.ds(k * QUARTER, QUARTER), :]
        return (
            base.astype(F32) + o_in[side, s, 0, k, source].astype(F32) + o_in[side, s, 1, k, source].astype(F32)
        )

    def o_arrived(j, s):
        wait_bytes(o_in.at[row_of(j), s], o_in_sem.at[row_of(j), s])
        wait_bytes(o_sib.at[row_of(j), s], o_sib_sem.at[row_of(j), s])

    def o_second_x(j):
        o_pass(j, 0)

        @pl.when(j < SPLIT)
        def _():
            o_pass(j, 1)

    def o_second_y(j):
        @pl.when(jnp.logical_and(j >= SPLIT, row_of(j) == y_lo))
        def _():
            wait_bytes(o_y_in.at[j], o_y_in_sem.at[j])
            p_out[j, lower, :] = (p_out[j, lower, :].astype(F32) + o_y_in[j].astype(F32)).astype(BF16)
            o_begin(j, 1)

    def o_over(j, s):
        o_arrived(j, s)
        for k in range(2):
            for mine in (True, False):
                o_send[s, core if mine else 1 - core, k] = o_total(j, s, k, mine).astype(BF16)
        remote(o_send.at[s], o_y.at[s], send_sem.at[8], o_y_sem.at[s], y_near).start()

    def o_third_x(j):
        @pl.when(jnp.logical_and(j >= SPLIT, row_of(j) == y_lo))
        def _():
            o_pass(j, 1)

    def o_third_y(j):
        @pl.when(jnp.logical_and(distance(j) == 0, row_of(j) != y_lo))
        def _():
            o_over(j, 0)

            @pl.when(j < SPLIT)
            def _():
                o_over(j, 1)

    def o_last(j):
        @pl.when(j == tp)
        def _():
            for s in (1, 0):
                o_arrived(j, s)
                if s == 0:
                    wait_bytes(o_y.at[0], o_y_sem.at[0])
                else:

                    @pl.when(j < SPLIT)
                    def _():
                        wait_bytes(o_y.at[1], o_y_sem.at[1])

                for k in range(2):
                    for mine in (True, False):
                        source = core if mine else 1 - core
                        total = o_total(j, s, k, mine) + o_y[s, source, k].astype(F32)
                        start = source * ROWS + s * HALF + k * QUARTER
                        out[pl.ds(pl.multiple_of(start, QUARTER), QUARTER), :] = total.astype(BF16)

    def step(n, carry):
        def stage(times, body):
            first_chunk, end_chunk = jnp.int32(0), jnp.int32(0)
            for time in times:
                first_chunk = first_chunk + jnp.where(n > time, 1, 0)
                end_chunk = end_chunk + jnp.where(n >= time, 1, 0)

            def call(j, unused):
                body(j)
                return unused

            lax.fori_loop(first_chunk, end_chunk, call, 0)

        @pl.when(n == 2)
        def _():
            wait_bytes(tok.at[near], tok_sem.at[near])
            relay_tokens(y_lo, 0)
            for peer in (x_next, x_prev):
                remote(tok.at[near], tok.at[near], send_sem.at[0], tok_sem.at[near], peer).start()

        @pl.when(n == 6)
        def _():
            relay_tokens(1 - y_lo, 1)

        stage(range(0, 2 * EARLY, 2), project)
        stage(START_LATE_AT, start_late)
        stage(range(1, 2 * EARLY, 2), lambda k: pass_on(order(k)))
        stage(range(3, 2 * EARLY + 2, 2), lambda k: cross(order(k)))
        stage([t + 1 for t in START_LATE_AT], pass_late)
        stage(PROJECT_LATE_AT, project_late)
        stage(CONVOLVE_AT, convolve)
        stage(FORWARD_AT, forward)
        stage(FINISH_AT, finish)
        stage([t + 1 for t in FINISH_AT], o_second_x)
        stage([t + 1 for t in FINISH_AT], o_second_y)
        stage([t + 2 for t in FINISH_AT], o_third_x)
        stage([t + 2 for t in FINISH_AT], o_third_y)
        stage([t + 3 for t in FINISH_AT], o_last)
        return carry

    lax.fori_loop(0, FINISH_AT[-1] + 4, step, 0)

    wait_bytes(tok.at[pl.ds(0, 7)], send_sem.at[0])
    wait_bytes(tok.at[0, :, pl.ds(0, FEATURES)], send_sem.at[0])
    wait_bytes(w_in.at[:, own_feat, :], send_sem.at[1])
    wait_bytes(out_weight, send_sem.at[1])
    early = pl.ds(0, EARLY)
    wait_bytes(relay.at[:, early], send_sem.at[2])
    wait_bytes(direct.at[:, early], send_sem.at[3])
    wait_bytes(summed.at[:, early], send_sem.at[4])
    wait_bytes(y_recv.at[early], send_sem.at[5])
    wait_bytes(crossed, send_sem.at[9])
    for arrived in (relay_l, direct_l, summed_l):
        wait_bytes(arrived, send_sem.at[10])
    wait_bytes(state_out.at[pl.ds(0, CHUNKS - 1)], send_sem.at[6])

    @pl.when(core == 0)
    def _():
        wait_bytes(state_out.at[0], send_sem.at[6])

    wait_bytes(gath.at[pl.ds(0, 7)], send_sem.at[7])
    wait_bytes(p_out.at[pl.ds(0, 7)], send_sem.at[8])
    wait_bytes(p_out.at[0, pl.ds(0, 3 * QUARTER)], send_sem.at[8])

    @pl.when(near < SPLIT)
    def _():
        wait_bytes(p_out.at[0, pl.ds(0, QUARTER)], send_sem.at[8])


def local(tokens, in_weight, residues, decay_rates, skip_gain, out_weight):
    channels = in_weight.shape[2]
    vmem = pl.BlockSpec(memory_space=pltpu.VMEM)
    anywhere = pl.BlockSpec(memory_space=pl.ANY)
    dma = pltpu.SemaphoreType.DMA
    scratch = [
        pltpu.VMEM((MODES, LANES), F32),
        pltpu.VMEM((MODES, LANES), F32),
        pltpu.VMEM((1, LANES), F32),
        pltpu.VMEM((CHUNKS, ROWS, WIDE), BF16),
        pltpu.VMEM((4, WIDE, 2 * QKV), BF16),
        pltpu.VMEM((2, WIDE, FEATURES), BF16),
        pltpu.VMEM((CHUNKS, 4, ROWS, 2 * QKV), BF16),
        pltpu.VMEM((2, CHUNKS, ROWS, QKV), BF16),
        pltpu.VMEM((2, CHUNKS, ROWS, QKV), BF16),
        pltpu.VMEM((2, CHUNKS, ROWS, QKV), BF16),
        pltpu.VMEM((CHUNKS, ROWS, QKV), BF16),
        pltpu.VMEM((CHUNKS, ROWS, QKV), BF16),
        pltpu.VMEM((LATE, 4, ROWS, QKV), BF16),
        pltpu.VMEM((LATE, 2, HALF, QKV), BF16),
        pltpu.VMEM((LATE, 2, HALF, QKV), BF16),
        pltpu.VMEM((LATE, 2, HALF, QKV), BF16),
        pltpu.VMEM((ROWS, LANES), F32),
        pltpu.VMEM((ROWS, LANES), F32),
        pltpu.VMEM((ROWS, LANES), F32),
        pltpu.VMEM((MODES, SEGS, LANES), F32),
        pltpu.VMEM((MODES, SEGS, LANES), F32),
        pltpu.VMEM((MODES, SEGS, LANES), F32),
        pltpu.VMEM((3, MODES, SEGS, LANES), F32),
        pltpu.VMEM((MODES, SEGS, LANES), F32),
        pltpu.VMEM((CHUNKS + 1, MODES, LANES), F32),
        pltpu.VMEM((CHUNKS, MODES, LANES), F32),
        pltpu.VMEM((MODES, LANES), F32),
        pltpu.VMEM((MODES, LANES), F32),
        pltpu.VMEM((MODES, LANES), F32),
        pltpu.VMEM((CHUNKS, ROWS, WIDE), BF16),
        pltpu.VMEM((CHUNKS, ROWS, WIDE), BF16),
        pltpu.VMEM((2, CHUNKS, QUARTER, WIDE), BF16),
        pltpu.VMEM((CHUNKS, HALF, WIDE), BF16),
        pltpu.VMEM((2, 2, 2, 2, 2, QUARTER, FEATURES), BF16),
        pltpu.VMEM((2, 2, HALF, FEATURES), BF16),
        pltpu.VMEM((2, 2, 2, QUARTER, FEATURES), BF16),
        pltpu.VMEM((2, 2, 2, QUARTER, FEATURES), BF16),
        dma((9,)),
        dma((CHUNKS + 1,)),
        dma((2, 2)),
        dma((5,)),
        dma((1,)),
        dma((2, CHUNKS)),
        dma((2, CHUNKS)),
        dma((2, CHUNKS)),
        dma((CHUNKS,)),
        dma((LATE,)),
        dma((LATE, 2)),
        dma((LATE, 2)),
        dma((LATE, 2)),
        dma((CHUNKS + 1,)),
        dma((8, CHUNKS)),
        dma((2, CHUNKS)),
        dma((CHUNKS,)),
        dma((2, 2)),
        dma((2, 2)),
        dma((2,)),
        dma((11,)),
    ]
    return pl.pallas_call(
        kernel,
        out_shape=pltpu.VMEM(tokens.shape, BF16),
        in_specs=[anywhere] * 6,
        out_specs=vmem,
        scratch_shapes=scratch,
        compiler_params=pltpu.CompilerParams(
            collective_id=0, has_side_effects=True, vmem_limit_bytes=56 * 2**20
        ),
        name="hyena_block",
    )(tokens, in_weight.transpose(1, 0, 2), residues, decay_rates, skip_gain.reshape(1, channels), out_weight)


def solution(mesh):
    in_specs = (
        P("tp", "seq"),
        P("seq", None, "tp"),
        P(None, "tp"),
        P(None, "tp"),
        P("tp"),
        P("tp", "seq"),
    )
    return jax.shard_map(local, mesh=mesh, in_specs=in_specs, out_specs=P("tp", "seq"), check_vma=False)
```
